512 devices in a mesh: gx: 32 (over x, y, core), gy: 16 (over z).
Axes of the slice: x: 4, y: 4, z: 16, core: 2. Of those that a mesh axis runs over, the one named last changes fastest.
Arguments:
- velocity: float32 [3, 512, 256, 128], P(None, 'gx', 'gy'), may hold values from -6 to 6
- density: float32 [512, 256, 128], P('gx', 'gy'), may hold values from 0.3 to 3
- viscosity: float32 [512, 256, 128], P('gx', 'gy'), may hold values from 0.05 to 0.5
- grad_out_velocity: float32 [3, 512, 256, 128], P(None, 'gx', 'gy'), may hold values from -6 to 6
- new_density_gradient: float32 [512, 256, 128], P('gx', 'gy'), may hold values from -6 to 6
Outputs:
- grad_velocity: float32 [3, 512, 256, 128], P(None, 'gx', 'gy')
- old_density_gradient: float32 [512, 256, 128], P('gx', 'gy')
- grad_viscosity: float32 [512, 256, 128], P('gx', 'gy')
The draws below stay inside these ranges and needn't reach their ends.
All inputs are finite; a program needn't handle non-finite values.
Results may differ from the reference program's by a relative error of at most 0.0001.
Values sent between devices are 32-bit elements; how exact they have to be, the bound alone decides.
No kernel may reach another device: no remote copies, remote signals or barrier semaphores. Data moves between devices by JAX's collectives and lax.ppermute only.
A program may use at most 64 MiB of HBM per device.

```python
import math
import jax
import jax.numpy as jnp

NZ = 128
LEVELS = 5
SMOOTH = 2
COARSE = 6
NX = 512
NY = 256


def block_levels(stream_key, dims, shards, least, high):
    gain = 1.0
    for dim, blocks in shards:
        steps = jax.random.uniform(jax.random.fold_in(jax.random.fold_in(stream_key, 6), dim), (blocks,), jnp.float32, least / len(shards), high / len(shards))
        gain = gain * jnp.repeat(jnp.exp(steps), dims[dim] // blocks).reshape((-1,) + (1,) * (len(dims) - 1 - dim))
    return gain


def normal_values(own_key, shape, deviation, most, shards=(), held_as=jnp.bfloat16):
    array = deviation * jax.random.normal(own_key, shape, jnp.float32)
    if shards:
        array = array * block_levels(own_key, shape, shards, -0.22, 0.18)
    return jnp.clip(array, -most, most).astype(held_as)


def setup_inputs(seed: int = 0) -> dict:
    arg_keys = jax.random.split(jax.random.key(seed), 6)
    return {
        "velocity": normal_values(arg_keys[0], (3, NX, NY, NZ), 1.0, 6.0, ((1, 32), (2, 16)), jnp.float32),
        "density": jnp.clip(jnp.exp(math.log(3.0) - 2.3025851 * jax.random.uniform(arg_keys[1], (NX, NY, NZ), jnp.float32) ** block_levels(arg_keys[1], (NX, NY, NZ), ((0, 32), (1, 16)), -0.2, 0.2)), 0.3, 3.0),
        "viscosity": jnp.clip(jnp.exp(math.log(0.5) - 2.3025851 * jax.random.uniform(arg_keys[2], (NX, NY, NZ), jnp.float32) ** block_levels(arg_keys[2], (NX, NY, NZ), ((0, 32), (1, 16)), -0.2, 0.2)), 0.05, 0.5),
        "grad_out_velocity": normal_values(arg_keys[3], (3, NX, NY, NZ), 1.0, 6.0, ((1, 32), (2, 16)), jnp.float32),
        "new_density_gradient": normal_values(arg_keys[4], (NX, NY, NZ), 1.0, 6.0, ((0, 32), (1, 16)), jnp.float32),
    }


STEP_INTERVAL = 0.2
SPECTRUM_MID = 1.2
SPECTRUM_HALF = 0.8


def shifted_up(scalar_field):
    return jnp.concatenate([scalar_field[:, :, 1:], jnp.zeros_like(scalar_field[:, :, :1])], 2)


def shifted_down(scalar_field):
    return jnp.concatenate([jnp.zeros_like(scalar_field[:, :, :1]), scalar_field[:, :, :-1]], 2)


def bottom_copy(scalar_field):
    return jnp.concatenate([scalar_field[:, :, :1], scalar_field[:, :, :-1]], 2)


def coarsen(scalar_field):
    size_x, size_y, size_z = scalar_field.shape
    return scalar_field.reshape(size_x // 2, 2, size_y // 2, 2, size_z).mean(axis=(1, 3))


def refine(scalar_field):
    return jnp.repeat(jnp.repeat(scalar_field, 2, axis=0), 2, axis=1)


def smooth(start, source, diagonal, operate, sweeps):
    sigma = SPECTRUM_MID / SPECTRUM_HALF
    ratio = 1.0 / sigma
    solver_state = start
    update = None
    for sweep in range(sweeps):
        if solver_state is None:
            scaled = source / diagonal
        else:
            scaled = (source - operate(solver_state)) / diagonal
        if update is None:
            update = scaled / SPECTRUM_MID
        else:
            following = 1.0 / (2.0 * sigma - ratio)
            update = following * ratio * update + (2.0 * following / SPECTRUM_HALF) * scaled
            ratio = following
        solver_state = update if solver_state is None else solver_state + update
    return solver_state


def rolled_faces(coefficient):
    face_x = 0.5 * (coefficient + jnp.roll(coefficient, 1, 0))
    face_y = 0.5 * (coefficient + jnp.roll(coefficient, 1, 1))
    face_z = 0.5 * (coefficient + bottom_copy(coefficient))
    return face_x, face_y, face_z


def rolled_operator(scalar_field, faces, scale):
    face_x, face_y, face_z = faces
    flux_x = face_x * (scalar_field - jnp.roll(scalar_field, 1, 0))
    flux_y = face_y * (scalar_field - jnp.roll(scalar_field, 1, 1))
    flux_z = face_z * (scalar_field - shifted_down(scalar_field))
    across = (jnp.roll(flux_x, -1, 0) - flux_x) + (jnp.roll(flux_y, -1, 1) - flux_y)
    return -(across * scale) - (shifted_up(flux_z) - flux_z)


def rolled_diagonal(faces, scale):
    face_x, face_y, face_z = faces
    across = face_x + jnp.roll(face_x, -1, 0) + face_y + jnp.roll(face_y, -1, 1)
    return across * scale + face_z + shifted_up(face_z)


def central_sum_term(loop_carry, scalar_field):
    direction_first = loop_carry[0] * scalar_field
    direction_second = loop_carry[1] * scalar_field
    direction_third = loop_carry[2] * scalar_field
    total = (jnp.roll(direction_first, -1, 0) - jnp.roll(direction_first, 1, 0)) + (jnp.roll(direction_second, -1, 1) - jnp.roll(direction_second, 1, 1))
    total = total + (shifted_up(direction_third) - shifted_down(direction_third))
    return 0.5 * total


def reference(velocity, density, viscosity, grad_out_velocity, new_density_gradient):
    coefficients = [1.0 / density]
    for level in range(1, LEVELS):
        coefficients.append(coarsen(coefficients[-1]))
    level_data = []
    for level in range(LEVELS):
        faces = rolled_faces(coefficients[level])
        level_data.append((faces, rolled_diagonal(faces, 0.25 ** level)))

    def cycle(level, source):
        faces, diagonal = level_data[level]
        scale = 0.25 ** level

        def operate(scalar_field):
            return rolled_operator(scalar_field, faces, scale)

        if level == LEVELS - 1:
            return smooth(None, source, diagonal, operate, COARSE)
        guess = smooth(None, source, diagonal, operate, SMOOTH)
        residual = source - operate(guess)
        guess = guess + refine(cycle(level + 1, coarsen(residual)))
        return smooth(guess, source, diagonal, operate, SMOOTH)

    face_x, face_y, face_z = level_data[0][0]
    flux_x = face_x * grad_out_velocity[0]
    flux_y = face_y * grad_out_velocity[1]
    flux_z = face_z * grad_out_velocity[2]
    divergence = (jnp.roll(flux_x, -1, 0) - flux_x) + (jnp.roll(flux_y, -1, 1) - flux_y) + (shifted_up(flux_z) - flux_z)
    potential = cycle(0, divergence)
    adjoint = jnp.stack([
        grad_out_velocity[0] + potential - jnp.roll(potential, 1, 0),
        grad_out_velocity[1] + potential - jnp.roll(potential, 1, 1),
        grad_out_velocity[2] + potential - shifted_down(potential)])
    visc_faces = rolled_faces(viscosity)
    grad_velocity = jnp.stack([
        adjoint[velocity_component] + STEP_INTERVAL * central_sum_term(velocity, adjoint[velocity_component]) - STEP_INTERVAL * rolled_operator(adjoint[velocity_component], visc_faces, 1.0)
        for velocity_component in range(3)])
    old_density_gradient = new_density_gradient + STEP_INTERVAL * central_sum_term(velocity, new_density_gradient)
    across_x = jnp.zeros_like(viscosity)
    across_y = jnp.zeros_like(viscosity)
    across_z = jnp.zeros_like(viscosity)
    for velocity_component in range(3):
        across_x = across_x + (adjoint[velocity_component] - jnp.roll(adjoint[velocity_component], 1, 0)) * (velocity[velocity_component] - jnp.roll(velocity[velocity_component], 1, 0))
        across_y = across_y + (adjoint[velocity_component] - jnp.roll(adjoint[velocity_component], 1, 1)) * (velocity[velocity_component] - jnp.roll(velocity[velocity_component], 1, 1))
        across_z = across_z + (adjoint[velocity_component] - shifted_down(adjoint[velocity_component])) * (velocity[velocity_component] - shifted_down(velocity[velocity_component]))
    across_x = -STEP_INTERVAL * across_x
    across_y = -STEP_INTERVAL * across_y
    across_z = -STEP_INTERVAL * across_z
    bottom = (jnp.arange(viscosity.shape[2]) == 0).astype(viscosity.dtype)[None, None, :]
    grad_viscosity = 0.5 * (across_x + jnp.roll(across_x, -1, 0)) + 0.5 * (across_y + jnp.roll(across_y, -1, 1))
    grad_viscosity = grad_viscosity + 0.5 * (across_z + shifted_up(across_z)) + 0.5 * bottom * across_z
    return grad_velocity, old_density_gradient, grad_viscosity
```

```python
import functools

import jax
import jax.numpy as jnp
from jax import lax
from jax.experimental import pallas as pl
from jax.experimental.pallas import tpu as pltpu
from jax.sharding import PartitionSpec as P

INTERPRET = False
DT = 0.2
MID = 1.2
HALF = 0.8
SIGMA = MID / HALF
RHO0 = 1.0 / SIGMA
RHO1 = 1.0 / (2.0 * SIGMA - RHO0)
A1 = RHO1 * RHO0
B1 = 2.0 * RHO1 / HALF
BLOCK = 16
PAD = 12
PAD1 = 6
WIN = 9
F32 = jnp.float32


def call(body, out_shapes, args, scratch=(), scalars=0, megabytes=24):
    smem = [pl.BlockSpec(memory_space=pltpu.SMEM)] * scalars
    vmem = [pl.BlockSpec(memory_space=pltpu.VMEM)] * (len(args) - scalars)
    return pl.pallas_call(
        body,
        out_shape=[jax.ShapeDtypeStruct(s, F32) for s in out_shapes],
        in_specs=smem + vmem,
        out_specs=[pl.BlockSpec(memory_space=pltpu.VMEM)] * len(out_shapes),
        scratch_shapes=[pltpu.VMEM(s, F32) for s in scratch],
        compiler_params=pltpu.CompilerParams(vmem_limit_bytes=megabytes * 2**20),
        interpret=INTERPRET,
    )(*args)


def loop(low, high, step):
    if high - low <= 4:
        for i in range(low, high):
            step(i)
    else:
        lax.fori_loop(low, high, lambda i, c: (step(i), c)[1], 0)


def ydn(v):
    return pltpu.roll(v, 1, axis=0)


def yup(v):
    return pltpu.roll(v, v.shape[0] - 1, axis=0)


def layer(v):
    return lax.broadcasted_iota(jnp.int32, v.shape, 1)


def zdn(v):
    return jnp.where(layer(v) == 0, 0.0, pltpu.roll(v, 1, axis=1))


def zdn_copy(v):
    return jnp.where(layer(v) == 0, v, pltpu.roll(v, 1, axis=1))


def zup(v):
    last = v.shape[1] - 1
    return jnp.where(layer(v) == last, 0.0, pltpu.roll(v, last, axis=1))


def faces(b, c, low, high, scale):
    cx, cy, cz, dinv = c

    def step(i):
        b0 = b[i]
        fx = (0.5 * scale) * (b0 + b[i - 1])
        fxp = (0.5 * scale) * (b[i + 1] + b0)
        fy = (0.5 * scale) * (b0 + ydn(b0))
        fz = 0.5 * (b0 + zdn_copy(b0))
        cx[i] = fx
        cy[i] = fy
        cz[i] = fz
        dinv[i] = 1.0 / (fx + fxp + fy + yup(fy) + fz + zup(fz))

    loop(low, high, step)
    cx[high] = (0.5 * scale) * (b[high] + b[high - 1])


def operate(q, c, i):
    cx, cy, cz, _ = c
    q0 = q[i]
    across = cx[i] * (q0 - q[i - 1]) - cx[i + 1] * (q[i + 1] - q0)
    fy = cy[i] * (q0 - ydn(q0))
    fz = cz[i] * (q0 - zdn(q0))
    return across + (fy - yup(fy)) + (fz - zup(fz))


def pre(f, x1, x2, c, low, high):
    dinv = c[3]

    def first(i):
        x1[i] = f[i] * dinv[i] * (1.0 / MID)

    loop(low - 1, high + 1, first)

    def second(i):
        x2[i] = (1.0 + A1) * x1[i] + B1 * ((f[i] - operate(x1, c, i)) * dinv[i])

    loop(low, high, second)


def post(x, f, e, y, out, c, low, high):
    dinv = c[3]

    def first(i):
        u = (f[i] - operate(x, c, i)) * dinv[i] * (1.0 / MID)
        e[i] = u
        y[i] = x[i] + u

    loop(low - 1, high + 1, first)

    def second(i):
        out[i] = y[i] + (A1 * e[i] + B1 * ((f[i] - operate(y, c, i)) * dinv[i]))

    loop(low, high, second)


def residual_pairs(f, x, c, pairs, start, low, high):
    def step(m):
        i = start + 2 * m
        pairs[m] = (f[i] - operate(x, c, i)) + (f[i + 1] - operate(x, c, i + 1))

    loop(low, high, step)


def plane_pairs(b, pairs, start, low, high):
    def step(m):
        pairs[m] = b[start + 2 * m] + b[start + 2 * m + 1]

    loop(low, high, step)


def row_pairs(pairs, coarse, low, high, row, count, target, shift=0):
    def step(m):
        even = pairs[m, pl.ds(row, count, 2), :]
        odd = pairs[m, pl.ds(row + 1, count, 2), :]
        coarse[m + shift, target : target + count, :] = 0.25 * (even + odd)

    loop(low, high, step)


def correct(x, coarse, wide, low, high, plane, row, count, target):
    def widen(m):
        v = coarse[m, row : row + count, :]
        wide[m, pl.ds(target, count, 2), :] = v
        wide[m, pl.ds(target + 1, count, 2), :] = v

    loop(low, high, widen)

    def add(m):
        i = 2 * m + plane
        w = wide[m]
        x[i] = x[i] + w
        x[i + 1] = x[i + 1] + w

    loop(low, high, add)


def own_body(vel, den, vis, g, ndg, up, down, b, d):
    def invert(i):
        b[i] = 1.0 / den[i]

    loop(0, BLOCK, invert)

    def step(i):
        b0 = b[i]
        fz = 0.5 * (b0 + zdn_copy(b0)) * g[2, i]
        fy = 0.5 * (b0 + ydn(b0)) * g[1, i]
        rows = lax.broadcasted_iota(jnp.int32, fy.shape, 0)
        fy = jnp.where(rows == 0, 0.0, fy)
        total = (zup(fz) - fz) + (yup(fy) - fy)
        left = jnp.maximum(i - 1, 0)
        right = jnp.minimum(i + 1, BLOCK - 1)
        inner = jnp.where(i > 0, 0.5, 0.0) * (b0 + b[left]) * g[0, i]
        outer = jnp.where(i < BLOCK - 1, 0.5, 0.0) * (b0 + b[right]) * g[0, right]
        total = total + (outer - inner)
        d[i] = total
        k = BLOCK + i
        edge = BLOCK - 1
        up[i, 0:PAD, :] = b0[BLOCK - PAD :]
        up[k, 0:PAD, :] = total[BLOCK - PAD :]
        down[i, 0:PAD, :] = b0[:PAD]
        down[k, 0:PAD, :] = total[:PAD]
        for c in range(3):
            up[i, PAD + c, :] = vel[c, i, edge, :]
            down[i, PAD + c, :] = vel[c, i, 0, :]
            up[k, PAD + 1 + c, :] = g[c, i, edge, :]
            down[k, PAD + 1 + c, :] = g[c, i, 0, :]
        up[i, PAD + 3, :] = vis[i, edge, :]
        down[i, PAD + 3, :] = vis[i, 0, :]
        up[k, PAD, :] = ndg[i, edge, :]
        down[k, PAD, :] = ndg[i, 0, :]

    loop(0, BLOCK, step)
    z = b.shape[2]
    up[2 * BLOCK] = jnp.zeros((BLOCK, z), F32)
    down[2 * BLOCK] = jnp.zeros((BLOCK, z), F32)
    up[2 * BLOCK, 0:PAD, :] = g[0, 0, BLOCK - PAD :, :]
    down[2 * BLOCK, 0:PAD, :] = g[0, 0, :PAD, :]


def rows_body(odd, vel, vis, g, ndg, b, d, before, after, bb, dd, g0, even_send, odd_send):
    top = PAD + BLOCK

    def join(out, own, i, k):
        out[i, 0:PAD, :] = before[k, 0:PAD, :]
        out[i, PAD:top, :] = own[i]
        out[i, top : top + PAD, :] = after[k, 0:PAD, :]

    def step(i):
        k = BLOCK + i
        join(bb, b, i, i)
        join(dd, d, i, k)
        own_flux = 0.5 * (b[i, 0:1, :] + before[i, PAD - 1 : PAD, :]) * g[1, i, 0:1, :]
        next_flux = (
            0.5
            * (b[i, BLOCK - 1 : BLOCK, :] + after[i, 0:1, :])
            * after[k, PAD + 2 : PAD + 3, :]
        )
        dd[i, PAD - 1 : PAD, :] = before[k, PAD - 1 : PAD, :] + own_flux
        dd[i, PAD : PAD + 1, :] = d[i, 0:1, :] - own_flux
        dd[i, top - 1 : top, :] = d[i, BLOCK - 1 : BLOCK, :] + next_flux
        dd[i, top : top + 1, :] = after[k, 0:1, :] - next_flux

    loop(0, BLOCK, step)
    g0[0:PAD, :] = before[2 * BLOCK, 0:PAD, :]
    g0[PAD:top, :] = g[0, 0]
    g0[top : top + PAD, :] = after[2 * BLOCK, 0:PAD, :]
    is_odd = odd[0]
    for send, last in ((even_send, 1 - is_odd), (odd_send, is_odd)):
        b_start = 5 * last
        d_start = 6 * last
        plane = (BLOCK - 1) * last

        def b_step(m, send=send, b_start=b_start):
            send[m] = bb[b_start + m]

        def d_step(m, send=send, d_start=d_start):
            send[11 + m] = dd[d_start + m]

        loop(0, 11, b_step)
        loop(0, 10, d_step)
        send[21] = g0[...]
        for c in range(3):
            send[22 + c, 0:BLOCK, :] = vel[c, plane]
            send[22 + c, BLOCK : 2 * BLOCK, :] = g[c, plane]
        send[25, 0:BLOCK, :] = vis[plane]
        send[25, BLOCK : 2 * BLOCK, :] = ndg[plane]


def fine_body(
    odd, bb, dd, g0, even_got, odd_got,
    f0, x0, cx, cy, cz, dinv, f1, b1, f2, b2, up, down,
    b, x1, pairs, xa, xb, c1x, c1y, c1z, d1, pairs1,
):
    is_odd = odd[0] == 1
    c0 = (cx, cy, cz, dinv)
    top = PAD + BLOCK

    def left(m):
        return jnp.where(is_odd, even_got[0, m], odd_got[0, m])

    def right(m):
        return jnp.where(is_odd, odd_got[1, m], even_got[1, m])

    def own(i):
        b[PAD + i] = bb[i]
        f0[PAD + i] = dd[i]

    loop(0, BLOCK, own)

    def b_rims(m):
        b[1 + m] = left(m)
        b[top + m] = right(m)

    loop(0, 11, b_rims)

    def d_rims(m):
        f0[2 + m] = left(11 + m)
        f0[top + m] = right(11 + m)

    loop(0, 10, d_rims)
    flux = 0.5 * (b[PAD] + b[PAD - 1]) * g0[...]
    f0[PAD - 1] = f0[PAD - 1] + flux
    f0[PAD] = f0[PAD] - flux
    flux = 0.5 * (b[top] + b[top - 1]) * right(21)
    f0[top - 1] = f0[top - 1] + flux
    f0[top] = f0[top] - flux

    faces(b, c0, 2, 38, 1.0)
    pre(f0, x1, x0, c0, 3, 37)
    residual_pairs(f0, x0, c0, pairs, 0, 2, 18)
    row_pairs(pairs, f1, 2, 18, 0, 20, 0)
    plane_pairs(b, pairs, 0, 1, 19)
    row_pairs(pairs, b1, 1, 19, 0, 20, 0)

    z = b.shape[2]
    f1[:, 20:24, :] = jnp.zeros((20, 4, z), F32)
    b1[:, 20:24, :] = jnp.ones((20, 4, z), F32)
    c1 = (c1x, c1y, c1z, d1)
    faces(b1, c1, 2, 18, 0.25)
    pre(f1, xa, xb, c1, 3, 17)
    residual_pairs(f1, xb, c1, pairs1, 4, 0, 6)
    row_pairs(pairs1, f2, 0, 6, 4, 6, 5, shift=5)
    plane_pairs(b1, pairs1, 2, 0, 8)
    row_pairs(pairs1, b2, 0, 8, 2, 8, 4, shift=4)

    for send, frow, brow, f1row, b1row in ((up, 5, 4, 9, 8), (down, 6, 6, 10, 11)):
        for m in range(6):
            send[m, 0:5, :] = f2[5 + m, frow : frow + 5, :]
        for m in range(8):
            send[m, 5:11, :] = b2[4 + m, brow : brow + 6, :]
        for m in range(16):
            send[m, 11:12, :] = f1[2 + m, f1row : f1row + 1, :]
        for m in range(18):
            send[m, 12:13, :] = b1[1 + m, b1row : b1row + 1, :]


def rows2_body(odd, f1, b1, f2, b2, before, after, g1, h1, g2, h2, even_send, odd_send):
    g1[...] = f1[...]
    h1[...] = b1[...]
    z = f1.shape[2]
    g2[...] = jnp.zeros((16, 16, z), F32)
    h2[...] = jnp.ones((16, 16, z), F32)
    for m in range(6):
        g2[5 + m, 6:10, :] = f2[5 + m, 6:10, :]
        g2[5 + m, 1:6, :] = before[m, 0:5, :]
        g2[5 + m, 10:15, :] = after[m, 0:5, :]
    for m in range(8):
        h2[4 + m, 6:10, :] = b2[4 + m, 6:10, :]
        h2[4 + m, 0:6, :] = before[m, 5:11, :]
        h2[4 + m, 10:16, :] = after[m, 5:11, :]
    for m in range(16):
        g1[2 + m, 1:2, :] = before[m, 11:12, :]
        g1[2 + m, 18:19, :] = after[m, 11:12, :]
    for m in range(18):
        h1[1 + m, 0:1, :] = before[m, 12:13, :]
        h1[1 + m, 19:20, :] = after[m, 12:13, :]
    is_odd = odd[0]
    for send, last in ((even_send, 1 - is_odd), (odd_send, is_odd)):
        for m in range(5):
            send[m, 0:16, :] = g2[6 - last + m]
        for m in range(6):
            send[5 + m, 0:16, :] = h2[6 - 2 * last + m]
        send[11] = g1[10 - last]
        send[12] = h1[11 - 3 * last]


def level2_body(
    odd, f1i, b1i, f2i, b2i, even_got, odd_got,
    f1, x1, c1x, c1y, c1z, d1, f2, x2, c2x, c2y, c2z, d2, slots,
    b1, b2, xa, xb, pairs,
):
    is_odd = odd[0] == 1

    def left(m):
        return jnp.where(is_odd, even_got[0, m], odd_got[0, m])

    def right(m):
        return jnp.where(is_odd, odd_got[1, m], even_got[1, m])

    f1[...] = f1i[...]
    b1[...] = b1i[...]
    f2[...] = f2i[...]
    b2[...] = b2i[...]
    for m in range(5):
        f2[1 + m] = left(m)[0:16]
        f2[10 + m] = right(m)[0:16]
    for m in range(6):
        b2[m] = left(5 + m)[0:16]
        b2[10 + m] = right(5 + m)[0:16]
    f1[1] = left(11)
    f1[18] = right(11)
    b1[0] = left(12)
    b1[19] = right(12)
    c1 = (c1x, c1y, c1z, d1)
    c2 = (c2x, c2y, c2z, d2)
    faces(b2, c2, 1, 15, 0.25**2)
    pre(f2, xb, x2, c2, 2, 14)
    residual_pairs(f2, x2, c2, pairs, 6, 0, 2)
    z = f1.shape[2]
    parts = []
    for m in range(2):
        even = pairs[m, pl.ds(6, 2, 2), :]
        parts.append(0.25 * (even + pairs[m, pl.ds(7, 2, 2), :]))
    plane_pairs(b2, pairs, 6, 0, 2)
    for m in range(2):
        even = pairs[m, pl.ds(6, 2, 2), :]
        parts.append(0.25 * (even + pairs[m, pl.ds(7, 2, 2), :]))
    for m in range(16):
        for n in range(4):
            slots[m, 2 * n : 2 * n + 2, :] = parts[n]
    faces(b1, c1, 1, 19, 0.25)
    pre(f1, xa, x1, c1, 2, 18)


def column_body(place, got, slots):
    def step(p):
        source = lax.rem(place[0] + (p + 8), 16)
        block = got[source]
        for n in range(4):
            slots[0, n, pl.ds(2 * p, 2), :] = block[2 * n : 2 * n + 2]

    for p in range(16):
        step(p)

    def spread(m):
        slots[m] = slots[0]

    loop(1, 32, spread)


def up_body(
    place, got, f1, x1, c1x, c1y, c1z, d1, f2, x2, c2x, c2y, c2z, d2,
    f0, x0, cx, cy, cz, dinv, vel, vis, g, ndg, before, after, even_got, odd_got,
    out_vel, out_ndg, out_vis,
    f3, b3, c3x, c3y, c3z, d3, xa3, xb3, pairs, f4, b4, c4x, c4y, c4z, d4, xa4, xb4, e4,
    w3, t3, e3, y3, v2, w2, t2, e2, y2, v1, w1, t1, e1, y1, v0, w0, t0, e0, y0,
    vp, ap, visp, np_,
):
    z = f1.shape[2]
    devices = 2 * WIN + 1

    def gather(q):
        source = lax.rem(place[1] + (q + 32 - WIN), 32)
        for n in range(2):
            f3[2 * q + n] = got[source, n]
            b3[2 * q + n] = got[source, 2 + n]

    loop(0, devices, gather)
    c3 = (c3x, c3y, c3z, d3)
    last = 2 * devices - 1
    faces(b3, c3, 1, last, 0.25**3)
    pre(f3, xa3, xb3, c3, 2, last - 1)
    residual_pairs(f3, xb3, c3, pairs, 0, 2, devices - 2)
    row_pairs(pairs, f4, 2, devices - 2, 0, 16, 0)
    plane_pairs(b3, pairs, 0, 0, devices)
    row_pairs(pairs, b4, 0, devices, 0, 16, 0)
    c4 = (c4x, c4y, c4z, d4)
    low, high = 2, devices - 2
    faces(b4, c4, low, high, 0.25**4)
    for i in range(low, high):
        u = f4[i] * d4[i] * (1.0 / MID)
        e4[i] = u
        xa4[i] = u
    ratio = RHO0
    x_now, x_next = xa4, xb4
    for _ in range(5):
        following = 1.0 / (2.0 * SIGMA - ratio)
        low, high = low + 1, high - 1
        for i in range(low, high):
            scaled = (f4[i] - operate(x_now, c4, i)) * d4[i]
            u = following * ratio * e4[i] + (2.0 * following / HALF) * scaled
            e4[i] = u
            x_next[i] = x_now[i] + u
        ratio = following
        x_now, x_next = x_next, x_now
    correct(xb3, x_now, w3, 7, 12, 0, 0, 16, 0)
    post(xb3, f3, e3, y3, t3, c3, 16, 22)
    v2[...] = x2[...]
    correct(v2, t3, w2, 16, 22, -30, 14, 6, 2)
    post(v2, f2, e2, y2, t2, (c2x, c2y, c2z, d2), 4, 12)
    v1[...] = x1[...]
    correct(v1, t2, w1, 4, 12, -6, 4, 8, 2)
    post(v1, f1, e1, y1, t1, (c1x, c1y, c1z, d1), 4, 16)

    def keep(i):
        v0[i] = x0[i]

    loop(8, 32, keep)
    correct(v0, t1, w0, 4, 16, 0, 4, 12, 8)
    post(v0, f0, e0, y0, t0, (cx, cy, cz, dinv), 10, 29)

    def pad(i):
        k = BLOCK + i

        def put(out, own, source, row):
            out[0:1, :] = before[source, row : row + 1, :]
            out[1:17, :] = own
            out[17:18, :] = after[source, row : row + 1, :]

        for c in range(3):
            put(vp.at[c, i + 1], vel[c, i], i, PAD + c)
            put(ap.at[c, i + 1], g[c, i], k, PAD + 1 + c)
        put(visp.at[i + 1], vis[i], i, PAD + 3)
        put(np_.at[i + 1], ndg[i], k, PAD)

    loop(0, BLOCK, pad)
    is_odd = lax.rem(place[1], 2) == 1

    def left(m):
        return jnp.where(is_odd, even_got[0, m], odd_got[0, m])

    def right(m):
        return jnp.where(is_odd, odd_got[1, m], even_got[1, m])

    for plane, side in ((0, left), (BLOCK + 1, right)):
        for c in range(3):
            both = side(22 + c)
            vp[c, plane, 1:17, :] = both[0:BLOCK]
            ap[c, plane, 1:17, :] = both[BLOCK : 2 * BLOCK]
        both = side(25)
        visp[plane, 1:17, :] = both[0:BLOCK]
        np_[plane, 1:17, :] = both[BLOCK : 2 * BLOCK]

    def lift(m):
        centre = t0[m + 11, 11:35, :]
        ap[0, m] = ap[0, m] + (centre - t0[m + 10, 11:35, :])
        ap[1, m] = ap[1, m] + (centre - t0[m + 11, 10:34, :])
        ap[2, m] = ap[2, m] + (centre - zdn(centre))

    loop(0, BLOCK + 2, lift)

    def finish(i):
        m = i + 1

        def around(ref):
            return (
                ref[m, 1:17, :],
                ref[m - 1, 1:17, :],
                ref[m + 1, 1:17, :],
                ref[m, 0:16, :],
                ref[m, 2:18, :],
            )

        speeds = [around(vp.at[c]) for c in range(3)]
        n0, nxm, nxp, nym, nyp = around(visp)
        fxm, fxp = 0.5 * (n0 + nxm), 0.5 * (nxp + n0)
        fym, fyp = 0.5 * (n0 + nym), 0.5 * (nyp + n0)
        fz = 0.5 * (n0 + zdn_copy(n0))
        u0m, u0p = speeds[0][1], speeds[0][2]
        u1m, u1p = speeds[1][3], speeds[1][4]
        u2 = speeds[2][0]

        def transport(q0, qxm, qxp, qym, qyp):
            up = u2 * q0
            return 0.5 * ((u0p * qxp - u0m * qxm) + (u1p * qyp - u1m * qym) + (zup(up) - zdn(up)))

        fields = around(np_)
        out_ndg[i] = fields[0] + DT * transport(*fields)
        gxm = gxp = gym = gyp = gz = 0.0
        for c in range(3):
            fields = around(ap.at[c])
            q0, qxm, qxp, qym, qyp = fields
            s0, sxm, sxp, sym, syp = speeds[c]
            dxm, dxp, dym, dyp = q0 - qxm, qxp - q0, q0 - qym, qyp - q0
            dz = q0 - zdn(q0)
            flux = fz * dz
            spread = (fxp * dxp - fxm * dxm) + (fyp * dyp - fym * dym) + (zup(flux) - flux)
            out_vel[c, i] = q0 + DT * (transport(*fields) + spread)
            gxm = gxm + dxm * (s0 - sxm)
            gxp = gxp + dxp * (sxp - s0)
            gym = gym + dym * (s0 - sym)
            gyp = gyp + dyp * (syp - s0)
            gz = gz + dz * (s0 - zdn(s0))
        bottom = jnp.where(layer(gz) == 0, gz, 0.0)
        out_vis[i] = (-0.5 * DT) * ((gxm + gxp) + (gym + gyp) + (gz + zup(gz)) + bottom)

    loop(0, BLOCK, finish)


def shards(velocity, density, viscosity, grad_out, density_gradient):
    z = density.shape[2]
    size_x, size_y = lax.axis_size("gx"), lax.axis_size("gy")
    at_x, at_y = lax.axis_index("gx"), lax.axis_index("gy")
    odd = lax.rem(at_x, 2).astype(jnp.int32).reshape(1)
    place = jnp.stack([at_y, at_x]).astype(jnp.int32)
    even_pairs = [[i, i + 1] for i in range(0, size_x, 2)]
    odd_pairs = [[i, (i + 1) % size_x] for i in range(1, size_x, 2)]
    forward = [(i, (i + 1) % size_y) for i in range(size_y)]
    backward = [(j, i) for i, j in forward]

    def along_y(up, down):
        return lax.ppermute(up, "gy", forward), lax.ppermute(down, "gy", backward)

    def along_x(even_send, odd_send):
        return (
            lax.all_gather(even_send, "gx", axis_index_groups=even_pairs),
            lax.all_gather(odd_send, "gx", axis_index_groups=odd_pairs),
        )

    fine = (40, 40, z)
    mid = (20, 24, z)
    low = (16, 16, z)
    rim = (2 * BLOCK + 1, BLOCK, z)
    own = (BLOCK, BLOCK, z)
    fields = (velocity, viscosity, grad_out, density_gradient)
    up, down, b, d = call(
        own_body,
        [rim, rim, own, own],
        (velocity, density, viscosity, grad_out, density_gradient),
    )
    before, after = along_y(up, down)
    send = (26, 40, z)
    bb, dd, g0, even_send, odd_send = call(
        rows_body,
        [(BLOCK, 40, z), (BLOCK, 40, z), (40, z), send, send],
        (odd, *fields, b, d, before, after),
        scalars=1,
    )
    even_got, odd_got = along_x(even_send, odd_send)
    fine_out = call(
        fine_body,
        [fine] * 6 + [mid, mid, low, low, (18, 16, z), (18, 16, z)],
        (odd, bb, dd, g0, even_got, odd_got),
        [fine, fine, (20, 40, z)] + [mid] * 6 + [(8, 24, z)],
        scalars=1,
    )
    f0, x0, cx, cy, cz, dinv, f1, b1, f2, b2, up, down = fine_out
    before2, after2 = along_y(up, down)
    send2 = (13, 24, z)
    f1, b1, f2, b2, even_send, odd_send = call(
        rows2_body,
        [mid, mid, low, low, send2, send2],
        (odd, f1, b1, f2, b2, before2, after2),
        scalars=1,
    )
    even_got2, odd_got2 = along_x(even_send, odd_send)
    coarse = call(
        level2_body,
        [mid] * 6 + [low] * 6 + [(size_y, 8, z)],
        (odd, f1, b1, f2, b2, even_got2, odd_got2),
        [mid, low, mid, low, (2, 16, z)],
        scalars=1,
    )
    got = lax.all_to_all(coarse[-1], "gy", 0, 0, tiled=True)
    (slots,) = call(column_body, [(size_x, 4, 2 * size_y, z)], (place, got), scalars=1)
    got = lax.all_to_all(slots, "gx", 0, 0, tiled=True)
    devices = 2 * WIN + 1
    level3 = (2 * devices, 32, z)
    level4 = (devices, 16, z)
    return tuple(
        call(
            up_body,
            [(3, *own), own, own],
            (place, got, *coarse[:-1], f0, x0, cx, cy, cz, dinv, *fields)
            + (before, after, even_got, odd_got),
            [level3] * 8
            + [(devices, 32, z)]
            + [level4] * 9
            + [(12, 32, z), level3, level3, level3]
            + [low, (22, 16, z), low, low, low]
            + [mid, (12, 24, z), mid, mid, mid]
            + [fine, (16, 40, z), fine, fine, fine]
            + [(3, 18, 24, z), (3, 18, 24, z), (18, 24, z), (18, 24, z)],
            scalars=1,
            megabytes=48,
        )
    )


def solution(mesh):
    placed = (
        P(None, "gx", "gy", None),
        P("gx", "gy", None),
        P("gx", "gy", None),
        P(None, "gx", "gy", None),
        P("gx", "gy", None),
    )
    return jax.shard_map(
        shards,
        mesh=mesh,
        in_specs=placed,
        out_specs=(P(None, "gx", "gy", None), P("gx", "gy", None), P("gx", "gy", None)),
        check_vma=False,
    )
```

```python
import functools

import jax
import jax.numpy as jnp
from jax import lax
from jax.experimental import pallas as pl
from jax.experimental.pallas import tpu as pltpu
from jax.sharding import PartitionSpec as P

INTERPRET = False
DT = 0.2
MID = 1.2
HALF = 0.8
SIGMA = MID / HALF
RHO0 = 1.0 / SIGMA
RHO1 = 1.0 / (2.0 * SIGMA - RHO0)
A1 = RHO1 * RHO0
B1 = 2.0 * RHO1 / HALF
BLOCK = 16
PAD = 12
PAD1 = 6
U0, U1, U2 = 4, 4, 6
WIN = 9
F32 = jnp.float32


def call(body, out_shapes, args, scratch=(), scalars=0, megabytes=16, fetched=0, sems=0):
    smem = [pl.BlockSpec(memory_space=pltpu.SMEM)] * scalars
    anywhere = [pl.BlockSpec(memory_space=pl.ANY)] * fetched
    vmem = [pl.BlockSpec(memory_space=pltpu.VMEM)] * (len(args) - scalars - fetched)
    scratch = [pltpu.VMEM(s, F32) for s in scratch]
    if sems:
        scratch.append(pltpu.SemaphoreType.DMA((sems,)))
    return pl.pallas_call(
        body,
        out_shape=[jax.ShapeDtypeStruct(s, F32) for s in out_shapes],
        in_specs=smem + anywhere + vmem,
        out_specs=[pl.BlockSpec(memory_space=pltpu.VMEM)] * len(out_shapes),
        scratch_shapes=scratch,
        compiler_params=pltpu.CompilerParams(vmem_limit_bytes=megabytes * 2**20),
        interpret=INTERPRET,
    )(*args)


def loop(low, high, step, unroll=1):
    def group(base, count):
        stores = []
        for u in range(count):
            stores.extend(step(base + u) or ())
        for ref, index, value in stores:
            ref[index] = value

    groups = (high - low) // unroll
    if groups == 1:
        group(low, unroll)
    elif groups > 1:
        lax.fori_loop(0, groups, lambda n, c: (group(low + n * unroll, unroll), c)[1], 0)
    rest = (high - low) - groups * unroll
    if rest:
        group(high - rest, rest)


def ydn(v):
    return pltpu.roll(v, 1, axis=0)


def yup(v):
    return pltpu.roll(v, v.shape[0] - 1, axis=0)


def layer(v):
    return lax.broadcasted_iota(jnp.int32, v.shape, 1)


def zroll_dn(v):
    return pltpu.roll(v, 1, axis=1)


def zroll_up(v):
    return pltpu.roll(v, v.shape[1] - 1, axis=1)


def zdn(v):
    return jnp.where(layer(v) == 0, 0.0, zroll_dn(v))


def zdn_copy(v):
    return jnp.where(layer(v) == 0, v, zroll_dn(v))


def zup(v):
    return jnp.where(layer(v) == v.shape[1] - 1, 0.0, zroll_up(v))


def setup(b, n, diag, low, high, scale, unroll, f=None, g=None, g_range=None):
    half = 0.5 * scale

    def step(i):
        b0 = b[i]
        fxm = half * (b0 + b[i - 1])
        fxp = half * (b[i + 1] + b0)
        fym = half * (b0 + ydn(b0))
        fyp = yup(fym)
        fz = 0.5 * (b0 + zdn_copy(b0))
        fzp = zup(fz)
        d = (fxm + fxp) + (fym + fyp) + (fz + fzp)
        inv = 1.0 / d
        fzm = jnp.where(layer(fz) == 0, 0.0, fz)
        out = [(ref, i, v * inv) for ref, v in zip(n, (fxm, fxp, fym, fyp, fzm, fzp), strict=True)]
        if diag is not None:
            out.append((diag, i, d))
        if f is not None:
            out.append((g, i, f[i] * inv))
        return out

    loop(low, high, step, unroll)


def around_sum(q, n, i, q0):
    total = (n[0][i] * q[i - 1] + n[1][i] * q[i + 1]) + (n[2][i] * ydn(q0) + n[3][i] * yup(q0))
    return total + (n[4][i] * zroll_dn(q0) + n[5][i] * zroll_up(q0))


def pre(g, x, n, low, high, unroll):
    first = (1.0 + A1) / MID + B1 * (1.0 - 1.0 / MID)

    def step(i):
        g0 = g[i]
        return [(x, i, first * g0 + (B1 / MID) * around_sum(g, n, i, g0))]

    loop(low, high, step, unroll)


def post(x, g, y, out, n, low, high, unroll):
    def first(i):
        x0 = x[i]
        return [(y, i, x0 + (1.0 / MID) * ((g[i] - x0) + around_sum(x, n, i, x0)))]

    loop(low - 1, high + 1, first, unroll)

    def second(i):
        y0 = y[i]
        z = (g[i] - y0) + around_sum(y, n, i, y0)
        return [(out, i, y0 + (A1 * (y0 - x[i]) + B1 * z))]

    loop(low, high, second, unroll)


def residual_pairs(g, x, diag, n, pairs, start, low, high, unroll):
    def one(i):
        x0 = x[i]
        return diag[i] * ((g[i] - x0) + around_sum(x, n, i, x0))

    def step(m):
        i = start + 2 * m
        return [(pairs, m, one(i) + one(i + 1))]

    loop(low, high, step, unroll)


def plane_pairs(b, pairs, start, low, high, unroll=4):
    def step(m):
        return [(pairs, m, b[start + 2 * m] + b[start + 2 * m + 1])]

    loop(low, high, step, unroll)


def row_pairs(pairs, coarse, low, high, row, count, target, shift=0, unroll=8):
    def step(m):
        even = pairs[m, pl.ds(row, count, 2), :]
        odd = pairs[m, pl.ds(row + 1, count, 2), :]
        return [(coarse, (m + shift, slice(target, target + count)), 0.25 * (even + odd))]

    loop(low, high, step, unroll)


def correct(x, coarse, wide, low, high, plane, row, count, target, unroll=4, out=None):
    def widen(m):
        v = coarse[m, row : row + count, :]
        return [
            (wide, (m, pl.ds(target, count, 2)), v),
            (wide, (m, pl.ds(target + 1, count, 2)), v),
        ]

    loop(low, high, widen, 2 * unroll)
    out = x if out is None else out

    def add(m):
        i = 2 * m + plane
        w = wide[m]
        return [(out, i, x[i] + w), (out, i + 1, x[i + 1] + w)]

    loop(low, high, add, unroll)


def own_body(
    vel_in, den_in, vis_in, g_in, ndg_in, up, down, b, d, planes, vel, den, vis, g, ndg, sems
):
    pairs = ((den_in, den), (g_in, g), (vel_in, vel), (vis_in, vis), (ndg_in, ndg))
    copies = [pltpu.make_async_copy(s, t, sems.at[n]) for n, (s, t) in enumerate(pairs)]
    for copy in copies:
        copy.start()
    copies[0].wait()

    def invert(i):
        return [(b, i, 1.0 / den[i])]

    loop(0, BLOCK, invert, 8)
    copies[1].wait()
    edge = BLOCK - 1

    def step(i):
        b0 = b[i]
        fz = 0.5 * (b0 + zdn_copy(b0)) * g[2, i]
        fy = 0.5 * (b0 + ydn(b0)) * g[1, i]
        rows = lax.broadcasted_iota(jnp.int32, fy.shape, 0)
        fy = jnp.where(rows == 0, 0.0, fy)
        total = (zup(fz) - fz) + (yup(fy) - fy)
        left = jnp.maximum(i - 1, 0)
        right = jnp.minimum(i + 1, edge)
        inner = jnp.where(i > 0, 0.5, 0.0) * (b0 + b[left]) * g[0, i]
        outer = jnp.where(i < edge, 0.5, 0.0) * (b0 + b[right]) * g[0, right]
        total = total + (outer - inner)
        k = BLOCK + i
        head = slice(0, PAD)
        out = [
            (d, i, total),
            (up, (i, head), b0[BLOCK - PAD :]),
            (up, (k, head), total[BLOCK - PAD :]),
            (down, (i, head), b0[:PAD]),
            (down, (k, head), total[:PAD]),
        ]
        for c in range(3):
            out.append((up, (k, PAD + 1 + c), g[c, i, edge, :]))
            out.append((down, (k, PAD + 1 + c), g[c, i, 0, :]))
        return out

    loop(0, BLOCK, step, 4)
    for copy in copies[2:]:
        copy.wait()

    def edges(i):
        k = BLOCK + i
        out = []
        for c in range(3):
            out.append((up, (i, PAD + c), vel[c, i, edge, :]))
            out.append((down, (i, PAD + c), vel[c, i, 0, :]))
        out.append((up, (i, PAD + 3), vis[i, edge, :]))
        out.append((down, (i, PAD + 3), vis[i, 0, :]))
        out.append((up, (k, PAD), ndg[i, edge, :]))
        out.append((down, (k, PAD), ndg[i, 0, :]))
        return out

    loop(0, BLOCK, edges, 4)
    z = b.shape[2]
    up[2 * BLOCK] = jnp.zeros((BLOCK, z), F32)
    down[2 * BLOCK] = jnp.zeros((BLOCK, z), F32)
    up[2 * BLOCK, 0:PAD, :] = g[0, 0, BLOCK - PAD :, :]
    down[2 * BLOCK, 0:PAD, :] = g[0, 0, :PAD, :]
    for n, plane in enumerate((0, edge)):
        for c in range(3):
            planes[n, c, 0:BLOCK, :] = vel[c, plane]
            planes[n, c, BLOCK : 2 * BLOCK, :] = g[c, plane]
        planes[n, 3, 0:BLOCK, :] = vis[plane]
        planes[n, 3, BLOCK : 2 * BLOCK, :] = ndg[plane]


def rows_body(odd, b, d, down, planes, before, after, bb, dd, g0, even_send, odd_send):
    top = PAD + BLOCK

    def step(i):
        k = BLOCK + i
        own_flux = 0.5 * (b[i, 0:1, :] + before[i, PAD - 1 : PAD, :]) * down[k, PAD + 2 : PAD + 3, :]
        next_flux = (
            0.5
            * (b[i, BLOCK - 1 : BLOCK, :] + after[i, 0:1, :])
            * after[k, PAD + 2 : PAD + 3, :]
        )
        out = []
        for ref, own, m in ((bb, b, i), (dd, d, k)):
            out.append((ref, (i, slice(0, PAD)), before[m, 0:PAD, :]))
            out.append((ref, (i, slice(PAD, top)), own[i]))
            out.append((ref, (i, slice(top, top + PAD)), after[m, 0:PAD, :]))
        out.append((dd, (i, slice(PAD - 1, PAD)), before[k, PAD - 1 : PAD, :] + own_flux))
        out.append((dd, (i, slice(PAD, PAD + 1)), d[i, 0:1, :] - own_flux))
        out.append((dd, (i, slice(top - 1, top)), d[i, BLOCK - 1 : BLOCK, :] + next_flux))
        out.append((dd, (i, slice(top, top + 1)), after[k, 0:1, :] - next_flux))
        return out

    loop(0, BLOCK, step, 4)
    g0[0:PAD, :] = before[2 * BLOCK, 0:PAD, :]
    g0[PAD:top, :] = planes[0, 0, BLOCK : 2 * BLOCK, :]
    g0[top : top + PAD, :] = after[2 * BLOCK, 0:PAD, :]
    is_odd = odd[0]
    for send, last in ((even_send, 1 - is_odd), (odd_send, is_odd)):
        b_start = 5 * last
        d_start = 6 * last

        def b_step(m, send=send, b_start=b_start):
            return [(send, m, bb[b_start + m])]

        def d_step(m, send=send, d_start=d_start):
            return [(send, 11 + m, dd[d_start + m])]

        loop(0, 11, b_step, 11)
        loop(0, 10, d_step, 10)
        send[21] = g0[...]
        for c in range(4):
            send[22 + c, 0 : 2 * BLOCK, :] = planes[last, c]


def fine_body(
    odd, bb, dd, g0, even_got, odd_got,
    gf, x0, nxm, nxp, nym, nyp, nzm, nzp, f1, b1, f2, b2, up, down,
    b, f0, diag, pairs, g1, xb, *rest,
):
    n1, (diag1, pairs1) = rest[:6], rest[6:]
    n0 = (nxm, nxp, nym, nyp, nzm, nzp)
    is_odd = odd[0] == 1
    top = PAD + BLOCK

    def left(m):
        return jnp.where(is_odd, even_got[m], odd_got[m])

    def right(m):
        return jnp.where(is_odd, odd_got[m], even_got[m])

    loop(0, BLOCK, lambda i: [(b, PAD + i, bb[i]), (f0, PAD + i, dd[i])], 4)
    loop(0, 11, lambda m: [(b, 1 + m, left(m)), (b, top + m, right(m))], 4)
    loop(0, 10, lambda m: [(f0, 2 + m, left(11 + m)), (f0, top + m, right(11 + m))], 5)
    flux = 0.5 * (b[PAD] + b[PAD - 1]) * g0[...]
    f0[PAD - 1] = f0[PAD - 1] + flux
    f0[PAD] = f0[PAD] - flux
    flux = 0.5 * (b[top] + b[top - 1]) * right(21)
    f0[top - 1] = f0[top - 1] + flux
    f0[top] = f0[top] - flux

    setup(b, n0, diag, 2, 38, 1.0, U0, f0, gf)
    pre(gf, x0, n0, 3, 37, U0)
    residual_pairs(gf, x0, diag, n0, pairs, 0, 2, 18, U0 // 2)
    row_pairs(pairs, f1, 2, 18, 0, 20, 0)
    plane_pairs(b, pairs, 0, 1, 19)
    row_pairs(pairs, b1, 1, 19, 0, 20, 0)

    z = b.shape[2]
    f1[:, 20:24, :] = jnp.zeros((20, 4, z), F32)
    b1[:, 20:24, :] = jnp.ones((20, 4, z), F32)
    setup(b1, n1, diag1, 2, 18, 0.25, U1, f1, g1)
    pre(g1, xb, n1, 3, 17, U1)
    residual_pairs(g1, xb, diag1, n1, pairs1, 4, 0, 6, U1 // 2)
    row_pairs(pairs1, f2, 0, 6, 4, 6, 5, shift=5)
    plane_pairs(b1, pairs1, 2, 0, 8)
    row_pairs(pairs1, b2, 0, 8, 2, 8, 4, shift=4)

    for send, frow, brow, f1row, b1row in ((up, 5, 4, 9, 8), (down, 6, 6, 10, 11)):
        for m in range(6):
            send[m, 0:5, :] = f2[5 + m, frow : frow + 5, :]
        for m in range(8):
            send[m, 5:11, :] = b2[4 + m, brow : brow + 6, :]
        for m in range(16):
            send[m, 11:12, :] = f1[2 + m, f1row : f1row + 1, :]
        for m in range(18):
            send[m, 12:13, :] = b1[1 + m, b1row : b1row + 1, :]


def rows2_body(odd, f1, b1, f2, b2, before, after, g1, h1, g2, h2, even_send, odd_send):
    g1[...] = f1[...]
    h1[...] = b1[...]
    z = f1.shape[2]
    g2[...] = jnp.zeros((16, 16, z), F32)
    h2[...] = jnp.ones((16, 16, z), F32)
    for m in range(6):
        g2[5 + m, 6:10, :] = f2[5 + m, 6:10, :]
        g2[5 + m, 1:6, :] = before[m, 0:5, :]
        g2[5 + m, 10:15, :] = after[m, 0:5, :]
    for m in range(8):
        h2[4 + m, 6:10, :] = b2[4 + m, 6:10, :]
        h2[4 + m, 0:6, :] = before[m, 5:11, :]
        h2[4 + m, 10:16, :] = after[m, 5:11, :]
    for m in range(16):
        g1[2 + m, 1:2, :] = before[m, 11:12, :]
        g1[2 + m, 18:19, :] = after[m, 11:12, :]
    for m in range(18):
        h1[1 + m, 0:1, :] = before[m, 12:13, :]
        h1[1 + m, 19:20, :] = after[m, 12:13, :]
    is_odd = odd[0]
    for send, last in ((even_send, 1 - is_odd), (odd_send, is_odd)):
        for m in range(5):
            send[m, 0:16, :] = g2[6 - last + m]
        for m in range(6):
            send[5 + m, 0:16, :] = h2[6 - 2 * last + m]
        send[11] = g1[10 - last]
        send[12] = h1[11 - 3 * last]


def level2_body(
    odd, f1i, b1i, f2i, b2i, even_got, odd_got,
    g1, x1, m1, m2, m3, m4, m5, m6, g2, x2, k1, k2, k3, k4, k5, k6, slots,
    f1, b1, f2, b2, diag, pairs,
):
    n1, n2 = (m1, m2, m3, m4, m5, m6), (k1, k2, k3, k4, k5, k6)
    is_odd = odd[0] == 1

    def left(m):
        return jnp.where(is_odd, even_got[0, m], odd_got[0, m])

    def right(m):
        return jnp.where(is_odd, odd_got[1, m], even_got[1, m])

    f1[...] = f1i[...]
    b1[...] = b1i[...]
    f2[...] = f2i[...]
    b2[...] = b2i[...]
    for m in range(5):
        f2[1 + m] = left(m)[0:16]
        f2[10 + m] = right(m)[0:16]
    for m in range(6):
        b2[m] = left(5 + m)[0:16]
        b2[10 + m] = right(5 + m)[0:16]
    f1[1] = left(11)
    f1[18] = right(11)
    b1[0] = left(12)
    b1[19] = right(12)
    setup(b2, n2, diag, 1, 15, 0.25**2, U2, f2, g2)
    pre(g2, x2, n2, 2, 14, U2)
    residual_pairs(g2, x2, diag, n2, pairs, 6, 0, 2, 2)
    parts = []
    for _ in range(2):
        for m in range(2):
            even = pairs[m, pl.ds(6, 2, 2), :]
            parts.append(0.25 * (even + pairs[m, pl.ds(7, 2, 2), :]))
        if len(parts) == 2:
            plane_pairs(b2, pairs, 6, 0, 2)
    for m in range(16):
        for n in range(4):
            slots[m, 2 * n : 2 * n + 2, :] = parts[n]
    setup(b1, n1, None, 1, 19, 0.25, U1, f1, g1)
    pre(g1, x1, n1, 2, 18, U1)


def column_body(place, got, slots):
    def step(p):
        source = lax.rem(place[0] + (p + 8), 16)
        block = got[source]
        for n in range(4):
            slots[0, n, pl.ds(2 * p, 2), :] = block[2 * n : 2 * n + 2]

    for p in range(16):
        step(p)

    def spread(m):
        return [(slots, (m, n), slots[0, n]) for n in range(4)]

    loop(1, 32, spread)


def up_body(place, got, *refs):
    refs = list(refs)

    def take(count):
        head = tuple(refs[:count])
        del refs[:count]
        return head

    g1, x1 = take(2)
    n1 = take(6)
    g2, x2 = take(2)
    n2 = take(6)
    g0, x0 = take(2)
    n0 = take(6)
    vel, vis, g, ndg, before, after, even_got, odd_got = take(8)
    out_vel, out_ndg, out_vis = take(3)
    f3, b3, g3, x3, diag = take(5)
    n3 = take(6)
    (pairs,) = take(1)
    f4, b4, g4, xa4, xb4, e4 = take(6)
    n4 = take(6)
    w3, y3, t3, v2, w2, y2, t2, v1, w1, y1, t1, v0, w0, y0, t0 = take(15)
    vp, ap, visp, np_ = take(4)
    devices = 2 * WIN + 1

    def gather(q):
        source = lax.rem(place[1] + (q + 32 - WIN), 32)
        out = []
        for n in range(2):
            out.append((f3, 2 * q + n, got[source, n]))
            out.append((b3, 2 * q + n, got[source, 2 + n]))
        return out

    loop(0, devices, gather, 2)
    last = 2 * devices - 1
    setup(b3, n3, diag, 1, last, 0.25**3, U0, f3, g3)
    pre(g3, x3, n3, 2, last - 1, U0)
    residual_pairs(g3, x3, diag, n3, pairs, 0, 2, devices - 2, U0 // 2)
    row_pairs(pairs, f4, 2, devices - 2, 0, 16, 0)
    plane_pairs(b3, pairs, 0, 0, devices)
    row_pairs(pairs, b4, 0, devices, 0, 16, 0)
    low, high = 2, devices - 2
    setup(b4, n4, None, low, high, 0.25**4, U2, f4, g4)

    def start(i):
        u = g4[i] * (1.0 / MID)
        return [(e4, i, u), (xa4, i, u)]

    loop(low, high, start, U2)
    ratio = RHO0
    x_now, x_next = xa4, xb4
    for _ in range(5):
        following = 1.0 / (2.0 * SIGMA - ratio)
        low, high = low + 1, high - 1

        def sweep(i, x_now=x_now, x_next=x_next, following=following, ratio=ratio):
            q0 = x_now[i]
            scaled = (g4[i] - q0) + around_sum(x_now, n4, i, q0)
            u = following * ratio * e4[i] + (2.0 * following / HALF) * scaled
            return [(e4, i, u), (x_next, i, q0 + u)]

        loop(low, high, sweep, U2)
        ratio = following
        x_now, x_next = x_next, x_now
    correct(x3, x_now, w3, 7, 12, 0, 0, 16, 0)
    post(x3, g3, y3, t3, n3, 16, 22, U0)
    correct(x2, t3, w2, 16, 22, -30, 14, 6, 2, out=v2)
    post(v2, g2, y2, t2, n2, 4, 12, U2)
    correct(x1, t2, w1, 4, 12, -6, 4, 8, 2, out=v1)
    post(v1, g1, y1, t1, n1, 4, 16, U1)
    correct(x0, t1, w0, 4, 16, 0, 4, 12, 8, 2, out=v0)
    post(v0, g0, y0, t0, n0, 10, 29, U0)

    def pad(i):
        k = BLOCK + i

        def put(out, own, source, row):
            out[0:1, :] = before[source, row : row + 1, :]
            out[1:17, :] = own
            out[17:18, :] = after[source, row : row + 1, :]

        for c in range(3):
            put(vp.at[c, i + 1], vel[c, i], i, PAD + c)
            put(ap.at[c, i + 1], g[c, i], k, PAD + 1 + c)
        put(visp.at[i + 1], vis[i], i, PAD + 3)
        put(np_.at[i + 1], ndg[i], k, PAD)

    loop(0, BLOCK, pad, 2)
    is_odd = lax.rem(place[1], 2) == 1

    def left(m):
        return jnp.where(is_odd, even_got[m], odd_got[m])

    def right(m):
        return jnp.where(is_odd, odd_got[m], even_got[m])

    for plane, side in ((0, left), (BLOCK + 1, right)):
        for c in range(3):
            both = side(22 + c)
            vp[c, plane, 1:17, :] = both[0:BLOCK]
            ap[c, plane, 1:17, :] = both[BLOCK : 2 * BLOCK]
        both = side(25)
        visp[plane, 1:17, :] = both[0:BLOCK]
        np_[plane, 1:17, :] = both[BLOCK : 2 * BLOCK]

    def lift(m):
        centre = t0[m + 11, 11:35, :]
        return [
            (ap, (0, m), ap[0, m] + (centre - t0[m + 10, 11:35, :])),
            (ap, (1, m), ap[1, m] + (centre - t0[m + 11, 10:34, :])),
            (ap, (2, m), ap[2, m] + (centre - zdn(centre))),
        ]

    loop(0, BLOCK + 2, lift, 3)

    def finish(i):
        m = i + 1

        def around(ref):
            return (
                ref[m, 1:17, :],
                ref[m - 1, 1:17, :],
                ref[m + 1, 1:17, :],
                ref[m, 0:16, :],
                ref[m, 2:18, :],
            )

        speeds = [around(vp.at[c]) for c in range(3)]
        n0, nxm, nxp, nym, nyp = around(visp)
        fxm, fxp = 0.5 * (n0 + nxm), 0.5 * (nxp + n0)
        fym, fyp = 0.5 * (n0 + nym), 0.5 * (nyp + n0)
        fz = 0.5 * (n0 + zdn_copy(n0))
        u0m, u0p = speeds[0][1], speeds[0][2]
        u1m, u1p = speeds[1][3], speeds[1][4]
        u2 = speeds[2][0]

        def transport(q0, qxm, qxp, qym, qyp):
            up = u2 * q0
            return 0.5 * ((u0p * qxp - u0m * qxm) + (u1p * qyp - u1m * qym) + (zup(up) - zdn(up)))

        fields = around(np_)
        out_ndg[i] = fields[0] + DT * transport(*fields)
        gxm = gxp = gym = gyp = gz = 0.0
        for c in range(3):
            fields = around(ap.at[c])
            q0, qxm, qxp, qym, qyp = fields
            s0, sxm, sxp, sym, syp = speeds[c]
            dxm, dxp, dym, dyp = q0 - qxm, qxp - q0, q0 - qym, qyp - q0
            dz = q0 - zdn(q0)
            flux = fz * dz
            spread = (fxp * dxp - fxm * dxm) + (fyp * dyp - fym * dym) + (zup(flux) - flux)
            out_vel[c, i] = q0 + DT * (transport(*fields) + spread)
            gxm = gxm + dxm * (s0 - sxm)
            gxp = gxp + dxp * (sxp - s0)
            gym = gym + dym * (s0 - sym)
            gyp = gyp + dyp * (syp - s0)
            gz = gz + dz * (s0 - zdn(s0))
        bottom = jnp.where(layer(gz) == 0, gz, 0.0)
        out_vis[i] = (-0.5 * DT) * ((gxm + gxp) + (gym + gyp) + (gz + zup(gz)) + bottom)

    loop(0, BLOCK, finish, 2)


def shards(velocity, density, viscosity, grad_out, density_gradient):
    z = density.shape[2]
    size_x, size_y = lax.axis_size("gx"), lax.axis_size("gy")
    at_x, at_y = lax.axis_index("gx"), lax.axis_index("gy")
    odd = lax.rem(at_x, 2).astype(jnp.int32).reshape(1)
    place = jnp.stack([at_y, at_x]).astype(jnp.int32)
    even_pairs = [[i, i + 1] for i in range(0, size_x, 2)]
    odd_pairs = [[i, (i + 1) % size_x] for i in range(1, size_x, 2)]
    forward = [(i, (i + 1) % size_y) for i in range(size_y)]
    backward = [(j, i) for i, j in forward]

    def along_y(up, down):
        return lax.ppermute(up, "gy", forward), lax.ppermute(down, "gy", backward)

    def swapped(block, pairs):
        return lax.ppermute(block, "gx", [q for i, j in pairs for q in ((i, j), (j, i))])

    fine = (40, 40, z)
    mid = (20, 24, z)
    low = (16, 16, z)
    rim = (2 * BLOCK + 1, BLOCK, z)
    own = (BLOCK, BLOCK, z)
    fields = (velocity, viscosity, grad_out, density_gradient)
    up, down, b, d, planes = call(
        own_body,
        [rim, rim, own, own, (2, 4, 2 * BLOCK, z)],
        (velocity, density, viscosity, grad_out, density_gradient),
        [(3, *own), own, own, (3, *own), own],
        fetched=5,
        sems=5,
    )
    before, after = along_y(up, down)
    send = (26, 40, z)
    bb, dd, g0, even_send, odd_send = call(
        rows_body,
        [(BLOCK, 40, z), (BLOCK, 40, z), (40, z), send, send],
        (odd, b, d, down, planes, before, after),
        scalars=1,
    )
    even_got = swapped(even_send, even_pairs)
    odd_got = swapped(odd_send, odd_pairs)
    fine_out = call(
        fine_body,
        [fine] * 8 + [mid, mid, low, low, (18, 16, z), (18, 16, z)],
        (odd, bb, dd, g0, even_got, odd_got),
        [fine, fine, fine, (20, 40, z)] + [mid] * 9 + [(8, 24, z)],
        scalars=1,
    )
    f1, b1, f2, b2, up, down = fine_out[8:]
    before2, after2 = along_y(up, down)
    send2 = (13, 24, z)
    f1, b1, f2, b2, even_send, odd_send = call(
        rows2_body,
        [mid, mid, low, low, send2, send2],
        (odd, f1, b1, f2, b2, before2, after2),
        scalars=1,
    )
    even_got2 = lax.all_gather(even_send, "gx", axis_index_groups=even_pairs)
    odd_got2 = lax.all_gather(odd_send, "gx", axis_index_groups=odd_pairs)
    coarse = call(
        level2_body,
        [mid] * 8 + [low] * 8 + [(size_y, 8, z)],
        (odd, f1, b1, f2, b2, even_got2, odd_got2),
        [mid, mid, low, low, low, (2, 16, z)],
        scalars=1,
    )
    got = lax.all_to_all(coarse[-1], "gy", 0, 0, tiled=True)
    (slots,) = call(column_body, [(size_x, 4, 2 * size_y, z)], (place, got), scalars=1)
    got = lax.all_to_all(slots, "gx", 0, 0, tiled=True)
    devices = 2 * WIN + 1
    level3 = (2 * devices, 32, z)
    level4 = (devices, 16, z)
    return tuple(
        call(
            up_body,
            [(3, *own), own, own],
            (place, got, *coarse[:-1], *fine_out[:8], *fields, before, after, even_got, odd_got),
            [level3] * 11
            + [(devices, 32, z)]
            + [level4] * 12
            + [(12, 32, z), level3, level3]
            + [low, (22, 16, z), low, low]
            + [mid, (12, 24, z), mid, mid]
            + [fine, (16, 40, z), fine, fine]
            + [(3, 18, 24, z), (3, 18, 24, z), (18, 24, z), (18, 24, z)],
            scalars=1,
            megabytes=24,
        )
    )


def solution(mesh):
    placed = (
        P(None, "gx", "gy", None),
        P("gx", "gy", None),
        P("gx", "gy", None),
        P(None, "gx", "gy", None),
        P("gx", "gy", None),
    )
    return jax.shard_map(
        shards,
        mesh=mesh,
        in_specs=placed,
        out_specs=(P(None, "gx", "gy", None), P("gx", "gy", None), P("gx", "gy", None)),
        check_vma=False,
    )
```

```python
import functools

import jax
import jax.numpy as jnp
from jax import lax
from jax.experimental import pallas as pl
from jax.experimental.pallas import tpu as pltpu
from jax.sharding import PartitionSpec as P

INTERPRET = False
DT = 0.2
MID = 1.2
HALF = 0.8
SIGMA = MID / HALF
RHO0 = 1.0 / SIGMA
RHO1 = 1.0 / (2.0 * SIGMA - RHO0)
A1 = RHO1 * RHO0
B1 = 2.0 * RHO1 / HALF
BLOCK = 16
PAD = 12
PAD1 = 6
U0, U1, U2 = 4, 4, 6
WIN = 8
F32 = jnp.float32


def call(body, out_shapes, args, scratch=(), scalars=0, megabytes=16, fetched=0, kept=0, sems=0):
    smem = [pl.BlockSpec(memory_space=pltpu.SMEM)] * scalars
    far = pl.BlockSpec(memory_space=pltpu.HBM)
    near = pl.BlockSpec(memory_space=pltpu.VMEM)
    scratch = [pltpu.VMEM(s, F32) for s in scratch]
    if sems:
        scratch.append(pltpu.SemaphoreType.DMA((sems,)))
    return pl.pallas_call(
        body,
        out_shape=[jax.ShapeDtypeStruct(s, F32) for s in out_shapes],
        in_specs=smem + [far] * fetched + [near] * (len(args) - scalars - fetched),
        out_specs=[near] * (len(out_shapes) - kept) + [far] * kept,
        scratch_shapes=scratch,
        compiler_params=pltpu.CompilerParams(vmem_limit_bytes=megabytes * 2**20),
        interpret=INTERPRET,
    )(*args)


def loop(low, high, step, unroll=1):
    def group(base, count):
        stores = []
        for u in range(count):
            stores.extend(step(base + u) or ())
        for ref, index, value in stores:
            ref[index] = value

    groups = (high - low) // unroll
    if groups == 1:
        group(low, unroll)
    elif groups > 1:
        lax.fori_loop(0, groups, lambda n, c: (group(low + n * unroll, unroll), c)[1], 0)
    rest = (high - low) - groups * unroll
    if rest:
        group(high - rest, rest)


def ydn(v):
    return pltpu.roll(v, 1, axis=0)


def yup(v):
    return pltpu.roll(v, v.shape[0] - 1, axis=0)


def layer(v):
    return lax.broadcasted_iota(jnp.int32, v.shape, 1)


def zroll_dn(v):
    return pltpu.roll(v, 1, axis=1)


def zroll_up(v):
    return pltpu.roll(v, v.shape[1] - 1, axis=1)


def zdn(v):
    return jnp.where(layer(v) == 0, 0.0, zroll_dn(v))


def zdn_copy(v):
    return jnp.where(layer(v) == 0, v, zroll_dn(v))


def zup(v):
    return jnp.where(layer(v) == v.shape[1] - 1, 0.0, zroll_up(v))


def setup(b, n, diag, low, high, scale, unroll, f=None, g=None, g_range=None):
    half = 0.5 * scale

    def step(i):
        b0 = b[i]
        fxm = half * (b0 + b[i - 1])
        fxp = half * (b[i + 1] + b0)
        fym = half * (b0 + ydn(b0))
        fyp = yup(fym)
        fz = 0.5 * (b0 + zdn_copy(b0))
        fzp = zup(fz)
        d = (fxm + fxp) + (fym + fyp) + (fz + fzp)
        inv = 1.0 / d
        fzm = jnp.where(layer(fz) == 0, 0.0, fz)
        out = [(ref, i, v * inv) for ref, v in zip(n, (fxm, fxp, fym, fyp, fzm, fzp), strict=True)]
        if diag is not None:
            out.append((diag, i, d))
        if f is not None:
            out.append((g, i, f[i] * inv))
        return out

    loop(low, high, step, unroll)


def around_sum(q, n, i, q0):
    total = (n[0][i] * q[i - 1] + n[1][i] * q[i + 1]) + (n[2][i] * ydn(q0) + n[3][i] * yup(q0))
    return total + (n[4][i] * zroll_dn(q0) + n[5][i] * zroll_up(q0))


def pre(g, x, n, low, high, unroll):
    first = (1.0 + A1) / MID + B1 * (1.0 - 1.0 / MID)

    def step(i):
        g0 = g[i]
        return [(x, i, first * g0 + (B1 / MID) * around_sum(g, n, i, g0))]

    loop(low, high, step, unroll)


def post(x, g, y, out, n, low, high, unroll):
    def first(i):
        x0 = x[i]
        return [(y, i, x0 + (1.0 / MID) * ((g[i] - x0) + around_sum(x, n, i, x0)))]

    loop(low - 1, high + 1, first, unroll)

    def second(i):
        y0 = y[i]
        z = (g[i] - y0) + around_sum(y, n, i, y0)
        return [(out, i, y0 + (A1 * (y0 - x[i]) + B1 * z))]

    loop(low, high, second, unroll)


def residual_pairs(g, x, diag, n, pairs, start, low, high, unroll):
    def one(i):
        x0 = x[i]
        return diag[i] * ((g[i] - x0) + around_sum(x, n, i, x0))

    def step(m):
        i = start + 2 * m
        return [(pairs, m, one(i) + one(i + 1))]

    loop(low, high, step, unroll)


def plane_pairs(b, pairs, start, low, high, unroll=4):
    def step(m):
        return [(pairs, m, b[start + 2 * m] + b[start + 2 * m + 1])]

    loop(low, high, step, unroll)


def row_pairs(pairs, coarse, low, high, row, count, target, shift=0, unroll=8):
    def step(m):
        even = pairs[m, pl.ds(row, count, 2), :]
        odd = pairs[m, pl.ds(row + 1, count, 2), :]
        return [(coarse, (m + shift, slice(target, target + count)), 0.25 * (even + odd))]

    loop(low, high, step, unroll)


def correct(x, coarse, wide, low, high, plane, row, count, target, unroll=4, out=None):
    def widen(m):
        v = coarse[m, row : row + count, :]
        return [
            (wide, (m, pl.ds(target, count, 2)), v),
            (wide, (m, pl.ds(target + 1, count, 2)), v),
        ]

    loop(low, high, widen, 2 * unroll)
    out = x if out is None else out

    def add(m):
        i = 2 * m + plane
        w = wide[m]
        return [(out, i, x[i] + w), (out, i + 1, x[i + 1] + w)]

    loop(low, high, add, unroll)


def own_body(
    vel_in, den_in, vis_in, g_in, ndg_in, up, down, b, d, planes, vel, den, vis, g, ndg, sems
):
    pairs = ((den_in, den), (g_in, g), (vel_in, vel), (vis_in, vis), (ndg_in, ndg))
    copies = [pltpu.make_async_copy(s, t, sems.at[n]) for n, (s, t) in enumerate(pairs)]
    for copy in copies:
        copy.start()
    copies[0].wait()

    def invert(i):
        return [(b, i, 1.0 / den[i])]

    loop(0, BLOCK, invert, 8)
    copies[1].wait()
    edge = BLOCK - 1

    def step(i):
        b0 = b[i]
        fz = 0.5 * (b0 + zdn_copy(b0)) * g[2, i]
        fy = 0.5 * (b0 + ydn(b0)) * g[1, i]
        rows = lax.broadcasted_iota(jnp.int32, fy.shape, 0)
        fy = jnp.where(rows == 0, 0.0, fy)
        total = (zup(fz) - fz) + (yup(fy) - fy)
        left = jnp.maximum(i - 1, 0)
        right = jnp.minimum(i + 1, edge)
        inner = jnp.where(i > 0, 0.5, 0.0) * (b0 + b[left]) * g[0, i]
        outer = jnp.where(i < edge, 0.5, 0.0) * (b0 + b[right]) * g[0, right]
        total = total + (outer - inner)
        k = BLOCK + i
        head = slice(0, PAD)
        out = [
            (d, i, total),
            (up, (i, head), b0[BLOCK - PAD :]),
            (up, (k, head), total[BLOCK - PAD :]),
            (down, (i, head), b0[:PAD]),
            (down, (k, head), total[:PAD]),
        ]
        for c in range(3):
            out.append((up, (k, PAD + 1 + c), g[c, i, edge, :]))
            out.append((down, (k, PAD + 1 + c), g[c, i, 0, :]))
        return out

    loop(0, BLOCK, step, 4)
    for copy in copies[2:]:
        copy.wait()

    def edges(i):
        k = BLOCK + i
        out = []
        for c in range(3):
            out.append((up, (i, PAD + c), vel[c, i, edge, :]))
            out.append((down, (i, PAD + c), vel[c, i, 0, :]))
        out.append((up, (i, PAD + 3), vis[i, edge, :]))
        out.append((down, (i, PAD + 3), vis[i, 0, :]))
        out.append((up, (k, PAD), ndg[i, edge, :]))
        out.append((down, (k, PAD), ndg[i, 0, :]))
        return out

    loop(0, BLOCK, edges, 4)
    z = b.shape[2]
    up[2 * BLOCK] = jnp.zeros((BLOCK, z), F32)
    down[2 * BLOCK] = jnp.zeros((BLOCK, z), F32)
    up[2 * BLOCK, 0:PAD, :] = g[0, 0, BLOCK - PAD :, :]
    down[2 * BLOCK, 0:PAD, :] = g[0, 0, :PAD, :]
    for n, plane in enumerate((0, edge)):
        for c in range(3):
            planes[n, c, 0:BLOCK, :] = vel[c, plane]
            planes[n, c, BLOCK : 2 * BLOCK, :] = g[c, plane]
        planes[n, 3, 0:BLOCK, :] = vis[plane]
        planes[n, 3, BLOCK : 2 * BLOCK, :] = ndg[plane]


def rows_body(odd, b, d, down, planes, before, after, bb, dd, g0, even_send, odd_send):
    top = PAD + BLOCK

    def step(i):
        k = BLOCK + i
        own_flux = 0.5 * (b[i, 0:1, :] + before[i, PAD - 1 : PAD, :]) * down[k, PAD + 2 : PAD + 3, :]
        next_flux = (
            0.5
            * (b[i, BLOCK - 1 : BLOCK, :] + after[i, 0:1, :])
            * after[k, PAD + 2 : PAD + 3, :]
        )
        out = []
        for ref, own, m in ((bb, b, i), (dd, d, k)):
            out.append((ref, (i, slice(0, PAD)), before[m, 0:PAD, :]))
            out.append((ref, (i, slice(PAD, top)), own[i]))
            out.append((ref, (i, slice(top, top + PAD)), after[m, 0:PAD, :]))
        out.append((dd, (i, slice(PAD - 1, PAD)), before[k, PAD - 1 : PAD, :] + own_flux))
        out.append((dd, (i, slice(PAD, PAD + 1)), d[i, 0:1, :] - own_flux))
        out.append((dd, (i, slice(top - 1, top)), d[i, BLOCK - 1 : BLOCK, :] + next_flux))
        out.append((dd, (i, slice(top, top + 1)), after[k, 0:1, :] - next_flux))
        return out

    loop(0, BLOCK, step, 4)
    g0[0:PAD, :] = before[2 * BLOCK, 0:PAD, :]
    g0[PAD:top, :] = planes[0, 0, BLOCK : 2 * BLOCK, :]
    g0[top : top + PAD, :] = after[2 * BLOCK, 0:PAD, :]
    is_odd = odd[0]
    for send, last in ((even_send, 1 - is_odd), (odd_send, is_odd)):
        b_start = 5 * last
        d_start = 6 * last

        def b_step(m, send=send, b_start=b_start):
            return [(send, m, bb[b_start + m])]

        def d_step(m, send=send, d_start=d_start):
            return [(send, 11 + m, dd[d_start + m])]

        loop(0, 11, b_step, 11)
        loop(0, 10, d_step, 10)
        send[21] = g0[...]
        for c in range(4):
            send[22 + c, 0 : 2 * BLOCK, :] = planes[last, c]


def fine_body(
    odd, bb, dd, g0, even_got, odd_got,
    f1, b1, f2, b2, up, down, kept,
    pack, b, f0, diag, pairs, g1, xb, *rest,
):
    n1, (diag1, pairs1, sems) = rest[:6], rest[6:]
    gf, x0 = pack.at[0], pack.at[7]
    n0 = tuple(pack.at[n] for n in range(1, 7))
    keep = slice(8, 32)
    saves = (
        pltpu.make_async_copy(pack.at[0:7, keep], kept.at[0:7], sems.at[0]),
        pltpu.make_async_copy(pack.at[7, keep], kept.at[7], sems.at[1]),
    )
    is_odd = odd[0] == 1
    top = PAD + BLOCK

    def left(m):
        return jnp.where(is_odd, even_got[m], odd_got[m])

    def right(m):
        return jnp.where(is_odd, odd_got[m], even_got[m])

    loop(0, BLOCK, lambda i: [(b, PAD + i, bb[i]), (f0, PAD + i, dd[i])], 4)
    loop(0, 11, lambda m: [(b, 1 + m, left(m)), (b, top + m, right(m))], 4)
    loop(0, 10, lambda m: [(f0, 2 + m, left(11 + m)), (f0, top + m, right(11 + m))], 5)
    flux = 0.5 * (b[PAD] + b[PAD - 1]) * g0[...]
    f0[PAD - 1] = f0[PAD - 1] + flux
    f0[PAD] = f0[PAD] - flux
    flux = 0.5 * (b[top] + b[top - 1]) * right(21)
    f0[top - 1] = f0[top - 1] + flux
    f0[top] = f0[top] - flux

    setup(b, n0, diag, 2, 38, 1.0, U0, f0, gf)
    saves[0].start()
    pre(gf, x0, n0, 3, 37, U0)
    saves[1].start()
    residual_pairs(gf, x0, diag, n0, pairs, 0, 2, 18, U0 // 2)
    row_pairs(pairs, f1, 2, 18, 0, 20, 0)
    plane_pairs(b, pairs, 0, 1, 19)
    row_pairs(pairs, b1, 1, 19, 0, 20, 0)

    z = b.shape[2]
    f1[:, 20:24, :] = jnp.zeros((20, 4, z), F32)
    b1[:, 20:24, :] = jnp.ones((20, 4, z), F32)
    setup(b1, n1, diag1, 2, 18, 0.25, U1, f1, g1)
    pre(g1, xb, n1, 3, 17, U1)
    residual_pairs(g1, xb, diag1, n1, pairs1, 4, 0, 6, U1 // 2)
    row_pairs(pairs1, f2, 0, 6, 4, 6, 5, shift=5)
    plane_pairs(b1, pairs1, 2, 0, 8)
    row_pairs(pairs1, b2, 0, 8, 2, 8, 4, shift=4)

    for send, frow, brow, f1row, b1row in ((up, 5, 4, 9, 8), (down, 6, 6, 10, 11)):
        for m in range(6):
            send[m, 0:5, :] = f2[5 + m, frow : frow + 5, :]
        for m in range(8):
            send[m, 5:11, :] = b2[4 + m, brow : brow + 6, :]
        for m in range(16):
            send[m, 11:12, :] = f1[2 + m, f1row : f1row + 1, :]
        for m in range(18):
            send[m, 12:13, :] = b1[1 + m, b1row : b1row + 1, :]
    for save in saves:
        save.wait()


def rows2_body(odd, f1, b1, f2, b2, before, after, g1, h1, g2, h2, even_send, odd_send):
    g1[...] = f1[...]
    h1[...] = b1[...]
    z = f1.shape[2]
    g2[...] = jnp.zeros((16, 16, z), F32)
    h2[...] = jnp.ones((16, 16, z), F32)
    for m in range(6):
        g2[5 + m, 6:10, :] = f2[5 + m, 6:10, :]
        g2[5 + m, 1:6, :] = before[m, 0:5, :]
        g2[5 + m, 10:15, :] = after[m, 0:5, :]
    for m in range(8):
        h2[4 + m, 6:10, :] = b2[4 + m, 6:10, :]
        h2[4 + m, 0:6, :] = before[m, 5:11, :]
        h2[4 + m, 10:16, :] = after[m, 5:11, :]
    for m in range(16):
        g1[2 + m, 1:2, :] = before[m, 11:12, :]
        g1[2 + m, 18:19, :] = after[m, 11:12, :]
    for m in range(18):
        h1[1 + m, 0:1, :] = before[m, 12:13, :]
        h1[1 + m, 19:20, :] = after[m, 12:13, :]
    is_odd = odd[0]
    for send, last in ((even_send, 1 - is_odd), (odd_send, is_odd)):
        for m in range(5):
            send[m, 0:16, :] = g2[6 - last + m]
        for m in range(6):
            send[5 + m, 0:16, :] = h2[6 - 2 * last + m]
        send[11] = g1[10 - last]
        send[12] = h1[11 - 3 * last]


def level2_body(
    odd, f1i, b1i, f2i, b2i, even_got, odd_got,
    slots, kept1, kept2,
    pack1, pack2, f1, b1, f2, b2, diag, pairs, sems,
):
    g1, x1, n1 = pack1.at[0], pack1.at[7], tuple(pack1.at[n] for n in range(1, 7))
    g2, x2, n2 = pack2.at[0], pack2.at[7], tuple(pack2.at[n] for n in range(1, 7))
    save1 = pltpu.make_async_copy(pack1, kept1, sems.at[0])
    save2 = pltpu.make_async_copy(pack2, kept2, sems.at[1])
    is_odd = odd[0] == 1

    def left(m):
        return jnp.where(is_odd, even_got[0, m], odd_got[0, m])

    def right(m):
        return jnp.where(is_odd, odd_got[1, m], even_got[1, m])

    f1[...] = f1i[...]
    b1[...] = b1i[...]
    f2[...] = f2i[...]
    b2[...] = b2i[...]
    for m in range(5):
        f2[1 + m] = left(m)[0:16]
        f2[10 + m] = right(m)[0:16]
    for m in range(6):
        b2[m] = left(5 + m)[0:16]
        b2[10 + m] = right(5 + m)[0:16]
    f1[1] = left(11)
    f1[18] = right(11)
    b1[0] = left(12)
    b1[19] = right(12)
    setup(b2, n2, diag, 1, 15, 0.25**2, U2, f2, g2)
    pre(g2, x2, n2, 2, 14, U2)
    save2.start()
    residual_pairs(g2, x2, diag, n2, pairs, 6, 0, 2, 2)
    parts = []
    for _ in range(2):
        for m in range(2):
            even = pairs[m, pl.ds(6, 2, 2), :]
            parts.append(0.25 * (even + pairs[m, pl.ds(7, 2, 2), :]))
        if len(parts) == 2:
            plane_pairs(b2, pairs, 6, 0, 2)
    for m in range(16):
        for n in range(4):
            slots[m, 2 * n : 2 * n + 2, :] = parts[n]
    setup(b1, n1, None, 1, 19, 0.25, U1, f1, g1)
    pre(g1, x1, n1, 2, 18, U1)
    save1.start()
    save1.wait()
    save2.wait()


def column_body(place, got, block):
    for p in range(16):
        source = lax.rem(place[0] + (p + 8), 16)
        rows = got[source]
        for n in range(4):
            block[n, 2 * p : 2 * p + 2, :] = rows[2 * n : 2 * n + 2]


def level3_body(odd, chip, other, far, slots, kept, pack, f3, b3, diag, pairs, small, sems):
    g3, x3, n3 = pack.at[0], pack.at[7], tuple(pack.at[n] for n in range(1, 7))
    save = pltpu.make_async_copy(pack, kept, sems.at[0])
    is_odd = odd[0] == 1
    blocks = [(other, (0, 0)), (other, (0, 1)), (chip, (0,)), (chip, (1,))]
    blocks += [(other, (1, 0)), (other, (1, 1))]
    for p in range(7):
        ref_even, at_even = (far, (0,)) if p == 0 else blocks[p - 1]
        ref_odd, at_odd = (far, (1,)) if p == 6 else blocks[p]
        for n in range(2):
            for out, k in ((f3, n), (b3, 2 + n)):
                even, odds = ref_even[(*at_even, k)], ref_odd[(*at_odd, k)]
                out[2 * p + n] = jnp.where(is_odd, odds, even)
    setup(b3, n3, diag, 1, 13, 0.25**3, U0, f3, g3)
    pre(g3, x3, n3, 2, 12, 5)
    save.start()
    residual_pairs(g3, x3, diag, n3, pairs, 6, 0, 1, 1)
    row_pairs(pairs, small, 0, 1, 0, 16, 0)
    plane_pairs(b3, pairs, 6, 0, 1)
    row_pairs(pairs, small, 0, 1, 0, 16, 0, shift=1)

    def spread(m):
        return [(slots, (m, n), small[n]) for n in range(2)]

    loop(0, 32, spread, 4)
    save.wait()


def up_body(place, *refs):
    refs = list(refs)

    def take(count):
        head = tuple(refs[:count])
        del refs[:count]
        return head

    kept = take(8)
    got, before, after, even_got, odd_got = take(5)
    out_vel, out_ndg, out_vis = take(3)
    pack3, pack2, pack1, pack0, vel, vis, g, ndg = held = take(8)
    f4, b4, g4, xa4, xb4, e4 = take(6)
    n4 = take(6)
    w3, v3, y3, t3, v2, w2, y2, t2, v1, w1, y1, t1, v0, w0, y0, t0 = take(16)
    vp, ap, visp, np_ = take(4)
    (sems,) = refs
    (g3, x3, n3), (g2, x2, n2), (g1, x1, n1), (g0, x0, n0) = (
        (pack.at[0], pack.at[7], tuple(pack.at[n] for n in range(1, 7)))
        for pack in (pack3, pack2, pack1, pack0)
    )
    targets = list(held)
    targets[3] = pack0.at[:, 8:32]
    loads = [
        pltpu.make_async_copy(source, target, sems.at[n])
        for n, (source, target) in enumerate(zip(kept, targets, strict=True))
    ]
    for load in loads:
        load.start()
    devices = 2 * WIN + 1

    def gather(q):
        source = lax.rem(place[1] + (q + 32 - WIN), 32)
        return [(f4, q, got[source, 0]), (b4, q, got[source, 1])]

    loop(0, devices, gather, devices)
    low, high = 1, devices - 1
    setup(b4, n4, None, low, high, 0.25**4, U2, f4, g4)

    def start(i):
        u = g4[i] * (1.0 / MID)
        return [(e4, i, u), (xa4, i, u)]

    loop(low, high, start, U2)
    ratio = RHO0
    x_now, x_next = xa4, xb4
    for _ in range(5):
        following = 1.0 / (2.0 * SIGMA - ratio)
        low, high = low + 1, high - 1

        def sweep(i, x_now=x_now, x_next=x_next, following=following, ratio=ratio):
            q0 = x_now[i]
            scaled = (g4[i] - q0) + around_sum(x_now, n4, i, q0)
            u = following * ratio * e4[i] + (2.0 * following / HALF) * scaled
            return [(e4, i, u), (x_next, i, q0 + u)]

        loop(low, high, sweep, U2)
        ratio = following
        x_now, x_next = x_next, x_now
    loads[0].wait()
    correct(x3, x_now, w3, 6, 11, -10, 0, 16, 0, out=v3)
    post(v3, g3, y3, t3, n3, 4, 10, U0)
    loads[1].wait()
    correct(x2, t3, w2, 4, 10, -6, 14, 6, 2, out=v2)
    post(v2, g2, y2, t2, n2, 4, 12, U2)
    loads[2].wait()
    correct(x1, t2, w1, 4, 12, -6, 4, 8, 2, out=v1)
    post(v1, g1, y1, t1, n1, 4, 16, U1)
    loads[3].wait()
    correct(x0, t1, w0, 4, 16, 0, 4, 12, 8, 2, out=v0)
    post(v0, g0, y0, t0, n0, 10, 29, U0)
    for load in loads[4:]:
        load.wait()

    def pad(i):
        k = BLOCK + i

        def put(out, own, source, row):
            out[0:1, :] = before[source, row : row + 1, :]
            out[1:17, :] = own
            out[17:18, :] = after[source, row : row + 1, :]

        for c in range(3):
            put(vp.at[c, i + 1], vel[c, i], i, PAD + c)
            put(ap.at[c, i + 1], g[c, i], k, PAD + 1 + c)
        put(visp.at[i + 1], vis[i], i, PAD + 3)
        put(np_.at[i + 1], ndg[i], k, PAD)

    loop(0, BLOCK, pad, 2)
    is_odd = lax.rem(place[1], 2) == 1

    def left(m):
        return jnp.where(is_odd, even_got[m], odd_got[m])

    def right(m):
        return jnp.where(is_odd, odd_got[m], even_got[m])

    for plane, side in ((0, left), (BLOCK + 1, right)):
        for c in range(3):
            both = side(22 + c)
            vp[c, plane, 1:17, :] = both[0:BLOCK]
            ap[c, plane, 1:17, :] = both[BLOCK : 2 * BLOCK]
        both = side(25)
        visp[plane, 1:17, :] = both[0:BLOCK]
        np_[plane, 1:17, :] = both[BLOCK : 2 * BLOCK]

    def lift(m):
        centre = t0[m + 11, 11:35, :]
        return [
            (ap, (0, m), ap[0, m] + (centre - t0[m + 10, 11:35, :])),
            (ap, (1, m), ap[1, m] + (centre - t0[m + 11, 10:34, :])),
            (ap, (2, m), ap[2, m] + (centre - zdn(centre))),
        ]

    loop(0, BLOCK + 2, lift, 3)

    def finish(i):
        m = i + 1

        def around(ref):
            return (
                ref[m, 1:17, :],
                ref[m - 1, 1:17, :],
                ref[m + 1, 1:17, :],
                ref[m, 0:16, :],
                ref[m, 2:18, :],
            )

        speeds = [around(vp.at[c]) for c in range(3)]
        n0, nxm, nxp, nym, nyp = around(visp)
        fxm, fxp = 0.5 * (n0 + nxm), 0.5 * (nxp + n0)
        fym, fyp = 0.5 * (n0 + nym), 0.5 * (nyp + n0)
        fz = 0.5 * (n0 + zdn_copy(n0))
        u0m, u0p = speeds[0][1], speeds[0][2]
        u1m, u1p = speeds[1][3], speeds[1][4]
        u2 = speeds[2][0]

        def transport(q0, qxm, qxp, qym, qyp):
            up = u2 * q0
            return 0.5 * ((u0p * qxp - u0m * qxm) + (u1p * qyp - u1m * qym) + (zup(up) - zdn(up)))

        fields = around(np_)
        out_ndg[i] = fields[0] + DT * transport(*fields)
        gxm = gxp = gym = gyp = gz = 0.0
        for c in range(3):
            fields = around(ap.at[c])
            q0, qxm, qxp, qym, qyp = fields
            s0, sxm, sxp, sym, syp = speeds[c]
            dxm, dxp, dym, dyp = q0 - qxm, qxp - q0, q0 - qym, qyp - q0
            dz = q0 - zdn(q0)
            flux = fz * dz
            spread = (fxp * dxp - fxm * dxm) + (fyp * dyp - fym * dym) + (zup(flux) - flux)
            out_vel[c, i] = q0 + DT * (transport(*fields) + spread)
            gxm = gxm + dxm * (s0 - sxm)
            gxp = gxp + dxp * (sxp - s0)
            gym = gym + dym * (s0 - sym)
            gyp = gyp + dyp * (syp - s0)
            gz = gz + dz * (s0 - zdn(s0))
        bottom = jnp.where(layer(gz) == 0, gz, 0.0)
        out_vis[i] = (-0.5 * DT) * ((gxm + gxp) + (gym + gyp) + (gz + zup(gz)) + bottom)

    loop(0, BLOCK, finish, 2)


def shards(velocity, density, viscosity, grad_out, density_gradient):
    z = density.shape[2]
    size_x, size_y = lax.axis_size("gx"), lax.axis_size("gy")
    at_x, at_y = lax.axis_index("gx"), lax.axis_index("gy")
    odd = lax.rem(at_x, 2).astype(jnp.int32).reshape(1)
    place = jnp.stack([at_y, at_x]).astype(jnp.int32)
    even_pairs = [[i, i + 1] for i in range(0, size_x, 2)]
    odd_pairs = [[i, (i + 1) % size_x] for i in range(1, size_x, 2)]
    forward = [(i, (i + 1) % size_y) for i in range(size_y)]
    backward = [(j, i) for i, j in forward]

    def along_y(up, down):
        return lax.ppermute(up, "gy", forward), lax.ppermute(down, "gy", backward)

    def swapped(block, pairs):
        return lax.ppermute(block, "gx", [q for i, j in pairs for q in ((i, j), (j, i))])

    fine = (40, 40, z)
    mid = (20, 24, z)
    low = (16, 16, z)
    rim = (2 * BLOCK + 1, BLOCK, z)
    own = (BLOCK, BLOCK, z)
    fields = (velocity, viscosity, grad_out, density_gradient)
    up, down, b, d, planes = call(
        own_body,
        [rim, rim, own, own, (2, 4, 2 * BLOCK, z)],
        (velocity, density, viscosity, grad_out, density_gradient),
        [(3, *own), own, own, (3, *own), own],
        fetched=5,
        sems=5,
    )
    before, after = along_y(up, down)
    send = (26, 40, z)
    bb, dd, g0, even_send, odd_send = call(
        rows_body,
        [(BLOCK, 40, z), (BLOCK, 40, z), (40, z), send, send],
        (odd, b, d, down, planes, before, after),
        scalars=1,
    )
    even_got = swapped(even_send, even_pairs)
    odd_got = swapped(odd_send, odd_pairs)
    fine_out = call(
        fine_body,
        [mid, mid, low, low, (18, 16, z), (18, 16, z), (8, 24, 40, z)],
        (odd, bb, dd, g0, even_got, odd_got),
        [(8, *fine), fine, fine, fine, (20, 40, z)] + [mid] * 9 + [(8, 24, z)],
        scalars=1,
        kept=1,
        sems=2,
    )
    f1, b1, f2, b2, up, down, kept0 = fine_out
    before2, after2 = along_y(up, down)
    send2 = (13, 24, z)
    f1, b1, f2, b2, even_send, odd_send = call(
        rows2_body,
        [mid, mid, low, low, send2, send2],
        (odd, f1, b1, f2, b2, before2, after2),
        scalars=1,
    )
    even_got2 = lax.all_gather(even_send, "gx", axis_index_groups=even_pairs)
    odd_got2 = lax.all_gather(odd_send, "gx", axis_index_groups=odd_pairs)
    slots, kept1, kept2 = call(
        level2_body,
        [(size_y, 8, z), (8, *mid), (8, *low)],
        (odd, f1, b1, f2, b2, even_got2, odd_got2),
        [(8, *mid), (8, *low), mid, mid, low, low, low, (2, 16, z)],
        scalars=1,
        kept=2,
        sems=2,
    )
    got = lax.all_to_all(slots, "gy", 0, 0, tiled=True)
    (block,) = call(column_body, [(4, 2 * size_y, z)], (place, got), scalars=1)
    at_odd = lax.rem(at_x, 2)
    chip = lax.all_gather(block, "gx", axis_index_groups=even_pairs)
    side = lax.all_gather(chip, "gx", axis_index_groups=odd_pairs)
    side = lax.dynamic_index_in_dim(side, at_odd, 0, keepdims=False)
    other = lax.all_gather(side, "gx", axis_index_groups=even_pairs)
    far = other.reshape(4, *block.shape)
    far = lax.dynamic_index_in_dim(far, 2 - at_odd, 0, keepdims=False)
    far = lax.all_gather(far, "gx", axis_index_groups=odd_pairs)
    level3 = (14, 32, z)
    slots, kept3 = call(
        level3_body,
        [(size_x, 2, 16, z), (8, *level3)],
        (odd, chip, other, far),
        [(8, *level3), level3, level3, level3, (1, 32, z), (2, 16, z)],
        scalars=1,
        kept=1,
        sems=1,
    )
    got = lax.all_to_all(slots, "gx", 0, 0, tiled=True)
    devices = 2 * WIN + 1
    return tuple(
        call(
            up_body,
            [(3, *own), own, own],
            (place, kept3, kept2, kept1, kept0, *fields, got, before, after, even_got, odd_got),
            [(8, *level3), (8, *low), (8, *mid), (8, *fine), (3, *own), own, (3, *own), own]
            + [(devices, 16, z)] * 12
            + [(11, 32, z), level3, level3, level3]
            + [low, (10, 16, z), low, low]
            + [mid, (12, 24, z), mid, mid]
            + [fine, (16, 40, z), fine, fine]
            + [(3, 18, 24, z), (3, 18, 24, z), (18, 24, z), (18, 24, z)],
            scalars=1,
            megabytes=32,
            fetched=8,
            sems=8,
        )
    )


def solution(mesh):
    placed = (
        P(None, "gx", "gy", None),
        P("gx", "gy", None),
        P("gx", "gy", None),
        P(None, "gx", "gy", None),
        P("gx", "gy", None),
    )
    return jax.shard_map(
        shards,
        mesh=mesh,
        in_specs=placed,
        out_specs=(P(None, "gx", "gy", None), P("gx", "gy", None), P("gx", "gy", None)),
        check_vma=False,
    )
```

```python
import functools

import jax
import jax.numpy as jnp
from jax import lax
from jax.experimental import pallas as pl
from jax.experimental.pallas import tpu as pltpu
from jax.sharding import PartitionSpec as P

INTERPRET = False
DT = 0.2
MID = 1.2
HALF = 0.8
SIGMA = MID / HALF
RHO0 = 1.0 / SIGMA
RHO1 = 1.0 / (2.0 * SIGMA - RHO0)
A1 = RHO1 * RHO0
B1 = 2.0 * RHO1 / HALF
BLOCK = 16
PAD = 12
PAD1 = 6
U0, U1, U2 = 4, 4, 6
WIN = 8
F32 = jnp.float32


def call(body, out_shapes, args, scratch=(), scalars=0, megabytes=16, fetched=0, kept=0, sems=0):
    smem = [pl.BlockSpec(memory_space=pltpu.SMEM)] * scalars
    far = pl.BlockSpec(memory_space=pltpu.HBM)
    near = pl.BlockSpec(memory_space=pltpu.VMEM)
    scratch = [pltpu.VMEM(s, F32) for s in scratch]
    if sems:
        scratch.append(pltpu.SemaphoreType.DMA((sems,)))
    return pl.pallas_call(
        body,
        out_shape=[jax.ShapeDtypeStruct(s, F32) for s in out_shapes],
        in_specs=smem + [far] * fetched + [near] * (len(args) - scalars - fetched),
        out_specs=[near] * (len(out_shapes) - kept) + [far] * kept,
        scratch_shapes=scratch,
        compiler_params=pltpu.CompilerParams(vmem_limit_bytes=megabytes * 2**20),
        interpret=INTERPRET,
    )(*args)


def loop(low, high, step, unroll=1):
    def group(base, count):
        stores = []
        for u in range(count):
            stores.extend(step(base + u) or ())
        for ref, index, value in stores:
            ref[index] = value

    groups = (high - low) // unroll
    if groups == 1:
        group(low, unroll)
    elif groups > 1:
        lax.fori_loop(0, groups, lambda n, c: (group(low + n * unroll, unroll), c)[1], 0)
    rest = (high - low) - groups * unroll
    if rest:
        group(high - rest, rest)


def ydn(v):
    return pltpu.roll(v, 1, axis=0)


def yup(v):
    return pltpu.roll(v, v.shape[0] - 1, axis=0)


def layer(v):
    return lax.broadcasted_iota(jnp.int32, v.shape, 1)


def zroll_dn(v):
    return pltpu.roll(v, 1, axis=1)


def zroll_up(v):
    return pltpu.roll(v, v.shape[1] - 1, axis=1)


def zdn(v):
    return jnp.where(layer(v) == 0, 0.0, zroll_dn(v))


def zdn_copy(v):
    return jnp.where(layer(v) == 0, v, zroll_dn(v))


def zup(v):
    return jnp.where(layer(v) == v.shape[1] - 1, 0.0, zroll_up(v))


def setup(b, n, diag, low, high, scale, unroll, f=None, g=None, g_range=None):
    half = 0.5 * scale

    def step(i):
        b0 = b[i]
        fxm = half * (b0 + b[i - 1])
        fxp = half * (b[i + 1] + b0)
        fym = half * (b0 + ydn(b0))
        fyp = yup(fym)
        fz = 0.5 * (b0 + zdn_copy(b0))
        fzp = zup(fz)
        d = (fxm + fxp) + (fym + fyp) + (fz + fzp)
        inv = 1.0 / d
        fzm = jnp.where(layer(fz) == 0, 0.0, fz)
        out = [(ref, i, v * inv) for ref, v in zip(n, (fxm, fxp, fym, fyp, fzm, fzp), strict=True)]
        if diag is not None:
            out.append((diag, i, d))
        if f is not None:
            out.append((g, i, f[i] * inv))
        return out

    loop(low, high, step, unroll)


def around_sum(q, n, i, q0):
    total = (n[0][i] * q[i - 1] + n[1][i] * q[i + 1]) + (n[2][i] * ydn(q0) + n[3][i] * yup(q0))
    return total + (n[4][i] * zroll_dn(q0) + n[5][i] * zroll_up(q0))


def pre(g, x, n, low, high, unroll):
    first = (1.0 + A1) / MID + B1 * (1.0 - 1.0 / MID)

    def step(i):
        g0 = g[i]
        return [(x, i, first * g0 + (B1 / MID) * around_sum(g, n, i, g0))]

    loop(low, high, step, unroll)


def post(x, g, y, out, n, low, high, unroll):
    def first(i):
        x0 = x[i]
        return [(y, i, x0 + (1.0 / MID) * ((g[i] - x0) + around_sum(x, n, i, x0)))]

    loop(low - 1, high + 1, first, unroll)

    def second(i):
        y0 = y[i]
        z = (g[i] - y0) + around_sum(y, n, i, y0)
        return [(out, i, y0 + (A1 * (y0 - x[i]) + B1 * z))]

    loop(low, high, second, unroll)


def residual_pairs(g, x, diag, n, pairs, start, low, high, unroll):
    def one(i):
        x0 = x[i]
        return diag[i] * ((g[i] - x0) + around_sum(x, n, i, x0))

    def step(m):
        i = start + 2 * m
        return [(pairs, m, one(i) + one(i + 1))]

    loop(low, high, step, unroll)


def plane_pairs(b, pairs, start, low, high, unroll=4):
    def step(m):
        return [(pairs, m, b[start + 2 * m] + b[start + 2 * m + 1])]

    loop(low, high, step, unroll)


def row_pairs(pairs, coarse, low, high, row, count, target, shift=0, unroll=8):
    def step(m):
        even = pairs[m, pl.ds(row, count, 2), :]
        odd = pairs[m, pl.ds(row + 1, count, 2), :]
        return [(coarse, (m + shift, slice(target, target + count)), 0.25 * (even + odd))]

    loop(low, high, step, unroll)


def correct(x, coarse, wide, low, high, plane, row, count, target, unroll=4, out=None):
    def widen(m):
        v = coarse[m, row : row + count, :]
        return [
            (wide, (m, pl.ds(target, count, 2)), v),
            (wide, (m, pl.ds(target + 1, count, 2)), v),
        ]

    loop(low, high, widen, 2 * unroll)
    out = x if out is None else out

    def add(m):
        i = 2 * m + plane
        w = wide[m]
        return [(out, i, x[i] + w), (out, i + 1, x[i + 1] + w)]

    loop(low, high, add, unroll)


def own_body(joined, up, down, b, d, planes):
    vel, g = joined.at[0:3], joined.at[3:6]
    den, vis, ndg = joined.at[6], joined.at[7], joined.at[8]

    def invert(i):
        return [(b, i, 1.0 / den[i])]

    loop(0, BLOCK, invert, 8)
    edge = BLOCK - 1

    def step(i):
        b0 = b[i]
        fz = 0.5 * (b0 + zdn_copy(b0)) * g[2, i]
        fy = 0.5 * (b0 + ydn(b0)) * g[1, i]
        rows = lax.broadcasted_iota(jnp.int32, fy.shape, 0)
        fy = jnp.where(rows == 0, 0.0, fy)
        total = (zup(fz) - fz) + (yup(fy) - fy)
        left = jnp.maximum(i - 1, 0)
        right = jnp.minimum(i + 1, edge)
        inner = jnp.where(i > 0, 0.5, 0.0) * (b0 + b[left]) * g[0, i]
        outer = jnp.where(i < edge, 0.5, 0.0) * (b0 + b[right]) * g[0, right]
        total = total + (outer - inner)
        k = BLOCK + i
        head = slice(0, PAD)
        out = [
            (d, i, total),
            (up, (i, head), b0[BLOCK - PAD :]),
            (up, (k, head), total[BLOCK - PAD :]),
            (down, (i, head), b0[:PAD]),
            (down, (k, head), total[:PAD]),
        ]
        for c in range(3):
            out.append((up, (k, PAD + 1 + c), g[c, i, edge, :]))
            out.append((down, (k, PAD + 1 + c), g[c, i, 0, :]))
        return out

    loop(0, BLOCK, step, 4)

    def edges(i):
        k = BLOCK + i
        out = []
        for c in range(3):
            out.append((up, (i, PAD + c), vel[c, i, edge, :]))
            out.append((down, (i, PAD + c), vel[c, i, 0, :]))
        out.append((up, (i, PAD + 3), vis[i, edge, :]))
        out.append((down, (i, PAD + 3), vis[i, 0, :]))
        out.append((up, (k, PAD), ndg[i, edge, :]))
        out.append((down, (k, PAD), ndg[i, 0, :]))
        return out

    loop(0, BLOCK, edges, 4)
    z = b.shape[2]
    up[2 * BLOCK] = jnp.zeros((BLOCK, z), F32)
    down[2 * BLOCK] = jnp.zeros((BLOCK, z), F32)
    up[2 * BLOCK, 0:PAD, :] = g[0, 0, BLOCK - PAD :, :]
    down[2 * BLOCK, 0:PAD, :] = g[0, 0, :PAD, :]
    for n, plane in enumerate((0, edge)):
        for c in range(3):
            planes[n, c, 0:BLOCK, :] = vel[c, plane]
            planes[n, c, BLOCK : 2 * BLOCK, :] = g[c, plane]
        planes[n, 3, 0:BLOCK, :] = vis[plane]
        planes[n, 3, BLOCK : 2 * BLOCK, :] = ndg[plane]


def rows_body(odd, b, d, down, planes, before, after, bb, dd, g0, even_send, odd_send):
    top = PAD + BLOCK

    def step(i):
        k = BLOCK + i
        own_flux = 0.5 * (b[i, 0:1, :] + before[i, PAD - 1 : PAD, :]) * down[k, PAD + 2 : PAD + 3, :]
        next_flux = (
            0.5
            * (b[i, BLOCK - 1 : BLOCK, :] + after[i, 0:1, :])
            * after[k, PAD + 2 : PAD + 3, :]
        )
        out = []
        for ref, own, m in ((bb, b, i), (dd, d, k)):
            out.append((ref, (i, slice(0, PAD)), before[m, 0:PAD, :]))
            out.append((ref, (i, slice(PAD, top)), own[i]))
            out.append((ref, (i, slice(top, top + PAD)), after[m, 0:PAD, :]))
        out.append((dd, (i, slice(PAD - 1, PAD)), before[k, PAD - 1 : PAD, :] + own_flux))
        out.append((dd, (i, slice(PAD, PAD + 1)), d[i, 0:1, :] - own_flux))
        out.append((dd, (i, slice(top - 1, top)), d[i, BLOCK - 1 : BLOCK, :] + next_flux))
        out.append((dd, (i, slice(top, top + 1)), after[k, 0:1, :] - next_flux))
        return out

    loop(0, BLOCK, step, 4)
    g0[0:PAD, :] = before[2 * BLOCK, 0:PAD, :]
    g0[PAD:top, :] = planes[0, 0, BLOCK : 2 * BLOCK, :]
    g0[top : top + PAD, :] = after[2 * BLOCK, 0:PAD, :]
    is_odd = odd[0]
    for send, last in ((even_send, 1 - is_odd), (odd_send, is_odd)):
        b_start = 5 * last
        d_start = 6 * last

        def b_step(m, send=send, b_start=b_start):
            return [(send, m, bb[b_start + m])]

        def d_step(m, send=send, d_start=d_start):
            return [(send, 11 + m, dd[d_start + m])]

        loop(0, 11, b_step, 11)
        loop(0, 10, d_step, 10)
        send[21] = g0[...]
        for c in range(4):
            send[22 + c, 0 : 2 * BLOCK, :] = planes[last, c]


def fine_body(
    odd, bb, dd, g0, even_got, odd_got,
    f1, b1, f2, b2, up, down, slots, kept,
    pack, b, f0, diag, pairs, g1, xb, *rest,
):
    n1, (diag1, pairs1) = rest[:6], rest[6:8]
    n2, (own2, g2, x2, diag2, pairs2, sems) = rest[8:14], rest[14:]
    gf, x0 = pack.at[0], pack.at[7]
    n0 = tuple(pack.at[n] for n in range(1, 7))
    keep = slice(8, 32)
    saves = (
        pltpu.make_async_copy(pack.at[0:7, keep, keep], kept.at[0:7], sems.at[0]),
        pltpu.make_async_copy(pack.at[7, keep, keep], kept.at[7], sems.at[1]),
    )
    is_odd = odd[0] == 1
    top = PAD + BLOCK

    def left(m):
        return jnp.where(is_odd, even_got[m], odd_got[m])

    def right(m):
        return jnp.where(is_odd, odd_got[m], even_got[m])

    loop(0, BLOCK, lambda i: [(b, PAD + i, bb[i]), (f0, PAD + i, dd[i])], 4)
    loop(0, 11, lambda m: [(b, 1 + m, left(m)), (b, top + m, right(m))], 4)
    loop(0, 10, lambda m: [(f0, 2 + m, left(11 + m)), (f0, top + m, right(11 + m))], 5)
    flux = 0.5 * (b[PAD] + b[PAD - 1]) * g0[...]
    f0[PAD - 1] = f0[PAD - 1] + flux
    f0[PAD] = f0[PAD] - flux
    flux = 0.5 * (b[top] + b[top - 1]) * right(21)
    f0[top - 1] = f0[top - 1] + flux
    f0[top] = f0[top] - flux

    setup(b, n0, diag, 2, 38, 1.0, U0, f0, gf)
    saves[0].start()
    pre(gf, x0, n0, 3, 37, U0)
    saves[1].start()
    residual_pairs(gf, x0, diag, n0, pairs, 0, 2, 18, U0 // 2)
    row_pairs(pairs, f1, 2, 18, 0, 20, 0)
    plane_pairs(b, pairs, 0, 1, 19)
    row_pairs(pairs, b1, 1, 19, 0, 20, 0)

    z = b.shape[2]
    f1[:, 20:24, :] = jnp.zeros((20, 4, z), F32)
    b1[:, 20:24, :] = jnp.ones((20, 4, z), F32)
    setup(b1, n1, diag1, 2, 18, 0.25, U1, f1, g1)
    pre(g1, xb, n1, 3, 17, U1)
    residual_pairs(g1, xb, diag1, n1, pairs1, 4, 0, 6, U1 // 2)
    b2[...] = jnp.ones((16, 16, z), F32)
    row_pairs(pairs1, f2, 0, 6, 4, 6, 5, shift=5)
    plane_pairs(b1, pairs1, 2, 0, 8)
    row_pairs(pairs1, b2, 0, 8, 2, 8, 4, shift=4)

    for send, frow, brow, f1row, b1row in ((up, 5, 4, 9, 8), (down, 6, 6, 10, 11)):
        for m in range(6):
            send[m, 0:5, :] = f2[5 + m, frow : frow + 5, :]
        for m in range(8):
            send[m, 5:11, :] = b2[4 + m, brow : brow + 6, :]
        for m in range(16):
            send[m, 11:12, :] = f1[2 + m, f1row : f1row + 1, :]
        for m in range(18):
            send[m, 12:13, :] = b1[1 + m, b1row : b1row + 1, :]
    own2[...] = jnp.zeros((16, 16, z), F32)
    x2[...] = jnp.zeros((16, 16, z), F32)
    for m in range(6, 10):
        own2[m, 6:10, :] = f2[m, 6:10, :]
    setup(b2, n2, diag2, 4, 12, 0.25**2, 4, own2, g2)
    pre(g2, x2, n2, 5, 11, U2)
    residual_pairs(g2, x2, diag2, n2, pairs2, 4, 0, 4, 4)
    parts = []
    for m in range(4):
        even = pairs2[m, pl.ds(4, 4, 2), :]
        parts.append(0.25 * (even + pairs2[m, pl.ds(5, 4, 2), :]))
    plane_pairs(b2, pairs2, 6, 0, 2)
    for m in range(2):
        even = pairs2[m, pl.ds(6, 2, 2), :]
        parts.append(0.25 * (even + pairs2[m, pl.ds(7, 2, 2), :]))
    for n in range(4):
        slots[0, 4 * n : 4 * n + 4, :] = parts[n]
    slots[0, 16:18, :] = parts[4]
    slots[0, 18:20, :] = parts[5]
    slots[0, 20:24, :] = jnp.zeros((4, z), F32)
    value = slots[0]
    for m in range(1, 16):
        slots[m] = value
    for save in saves:
        save.wait()


def rows2_body(odd, f1, b1, f2, b2, before, after, got, g1, h1, g2, h2, even_send, odd_strip):
    g1[...] = f1[...]
    h1[...] = b1[...]
    z = f1.shape[2]
    g2[...] = jnp.zeros((16, 16, z), F32)
    h2[...] = jnp.ones((16, 16, z), F32)
    for m in range(6):
        g2[5 + m, 6:10, :] = f2[5 + m, 6:10, :]
        g2[5 + m, 1:6, :] = before[m, 0:5, :]
        g2[5 + m, 10:15, :] = after[m, 0:5, :]
    for m in range(8):
        h2[4 + m, 6:10, :] = b2[4 + m, 6:10, :]
        h2[4 + m, 0:6, :] = before[m, 5:11, :]
        h2[4 + m, 10:16, :] = after[m, 5:11, :]
    for m in range(16):
        g1[2 + m, 1:2, :] = before[m, 11:12, :]
        g1[2 + m, 18:19, :] = after[m, 11:12, :]
    for m in range(18):
        h1[1 + m, 0:1, :] = before[m, 12:13, :]
        h1[1 + m, 19:20, :] = after[m, 12:13, :]
    at_y = lax.axis_index("gy")
    for p in range(16):
        here = lax.rem(at_y + (p + 8), 16)
        above = lax.rem(at_y + (p + 9), 16)
        below = lax.rem(at_y + (p + 7), 16)
        for n in range(4):
            k = 4 * n
            low = got[here, k + 1 : k + 2, :] + got[below, k + 3 : k + 4, :]
            high = got[here, k + 2 : k + 3, :] + got[above, k : k + 1, :]
            even_send[n, 2 * p : 2 * p + 1, :] = low
            even_send[n, 2 * p + 1 : 2 * p + 2, :] = high
        for n in range(2):
            even_send[4 + n, 2 * p : 2 * p + 2, :] = got[here, 16 + 2 * n : 18 + 2 * n, :]
    is_odd = odd[0]
    for send, first, last in ((even_send, 6, 1 - is_odd), (odd_strip, 0, is_odd)):
        for u in range(11):
            v = g2[6 - last + u] if u < 5 else h2[6 - 2 * last + (u - 5)]
            send[first + u // 2, (u % 2) * 16 : (u % 2) * 16 + 16, :] = v
        send[first + 5, 16:32, :] = jnp.zeros((16, z), F32)
        for n, v in ((6, g1[10 - last]), (7, h1[11 - 3 * last])):
            send[first + n, 0:24, :] = v
            send[first + n, 24:32, :] = jnp.zeros((8, z), F32)


def level3_body(
    odd, f1i, b1i, f2i, b2i, pair, other, far, slots, f1, b1, f2, b2, kept,
    pack, f3, b3, diag, pairs, small, sems,
):
    g3, x3, n3 = pack.at[0], pack.at[7], tuple(pack.at[n] for n in range(1, 7))
    save = pltpu.make_async_copy(pack, kept, sems.at[0])
    is_odd = odd[0] == 1
    blocks = [(other, (0, 0)), (other, (0, 1)), (pair, (0,)), (pair, (1,))]
    blocks += [(other, (1, 0)), (other, (1, 1))]

    def part(p, k):
        ref_even, at_even = (far, (0,)) if p == 0 else blocks[p - 1]
        ref_odd, at_odd = (far, (1,)) if p == 6 else blocks[p]
        return jnp.where(is_odd, ref_odd[(*at_odd, k)], ref_even[(*at_even, k)])

    for p in range(7):
        low, high = part(p, 1), part(p, 2)
        f3[2 * p] = low + part(p - 1, 3) if p > 0 else low
        f3[2 * p + 1] = high + part(p + 1, 0) if p < 6 else high
        b3[2 * p] = part(p, 4)
        b3[2 * p + 1] = part(p, 5)
    setup(b3, n3, diag, 1, 13, 0.25**3, U0, f3, g3)
    pre(g3, x3, n3, 2, 12, 5)
    save.start()
    residual_pairs(g3, x3, diag, n3, pairs, 6, 0, 1, 1)
    row_pairs(pairs, small, 0, 1, 0, 16, 0)
    plane_pairs(b3, pairs, 6, 0, 1)
    row_pairs(pairs, small, 0, 1, 0, 16, 0, shift=1)

    def spread(m):
        return [(slots, (m, n), small[n]) for n in range(2)]

    loop(0, 32, spread, 4)

    def left(n, rows):
        return jnp.where(is_odd, pair[0, 6 + n, rows, :], far[0, 6 + n, rows, :])

    def right(n, rows):
        return jnp.where(is_odd, far[1, 6 + n, rows, :], pair[1, 6 + n, rows, :])

    f1[...] = f1i[...]
    b1[...] = b1i[...]
    f2[...] = f2i[...]
    b2[...] = b2i[...]
    for u in range(11):
        rows = slice((u % 2) * 16, (u % 2) * 16 + 16)
        if u < 5:
            f2[1 + u] = left(u // 2, rows)
            f2[10 + u] = right(u // 2, rows)
        else:
            b2[u - 5] = left(u // 2, rows)
            b2[u + 5] = right(u // 2, rows)
    rows = slice(0, 24)
    f1[1] = left(6, rows)
    f1[18] = right(6, rows)
    b1[0] = left(7, rows)
    b1[19] = right(7, rows)
    save.wait()


def up_body(*refs):
    refs = list(refs)
    at_x = lax.axis_index("gx")

    def take(count):
        head = tuple(refs[:count])
        del refs[:count]
        return head

    kept = take(6)
    f1, b1, f2, b2, got, before, after, even_got, odd_got = take(9)
    out_vel, out_ndg, out_vis = take(3)
    held = take(6)
    pack3, pack0, vel, vis, g, ndg = held
    pack1, pack2 = take(2)
    f4, b4, g4, xa4, xb4, e4 = take(6)
    n4 = take(6)
    w3, v3, y3, t3, v2, w2, y2, t2, v1, w1, y1, t1, v0, w0, y0, t0 = take(16)
    vp, ap, visp, np_ = take(4)
    (sems,) = refs
    (g3, x3, n3), (g2, x2, n2), (g1, x1, n1), (g0, x0, n0) = (
        (pack.at[0], pack.at[7], tuple(pack.at[n] for n in range(1, 7)))
        for pack in (pack3, pack2, pack1, pack0)
    )
    loads = [
        pltpu.make_async_copy(source, target, sems.at[n])
        for n, (source, target) in enumerate(zip(kept, held, strict=True))
    ]
    for load in loads:
        load.start()
    devices = 2 * WIN + 1

    def gather(q):
        source = lax.rem(at_x + (q + 32 - WIN), 32)
        return [(f4, q, got[source, 0]), (b4, q, got[source, 1])]

    loop(0, devices, gather, devices)
    low, high = 1, devices - 1
    setup(b4, n4, None, low, high, 0.25**4, U2, f4, g4)

    def start(i):
        u = g4[i] * (1.0 / MID)
        return [(e4, i, u), (xa4, i, u)]

    loop(low, high, start, U2)
    ratio = RHO0
    x_now, x_next = xa4, xb4
    for _ in range(5):
        following = 1.0 / (2.0 * SIGMA - ratio)
        low, high = low + 1, high - 1

        def sweep(i, x_now=x_now, x_next=x_next, following=following, ratio=ratio):
            q0 = x_now[i]
            scaled = (g4[i] - q0) + around_sum(x_now, n4, i, q0)
            u = following * ratio * e4[i] + (2.0 * following / HALF) * scaled
            return [(e4, i, u), (x_next, i, q0 + u)]

        loop(low, high, sweep, U2)
        ratio = following
        x_now, x_next = x_next, x_now
    loads[0].wait()
    correct(x3, x_now, w3, 6, 11, -10, 0, 16, 0, out=v3)
    post(v3, g3, y3, t3, n3, 4, 10, U0)
    setup(b2, n2, None, 1, 15, 0.25**2, U2, f2, g2)
    pre(g2, x2, n2, 2, 14, U2)
    correct(x2, t3, w2, 4, 10, -6, 14, 6, 2, out=v2)
    post(v2, g2, y2, t2, n2, 4, 12, U2)
    setup(b1, n1, None, 1, 19, 0.25, U1, f1, g1)
    pre(g1, x1, n1, 2, 18, U1)
    correct(x1, t2, w1, 4, 12, -6, 4, 8, 2, out=v1)
    post(v1, g1, y1, t1, n1, 4, 16, U1)
    loads[1].wait()
    correct(x0, t1, w0, 4, 16, -8, 4, 12, 0, 2, out=v0)
    post(v0, g0, y0, t0, n0, 2, 21, U0)
    for load in loads[2:]:
        load.wait()

    def pad(i):
        k = BLOCK + i

        def put(out, own, source, row):
            out[0:1, :] = before[source, row : row + 1, :]
            out[1:17, :] = own
            out[17:18, :] = after[source, row : row + 1, :]

        for c in range(3):
            put(vp.at[c, i + 1], vel[c, i], i, PAD + c)
            put(ap.at[c, i + 1], g[c, i], k, PAD + 1 + c)
        put(visp.at[i + 1], vis[i], i, PAD + 3)
        put(np_.at[i + 1], ndg[i], k, PAD)

    loop(0, BLOCK, pad, 2)
    is_odd = lax.rem(at_x, 2) == 1

    def left(m):
        return jnp.where(is_odd, even_got[m], odd_got[m])

    def right(m):
        return jnp.where(is_odd, odd_got[m], even_got[m])

    for plane, side in ((0, left), (BLOCK + 1, right)):
        for c in range(3):
            both = side(22 + c)
            vp[c, plane, 1:17, :] = both[0:BLOCK]
            ap[c, plane, 1:17, :] = both[BLOCK : 2 * BLOCK]
        both = side(25)
        visp[plane, 1:17, :] = both[0:BLOCK]
        np_[plane, 1:17, :] = both[BLOCK : 2 * BLOCK]

    def lift(m):
        rows = slice(0, BLOCK + 2)
        centre = t0[m + 3, 3:21, :]
        return [
            (ap, (0, m, rows), ap[0, m, rows, :] + (centre - t0[m + 2, 3:21, :])),
            (ap, (1, m, rows), ap[1, m, rows, :] + (centre - t0[m + 3, 2:20, :])),
            (ap, (2, m, rows), ap[2, m, rows, :] + (centre - zdn(centre))),
        ]

    loop(0, BLOCK + 2, lift, 3)

    def finish(i):
        m = i + 1

        def around(ref):
            return (
                ref[m, 1:17, :],
                ref[m - 1, 1:17, :],
                ref[m + 1, 1:17, :],
                ref[m, 0:16, :],
                ref[m, 2:18, :],
            )

        speeds = [around(vp.at[c]) for c in range(3)]
        n0, nxm, nxp, nym, nyp = around(visp)
        fxm, fxp = 0.5 * (n0 + nxm), 0.5 * (nxp + n0)
        fym, fyp = 0.5 * (n0 + nym), 0.5 * (nyp + n0)
        fz = 0.5 * (n0 + zdn_copy(n0))
        u0m, u0p = speeds[0][1], speeds[0][2]
        u1m, u1p = speeds[1][3], speeds[1][4]
        u2 = speeds[2][0]

        def transport(q0, qxm, qxp, qym, qyp):
            up = u2 * q0
            return 0.5 * ((u0p * qxp - u0m * qxm) + (u1p * qyp - u1m * qym) + (zup(up) - zdn(up)))

        fields = around(np_)
        out_ndg[i] = fields[0] + DT * transport(*fields)
        gxm = gxp = gym = gyp = gz = 0.0
        for c in range(3):
            fields = around(ap.at[c])
            q0, qxm, qxp, qym, qyp = fields
            s0, sxm, sxp, sym, syp = speeds[c]
            dxm, dxp, dym, dyp = q0 - qxm, qxp - q0, q0 - qym, qyp - q0
            dz = q0 - zdn(q0)
            flux = fz * dz
            spread = (fxp * dxp - fxm * dxm) + (fyp * dyp - fym * dym) + (zup(flux) - flux)
            out_vel[c, i] = q0 + DT * (transport(*fields) + spread)
            gxm = gxm + dxm * (s0 - sxm)
            gxp = gxp + dxp * (sxp - s0)
            gym = gym + dym * (s0 - sym)
            gyp = gyp + dyp * (syp - s0)
            gz = gz + dz * (s0 - zdn(s0))
        bottom = jnp.where(layer(gz) == 0, gz, 0.0)
        out_vis[i] = (-0.5 * DT) * ((gxm + gxp) + (gym + gyp) + (gz + zup(gz)) + bottom)

    loop(0, BLOCK, finish, 2)


def shards(velocity, density, viscosity, grad_out, density_gradient):
    z = density.shape[2]
    size_x, size_y = lax.axis_size("gx"), lax.axis_size("gy")
    at_x = lax.axis_index("gx")
    odd = lax.rem(at_x, 2).astype(jnp.int32).reshape(1)
    even_pairs = [[i, i + 1] for i in range(0, size_x, 2)]
    odd_pairs = [[i, (i + 1) % size_x] for i in range(1, size_x, 2)]
    forward = [(i, (i + 1) % size_y) for i in range(size_y)]
    backward = [(j, i) for i, j in forward]

    def along_y(up, down):
        return lax.ppermute(up, "gy", forward), lax.ppermute(down, "gy", backward)

    def swapped(block, pairs):
        return lax.ppermute(block, "gx", [q for i, j in pairs for q in ((i, j), (j, i))])

    fine = (40, 40, z)
    mid = (20, 24, z)
    low = (16, 16, z)
    rim = (2 * BLOCK + 1, BLOCK, z)
    own = (BLOCK, BLOCK, z)
    fields = (velocity, viscosity, grad_out, density_gradient)
    single = [v[None] for v in (density, viscosity, density_gradient)]
    joined = jnp.concatenate([velocity, grad_out, *single], 0)
    up, down, b, d, planes = call(
        own_body,
        [rim, rim, own, own, (2, 4, 2 * BLOCK, z)],
        (joined,),
    )
    before, after = along_y(up, down)
    send = (26, 40, z)
    bb, dd, g0, even_send, odd_send = call(
        rows_body,
        [(BLOCK, 40, z), (BLOCK, 40, z), (40, z), send, send],
        (odd, b, d, down, planes, before, after),
        scalars=1,
    )
    even_got = swapped(even_send, even_pairs)
    odd_got = swapped(odd_send, odd_pairs)
    f1, b1, f2, b2, up, down, slots, kept0 = call(
        fine_body,
        [mid, mid, low, low, (18, 16, z), (18, 16, z), (size_y, 24, z), (8, 24, 24, z)],
        (odd, bb, dd, g0, even_got, odd_got),
        [(8, *fine), fine, fine, fine, (20, 40, z)]
        + [mid] * 9
        + [(8, 24, z)]
        + [low] * 10
        + [(4, 16, z)],
        scalars=1,
        kept=1,
        sems=2,
    )
    got = lax.all_to_all(slots, "gy", 0, 0, tiled=True)
    before2, after2 = along_y(up, down)
    f1, b1, f2, b2, even_send, odd_strip = call(
        rows2_body,
        [mid, mid, low, low, (14, 32, z), (8, 32, z)],
        (odd, f1, b1, f2, b2, before2, after2, got),
        scalars=1,
    )
    at_odd = lax.rem(at_x, 2)
    pair = lax.all_gather(even_send, "gx", axis_index_groups=even_pairs)
    side = lax.all_gather(pair[:, 0:6], "gx", axis_index_groups=odd_pairs)
    side = lax.dynamic_index_in_dim(side, at_odd, 0, keepdims=False)
    other = lax.all_gather(side, "gx", axis_index_groups=even_pairs)
    far = lax.dynamic_index_in_dim(other.reshape(4, 6, 32, z), 2 - at_odd, 0, keepdims=False)
    far = jnp.concatenate([far, odd_strip], 0)
    far = lax.all_gather(far, "gx", axis_index_groups=odd_pairs)
    level3 = (14, 32, z)
    slots, f1, b1, f2, b2, kept3 = call(
        level3_body,
        [(size_x, 2, 16, z), mid, mid, low, low, (8, *level3)],
        (odd, f1, b1, f2, b2, pair, other, far),
        [(8, *level3), level3, level3, level3, (1, 32, z), (2, 16, z)],
        scalars=1,
        kept=1,
        sems=1,
    )
    got = lax.all_to_all(slots, "gx", 0, 0, tiled=True)
    devices = 2 * WIN + 1
    return tuple(
        call(
            up_body,
            [(3, *own), own, own],
            (kept3, kept0, *fields, f1, b1, f2, b2, got, before, after, even_got, odd_got),
            [(8, *level3), (8, 24, 24, z), (3, *own), own, (3, *own), own, (8, *mid), (8, *low)]
            + [(devices, 16, z)] * 12
            + [(11, 32, z), level3, level3, level3]
            + [low, (10, 16, z), low, low]
            + [mid, (12, 24, z), mid, mid]
            + [(24, 24, z), (16, 24, z), (24, 24, z), (24, 24, z)]
            + [(3, 18, 24, z), (3, 18, 24, z), (18, 24, z), (18, 24, z)],
            megabytes=24,
            fetched=6,
            sems=6,
        )
    )


def solution(mesh):
    placed = (
        P(None, "gx", "gy", None),
        P("gx", "gy", None),
        P("gx", "gy", None),
        P(None, "gx", "gy", None),
        P("gx", "gy", None),
    )
    return jax.shard_map(
        shards,
        mesh=mesh,
        in_specs=placed,
        out_specs=(P(None, "gx", "gy", None), P("gx", "gy", None), P("gx", "gy", None)),
        check_vma=False,
    )
```

```python
import functools

import jax
import jax.numpy as jnp
from jax import lax
from jax.experimental import pallas as pl
from jax.experimental.pallas import tpu as pltpu
from jax.sharding import PartitionSpec as P

INTERPRET = False
DT = 0.2
MID = 1.2
HALF = 0.8
SIGMA = MID / HALF
RHO0 = 1.0 / SIGMA
RHO1 = 1.0 / (2.0 * SIGMA - RHO0)
A1 = RHO1 * RHO0
B1 = 2.0 * RHO1 / HALF
BLOCK = 16
PAD = 12
PAD1 = 6
U0, U1, U2 = 4, 4, 6
WIN = 8
F32 = jnp.float32


def call(body, out_shapes, args, scratch=(), scalars=0, megabytes=16, fetched=0, kept=0, sems=0):
    smem = [pl.BlockSpec(memory_space=pltpu.SMEM)] * scalars
    far = pl.BlockSpec(memory_space=pltpu.HBM)
    near = pl.BlockSpec(memory_space=pltpu.VMEM)
    scratch = [pltpu.VMEM(s, F32) for s in scratch]
    if sems:
        scratch.append(pltpu.SemaphoreType.DMA((sems,)))
    return pl.pallas_call(
        body,
        out_shape=[jax.ShapeDtypeStruct(s, F32) for s in out_shapes],
        in_specs=smem + [far] * fetched + [near] * (len(args) - scalars - fetched),
        out_specs=[near] * (len(out_shapes) - kept) + [far] * kept,
        scratch_shapes=scratch,
        compiler_params=pltpu.CompilerParams(vmem_limit_bytes=megabytes * 2**20),
        interpret=INTERPRET,
    )(*args)


def loop(low, high, step, unroll=1):
    def group(base, count):
        stores = []
        for u in range(count):
            stores.extend(step(base + u) or ())
        for ref, index, value in stores:
            ref[index] = value

    groups = (high - low) // unroll
    if groups == 1:
        group(low, unroll)
    elif groups > 1:
        lax.fori_loop(0, groups, lambda n, c: (group(low + n * unroll, unroll), c)[1], 0)
    rest = (high - low) - groups * unroll
    if rest:
        group(high - rest, rest)


def ydn(v):
    return pltpu.roll(v, 1, axis=0)


def yup(v):
    return pltpu.roll(v, v.shape[0] - 1, axis=0)


def layer(v):
    return lax.broadcasted_iota(jnp.int32, v.shape, 1)


def zroll_dn(v):
    return pltpu.roll(v, 1, axis=1)


def zroll_up(v):
    return pltpu.roll(v, v.shape[1] - 1, axis=1)


def zdn(v):
    return jnp.where(layer(v) == 0, 0.0, zroll_dn(v))


def zdn_copy(v):
    return jnp.where(layer(v) == 0, v, zroll_dn(v))


def zup(v):
    return jnp.where(layer(v) == v.shape[1] - 1, 0.0, zroll_up(v))


def setup(b, n, diag, low, high, scale, unroll, f=None, g=None, g_range=None):
    half = 0.5 * scale

    def step(i):
        b0 = b[i]
        fxm = half * (b0 + b[i - 1])
        fxp = half * (b[i + 1] + b0)
        fym = half * (b0 + ydn(b0))
        fyp = yup(fym)
        fz = 0.5 * (b0 + zdn_copy(b0))
        fzp = zup(fz)
        d = (fxm + fxp) + (fym + fyp) + (fz + fzp)
        inv = 1.0 / d
        fzm = jnp.where(layer(fz) == 0, 0.0, fz)
        out = [(ref, i, v * inv) for ref, v in zip(n, (fxm, fxp, fym, fyp, fzm, fzp), strict=True)]
        if diag is not None:
            out.append((diag, i, d))
        if f is not None:
            out.append((g, i, f[i] * inv))
        return out

    loop(low, high, step, unroll)


def around_sum(q, n, i, q0):
    total = (n[0][i] * q[i - 1] + n[1][i] * q[i + 1]) + (n[2][i] * ydn(q0) + n[3][i] * yup(q0))
    return total + (n[4][i] * zroll_dn(q0) + n[5][i] * zroll_up(q0))


def pre(g, x, n, low, high, unroll):
    first = (1.0 + A1) / MID + B1 * (1.0 - 1.0 / MID)

    def step(i):
        g0 = g[i]
        return [(x, i, first * g0 + (B1 / MID) * around_sum(g, n, i, g0))]

    loop(low, high, step, unroll)


def post(x, g, y, out, n, low, high, unroll):
    def first(i):
        x0 = x[i]
        return [(y, i, x0 + (1.0 / MID) * ((g[i] - x0) + around_sum(x, n, i, x0)))]

    loop(low - 1, high + 1, first, unroll)

    def second(i):
        y0 = y[i]
        z = (g[i] - y0) + around_sum(y, n, i, y0)
        return [(out, i, y0 + (A1 * (y0 - x[i]) + B1 * z))]

    loop(low, high, second, unroll)


def residual_pairs(g, x, diag, n, pairs, start, low, high, unroll):
    def one(i):
        x0 = x[i]
        return diag[i] * ((g[i] - x0) + around_sum(x, n, i, x0))

    def step(m):
        i = start + 2 * m
        return [(pairs, m, one(i) + one(i + 1))]

    loop(low, high, step, unroll)


def plane_pairs(b, pairs, start, low, high, unroll=4):
    def step(m):
        return [(pairs, m, b[start + 2 * m] + b[start + 2 * m + 1])]

    loop(low, high, step, unroll)


def row_pairs(pairs, coarse, low, high, row, count, target, shift=0, unroll=8):
    def step(m):
        even = pairs[m, pl.ds(row, count, 2), :]
        odd = pairs[m, pl.ds(row + 1, count, 2), :]
        return [(coarse, (m + shift, slice(target, target + count)), 0.25 * (even + odd))]

    loop(low, high, step, unroll)


def correct(x, coarse, wide, low, high, plane, row, count, target, unroll=4, out=None):
    def widen(m):
        v = coarse[m, row : row + count, :]
        return [
            (wide, (m, pl.ds(target, count, 2)), v),
            (wide, (m, pl.ds(target + 1, count, 2)), v),
        ]

    loop(low, high, widen, 2 * unroll)
    out = x if out is None else out

    def add(m):
        i = 2 * m + plane
        w = wide[m]
        return [(out, i, x[i] + w), (out, i + 1, x[i + 1] + w)]

    loop(low, high, add, unroll)


def own_body(joined, up, down, b, d, planes):
    vel, g = joined.at[0:3], joined.at[3:6]
    den, vis, ndg = joined.at[6], joined.at[7], joined.at[8]

    def invert(i):
        return [(b, i, 1.0 / den[i])]

    loop(0, BLOCK, invert, 8)
    edge = BLOCK - 1

    def step(i):
        b0 = b[i]
        fz = 0.5 * (b0 + zdn_copy(b0)) * g[2, i]
        fy = 0.5 * (b0 + ydn(b0)) * g[1, i]
        rows = lax.broadcasted_iota(jnp.int32, fy.shape, 0)
        fy = jnp.where(rows == 0, 0.0, fy)
        total = (zup(fz) - fz) + (yup(fy) - fy)
        left = jnp.maximum(i - 1, 0)
        right = jnp.minimum(i + 1, edge)
        inner = jnp.where(i > 0, 0.5, 0.0) * (b0 + b[left]) * g[0, i]
        outer = jnp.where(i < edge, 0.5, 0.0) * (b0 + b[right]) * g[0, right]
        total = total + (outer - inner)
        k = BLOCK + i
        head = slice(0, PAD)
        out = [
            (d, i, total),
            (up, (i, head), b0[BLOCK - PAD :]),
            (up, (k, head), total[BLOCK - PAD :]),
            (down, (i, head), b0[:PAD]),
            (down, (k, head), total[:PAD]),
        ]
        for c in range(3):
            out.append((up, (k, PAD + 1 + c), g[c, i, edge, :]))
            out.append((down, (k, PAD + 1 + c), g[c, i, 0, :]))
        return out

    loop(0, BLOCK, step, 4)

    def edges(i):
        k = BLOCK + i
        out = []
        for c in range(3):
            out.append((up, (i, PAD + c), vel[c, i, edge, :]))
            out.append((down, (i, PAD + c), vel[c, i, 0, :]))
        out.append((up, (i, PAD + 3), vis[i, edge, :]))
        out.append((down, (i, PAD + 3), vis[i, 0, :]))
        out.append((up, (k, PAD), ndg[i, edge, :]))
        out.append((down, (k, PAD), ndg[i, 0, :]))
        return out

    loop(0, BLOCK, edges, 4)
    z = b.shape[2]
    up[2 * BLOCK] = jnp.zeros((BLOCK, z), F32)
    down[2 * BLOCK] = jnp.zeros((BLOCK, z), F32)
    up[2 * BLOCK, 0:PAD, :] = g[0, 0, BLOCK - PAD :, :]
    down[2 * BLOCK, 0:PAD, :] = g[0, 0, :PAD, :]
    for n, plane in enumerate((0, edge)):
        for c in range(3):
            planes[n, c, 0:BLOCK, :] = vel[c, plane]
            planes[n, c, BLOCK : 2 * BLOCK, :] = g[c, plane]
        planes[n, 3, 0:BLOCK, :] = vis[plane]
        planes[n, 3, BLOCK : 2 * BLOCK, :] = ndg[plane]


def rows_body(odd, b, d, down, planes, before, after, bb, dd, g0, even_send, odd_send):
    top = PAD + BLOCK

    def step(i):
        k = BLOCK + i
        own_flux = 0.5 * (b[i, 0:1, :] + before[i, PAD - 1 : PAD, :]) * down[k, PAD + 2 : PAD + 3, :]
        next_flux = (
            0.5
            * (b[i, BLOCK - 1 : BLOCK, :] + after[i, 0:1, :])
            * after[k, PAD + 2 : PAD + 3, :]
        )
        out = []
        for ref, own, m in ((bb, b, i), (dd, d, k)):
            out.append((ref, (i, slice(0, PAD)), before[m, 0:PAD, :]))
            out.append((ref, (i, slice(PAD, top)), own[i]))
            out.append((ref, (i, slice(top, top + PAD)), after[m, 0:PAD, :]))
        out.append((dd, (i, slice(PAD - 1, PAD)), before[k, PAD - 1 : PAD, :] + own_flux))
        out.append((dd, (i, slice(PAD, PAD + 1)), d[i, 0:1, :] - own_flux))
        out.append((dd, (i, slice(top - 1, top)), d[i, BLOCK - 1 : BLOCK, :] + next_flux))
        out.append((dd, (i, slice(top, top + 1)), after[k, 0:1, :] - next_flux))
        return out

    loop(0, BLOCK, step, 4)
    g0[0:PAD, :] = before[2 * BLOCK, 0:PAD, :]
    g0[PAD:top, :] = planes[0, 0, BLOCK : 2 * BLOCK, :]
    g0[top : top + PAD, :] = after[2 * BLOCK, 0:PAD, :]
    is_odd = odd[0]
    for send, last in ((even_send, 1 - is_odd), (odd_send, is_odd)):
        b_start = 5 * last
        d_start = 6 * last

        def b_step(m, send=send, b_start=b_start):
            return [(send, m, bb[b_start + m])]

        def d_step(m, send=send, d_start=d_start):
            return [(send, 11 + m, dd[d_start + m])]

        loop(0, 11, b_step, 11)
        loop(0, 10, d_step, 10)
        for c in range(4):
            send[21 + c, 0 : 2 * BLOCK, :] = planes[last, c]
        send[21, 32:40, :] = g0[0:8, :]
        send[22, 32:36, :] = g0[8:12, :]
        send[22, 36:40, :] = g0[28:32, :]
        send[23, 32:40, :] = g0[32:40, :]
        send[24, 32:40, :] = g0[32:40, :]


def fine_body(
    odd, bb, dd, g0, even_got, odd_got,
    f1_out, b1_out, f2_out, b2_out, up_out, down_out, slots_out, kept,
    pack, b, f0, diag, pairs, g1, xb, *rest,
):
    n1, (diag1, pairs1) = rest[:6], rest[6:8]
    n2, (own2, g2, x2, diag2, pairs2) = rest[8:14], rest[14:19]
    f1, b1, f2, b2, up, down, slots, sems = rest[19:]
    outs = ((f1, f1_out), (b1, b1_out), (up, up_out), (down, down_out))
    outs += ((f2, f2_out), (b2, b2_out), (slots, slots_out))
    moves = [pltpu.make_async_copy(a, b, sems.at[2 + n]) for n, (a, b) in enumerate(outs)]
    gf, x0 = pack.at[0], pack.at[7]
    n0 = tuple(pack.at[n] for n in range(1, 7))
    keep = slice(8, 32)
    saves = (
        pltpu.make_async_copy(pack.at[0:7, keep, keep], kept.at[0:7], sems.at[0]),
        pltpu.make_async_copy(pack.at[7, keep, keep], kept.at[7], sems.at[1]),
    )
    is_odd = odd[0] == 1
    top = PAD + BLOCK

    def left(m):
        return jnp.where(is_odd, even_got[0, m], odd_got[0, m])

    def right(m):
        return jnp.where(is_odd, odd_got[1, m], even_got[1, m])

    loop(0, BLOCK, lambda i: [(b, PAD + i, bb[i]), (f0, PAD + i, dd[i])], 4)
    loop(0, 11, lambda m: [(b, 1 + m, left(m)), (b, top + m, right(m))], 4)
    loop(0, 10, lambda m: [(f0, 2 + m, left(11 + m)), (f0, top + m, right(11 + m))], 5)
    flux = 0.5 * (b[PAD] + b[PAD - 1]) * g0[...]
    f0[PAD - 1] = f0[PAD - 1] + flux
    f0[PAD] = f0[PAD] - flux
    r1, r2, r3 = right(21), right(22), right(23)
    next_g0 = jnp.concatenate([r1[32:40], r2[32:36], r1[16:32], r2[36:40], r3[32:40]], 0)
    flux = 0.5 * (b[top] + b[top - 1]) * next_g0
    f0[top - 1] = f0[top - 1] + flux
    f0[top] = f0[top] - flux

    setup(b, n0, diag, 2, 38, 1.0, U0, f0, gf)
    saves[0].start()
    pre(gf, x0, n0, 3, 37, U0)
    saves[1].start()
    residual_pairs(gf, x0, diag, n0, pairs, 0, 2, 18, U0 // 2)
    row_pairs(pairs, f1, 2, 18, 0, 20, 0)
    plane_pairs(b, pairs, 0, 1, 19)
    row_pairs(pairs, b1, 1, 19, 0, 20, 0)

    z = b.shape[2]
    f1[:, 20:24, :] = jnp.zeros((20, 4, z), F32)
    b1[:, 20:24, :] = jnp.ones((20, 4, z), F32)
    setup(b1, n1, diag1, 2, 18, 0.25, U1, f1, g1)
    pre(g1, xb, n1, 3, 17, U1)
    residual_pairs(g1, xb, diag1, n1, pairs1, 4, 0, 6, U1 // 2)
    b2[...] = jnp.ones((16, 16, z), F32)
    row_pairs(pairs1, f2, 0, 6, 4, 6, 5, shift=5)
    plane_pairs(b1, pairs1, 2, 0, 8)
    row_pairs(pairs1, b2, 0, 8, 2, 8, 4, shift=4)

    for send, frow, brow, f1row, b1row in ((up, 5, 4, 9, 8), (down, 6, 6, 10, 11)):
        for m in range(6):
            send[m, 0:5, :] = f2[5 + m, frow : frow + 5, :]
        for m in range(8):
            send[m, 5:11, :] = b2[4 + m, brow : brow + 6, :]
        for m in range(16):
            send[m, 11:12, :] = f1[2 + m, f1row : f1row + 1, :]
        for m in range(18):
            send[m, 12:13, :] = b1[1 + m, b1row : b1row + 1, :]
    for move in moves[:6]:
        move.start()
    own2[...] = jnp.zeros((16, 16, z), F32)
    x2[...] = jnp.zeros((16, 16, z), F32)
    for m in range(6, 10):
        own2[m, 6:10, :] = f2[m, 6:10, :]
    setup(b2, n2, diag2, 4, 12, 0.25**2, 4, own2, g2)
    pre(g2, x2, n2, 5, 11, U2)
    residual_pairs(g2, x2, diag2, n2, pairs2, 4, 0, 4, 4)
    parts = []
    for m in range(4):
        even = pairs2[m, pl.ds(4, 4, 2), :]
        parts.append(0.25 * (even + pairs2[m, pl.ds(5, 4, 2), :]))
    plane_pairs(b2, pairs2, 6, 0, 2)
    for m in range(2):
        even = pairs2[m, pl.ds(6, 2, 2), :]
        parts.append(0.25 * (even + pairs2[m, pl.ds(7, 2, 2), :]))
    for n in range(4):
        slots[0, 4 * n : 4 * n + 4, :] = parts[n]
    slots[0, 16:18, :] = parts[4]
    slots[0, 18:20, :] = parts[5]
    slots[0, 20:24, :] = jnp.zeros((4, z), F32)
    value = slots[0]
    for m in range(1, 16):
        slots[m] = value
    moves[6].start()
    for save in (*saves, *moves):
        save.wait()


def rows2_body(
    odd, f1_in, b1_in, f2_in, b2_in, before_in, after_in, got_in,
    g1, h1, g2, h2, even_send, odd_strip, f2, b2, before, after, got, sems,
):
    pairs = ((got_in, got), (f1_in, g1), (b1_in, h1), (f2_in, f2), (b2_in, b2))
    pairs += ((before_in, before), (after_in, after))
    moves = [pltpu.make_async_copy(a, b, sems.at[n]) for n, (a, b) in enumerate(pairs)]
    for move in moves:
        move.start()
    for move in moves:
        move.wait()
    z = g1.shape[2]
    g2[...] = jnp.zeros((16, 16, z), F32)
    h2[...] = jnp.ones((16, 16, z), F32)
    for m in range(6):
        g2[5 + m, 6:10, :] = f2[5 + m, 6:10, :]
        g2[5 + m, 1:6, :] = before[m, 0:5, :]
        g2[5 + m, 10:15, :] = after[m, 0:5, :]
    for m in range(8):
        h2[4 + m, 6:10, :] = b2[4 + m, 6:10, :]
        h2[4 + m, 0:6, :] = before[m, 5:11, :]
        h2[4 + m, 10:16, :] = after[m, 5:11, :]
    for m in range(16):
        g1[2 + m, 1:2, :] = before[m, 11:12, :]
        g1[2 + m, 18:19, :] = after[m, 11:12, :]
    for m in range(18):
        h1[1 + m, 0:1, :] = before[m, 12:13, :]
        h1[1 + m, 19:20, :] = after[m, 12:13, :]
    at_y = lax.axis_index("gy")
    for p in range(16):
        here = lax.rem(at_y + (p + 8), 16)
        above = lax.rem(at_y + (p + 9), 16)
        below = lax.rem(at_y + (p + 7), 16)
        for n in range(4):
            k = 4 * n
            low = got[here, k + 1 : k + 2, :] + got[below, k + 3 : k + 4, :]
            high = got[here, k + 2 : k + 3, :] + got[above, k : k + 1, :]
            even_send[n, 2 * p : 2 * p + 1, :] = low
            even_send[n, 2 * p + 1 : 2 * p + 2, :] = high
        for n in range(2):
            even_send[4 + n, 2 * p : 2 * p + 2, :] = got[here, 16 + 2 * n : 18 + 2 * n, :]
    is_odd = odd[0]
    for send, first, last in ((even_send, 6, 1 - is_odd), (odd_strip, 0, is_odd)):
        for u in range(11):
            v = g2[6 - last + u] if u < 5 else h2[6 - 2 * last + (u - 5)]
            send[first + u // 2, (u % 2) * 16 : (u % 2) * 16 + 16, :] = v
        send[first + 5, 16:32, :] = jnp.zeros((16, z), F32)
        for n, v in ((6, g1[10 - last]), (7, h1[11 - 3 * last])):
            send[first + n, 0:24, :] = v
            send[first + n, 24:32, :] = jnp.zeros((8, z), F32)


def level3_body(
    odd, f1i, b1i, f2i, b2i, pair, other, far, slots, f1, b1, f2, b2, kept,
    pack, f3, b3, diag, pairs, small, sems,
):
    g3, x3, n3 = pack.at[0], pack.at[7], tuple(pack.at[n] for n in range(1, 7))
    save = pltpu.make_async_copy(pack, kept, sems.at[0])
    is_odd = odd[0] == 1
    blocks = [(other, (0, 0)), (other, (0, 1)), (pair, (0,)), (pair, (1,))]
    blocks += [(other, (1, 0)), (other, (1, 1))]

    def part(p, k):
        ref_even, at_even = (far, (0,)) if p == 0 else blocks[p - 1]
        ref_odd, at_odd = (far, (1,)) if p == 6 else blocks[p]
        return jnp.where(is_odd, ref_odd[(*at_odd, k)], ref_even[(*at_even, k)])

    for p in range(7):
        low, high = part(p, 1), part(p, 2)
        f3[2 * p] = low + part(p - 1, 3) if p > 0 else low
        f3[2 * p + 1] = high + part(p + 1, 0) if p < 6 else high
        b3[2 * p] = part(p, 4)
        b3[2 * p + 1] = part(p, 5)
    setup(b3, n3, diag, 1, 13, 0.25**3, U0, f3, g3)
    pre(g3, x3, n3, 2, 12, 5)
    save.start()
    residual_pairs(g3, x3, diag, n3, pairs, 6, 0, 1, 1)
    row_pairs(pairs, small, 0, 1, 0, 16, 0)
    plane_pairs(b3, pairs, 6, 0, 1)
    row_pairs(pairs, small, 0, 1, 0, 16, 0, shift=1)

    def spread(m):
        return [(slots, (m, n), small[n]) for n in range(2)]

    loop(0, 32, spread, 4)

    def left(n, rows):
        return jnp.where(is_odd, pair[0, 6 + n, rows, :], far[0, 6 + n, rows, :])

    def right(n, rows):
        return jnp.where(is_odd, far[1, 6 + n, rows, :], pair[1, 6 + n, rows, :])

    f1[...] = f1i[...]
    b1[...] = b1i[...]
    f2[...] = f2i[...]
    b2[...] = b2i[...]
    for u in range(11):
        rows = slice((u % 2) * 16, (u % 2) * 16 + 16)
        if u < 5:
            f2[1 + u] = left(u // 2, rows)
            f2[10 + u] = right(u // 2, rows)
        else:
            b2[u - 5] = left(u // 2, rows)
            b2[u + 5] = right(u // 2, rows)
    rows = slice(0, 24)
    f1[1] = left(6, rows)
    f1[18] = right(6, rows)
    b1[0] = left(7, rows)
    b1[19] = right(7, rows)
    save.wait()


def up_body(*refs):
    refs = list(refs)
    at_x = lax.axis_index("gx")

    def take(count):
        head = tuple(refs[:count])
        del refs[:count]
        return head

    kept = take(6)
    f1, b1, f2, b2, got, before, after, even_got, odd_got = take(9)
    out_vel, out_ndg, out_vis = take(3)
    held = take(6)
    pack3, pack0, vel, vis, g, ndg = held
    pack1, pack2 = take(2)
    f4, b4, g4, xa4, xb4, e4 = take(6)
    n4 = take(6)
    w3, v3, y3, t3, v2, w2, y2, t2, v1, w1, y1, t1, v0, w0, y0, t0 = take(16)
    vp, ap, visp, np_ = take(4)
    (sems,) = refs
    (g3, x3, n3), (g2, x2, n2), (g1, x1, n1), (g0, x0, n0) = (
        (pack.at[0], pack.at[7], tuple(pack.at[n] for n in range(1, 7)))
        for pack in (pack3, pack2, pack1, pack0)
    )
    loads = [
        pltpu.make_async_copy(source, target, sems.at[n])
        for n, (source, target) in enumerate(zip(kept, held, strict=True))
    ]
    for load in loads:
        load.start()
    devices = 2 * WIN + 1

    def gather(q):
        source = lax.rem(at_x + (q + 32 - WIN), 32)
        return [(f4, q, got[source, 0]), (b4, q, got[source, 1])]

    loop(0, devices, gather, devices)
    low, high = 1, devices - 1
    setup(b4, n4, None, low, high, 0.25**4, U2, f4, g4)

    def start(i):
        u = g4[i] * (1.0 / MID)
        return [(e4, i, u), (xa4, i, u)]

    loop(low, high, start, U2)
    ratio = RHO0
    x_now, x_next = xa4, xb4
    for _ in range(5):
        following = 1.0 / (2.0 * SIGMA - ratio)
        low, high = low + 1, high - 1

        def sweep(i, x_now=x_now, x_next=x_next, following=following, ratio=ratio):
            q0 = x_now[i]
            scaled = (g4[i] - q0) + around_sum(x_now, n4, i, q0)
            u = following * ratio * e4[i] + (2.0 * following / HALF) * scaled
            return [(e4, i, u), (x_next, i, q0 + u)]

        loop(low, high, sweep, U2)
        ratio = following
        x_now, x_next = x_next, x_now
    loads[0].wait()
    correct(x3, x_now, w3, 6, 11, -10, 0, 16, 0, out=v3)
    post(v3, g3, y3, t3, n3, 4, 10, U0)
    setup(b2, n2, None, 1, 15, 0.25**2, U2, f2, g2)
    pre(g2, x2, n2, 2, 14, U2)
    correct(x2, t3, w2, 4, 10, -6, 14, 6, 2, out=v2)
    post(v2, g2, y2, t2, n2, 4, 12, U2)
    setup(b1, n1, None, 1, 19, 0.25, U1, f1, g1)
    pre(g1, x1, n1, 2, 18, U1)
    correct(x1, t2, w1, 4, 12, -6, 4, 8, 2, out=v1)
    post(v1, g1, y1, t1, n1, 4, 16, U1)
    loads[1].wait()
    correct(x0, t1, w0, 4, 16, -8, 4, 12, 0, 2, out=v0)
    post(v0, g0, y0, t0, n0, 2, 21, U0)
    for load in loads[2:]:
        load.wait()

    def pad(i):
        k = BLOCK + i

        def put(out, own, source, row):
            out[0:1, :] = before[source, row : row + 1, :]
            out[1:17, :] = own
            out[17:18, :] = after[source, row : row + 1, :]

        for c in range(3):
            put(vp.at[c, i + 1], vel[c, i], i, PAD + c)
            put(ap.at[c, i + 1], g[c, i], k, PAD + 1 + c)
        put(visp.at[i + 1], vis[i], i, PAD + 3)
        put(np_.at[i + 1], ndg[i], k, PAD)

    loop(0, BLOCK, pad, 2)
    is_odd = lax.rem(at_x, 2) == 1

    def left(m):
        return jnp.where(is_odd, even_got[0, m], odd_got[0, m])

    def right(m):
        return jnp.where(is_odd, odd_got[1, m], even_got[1, m])

    for plane, side in ((0, left), (BLOCK + 1, right)):
        for c in range(3):
            both = side(21 + c)
            vp[c, plane, 1:17, :] = both[0:BLOCK]
            ap[c, plane, 1:17, :] = both[BLOCK : 2 * BLOCK]
        both = side(24)
        visp[plane, 1:17, :] = both[0:BLOCK]
        np_[plane, 1:17, :] = both[BLOCK : 2 * BLOCK]

    def lift(m):
        rows = slice(0, BLOCK + 2)
        centre = t0[m + 3, 3:21, :]
        return [
            (ap, (0, m, rows), ap[0, m, rows, :] + (centre - t0[m + 2, 3:21, :])),
            (ap, (1, m, rows), ap[1, m, rows, :] + (centre - t0[m + 3, 2:20, :])),
            (ap, (2, m, rows), ap[2, m, rows, :] + (centre - zdn(centre))),
        ]

    loop(0, BLOCK + 2, lift, 3)

    def finish(i):
        m = i + 1

        def around(ref):
            return (
                ref[m, 1:17, :],
                ref[m - 1, 1:17, :],
                ref[m + 1, 1:17, :],
                ref[m, 0:16, :],
                ref[m, 2:18, :],
            )

        speeds = [around(vp.at[c]) for c in range(3)]
        n0, nxm, nxp, nym, nyp = around(visp)
        fxm, fxp = 0.5 * (n0 + nxm), 0.5 * (nxp + n0)
        fym, fyp = 0.5 * (n0 + nym), 0.5 * (nyp + n0)
        fz = 0.5 * (n0 + zdn_copy(n0))
        u0m, u0p = speeds[0][1], speeds[0][2]
        u1m, u1p = speeds[1][3], speeds[1][4]
        u2 = speeds[2][0]

        def transport(q0, qxm, qxp, qym, qyp):
            up = u2 * q0
            return 0.5 * ((u0p * qxp - u0m * qxm) + (u1p * qyp - u1m * qym) + (zup(up) - zdn(up)))

        fields = around(np_)
        out_ndg[i] = fields[0] + DT * transport(*fields)
        gxm = gxp = gym = gyp = gz = 0.0
        for c in range(3):
            fields = around(ap.at[c])
            q0, qxm, qxp, qym, qyp = fields
            s0, sxm, sxp, sym, syp = speeds[c]
            dxm, dxp, dym, dyp = q0 - qxm, qxp - q0, q0 - qym, qyp - q0
            dz = q0 - zdn(q0)
            flux = fz * dz
            spread = (fxp * dxp - fxm * dxm) + (fyp * dyp - fym * dym) + (zup(flux) - flux)
            out_vel[c, i] = q0 + DT * (transport(*fields) + spread)
            gxm = gxm + dxm * (s0 - sxm)
            gxp = gxp + dxp * (sxp - s0)
            gym = gym + dym * (s0 - sym)
            gyp = gyp + dyp * (syp - s0)
            gz = gz + dz * (s0 - zdn(s0))
        bottom = jnp.where(layer(gz) == 0, gz, 0.0)
        out_vis[i] = (-0.5 * DT) * ((gxm + gxp) + (gym + gyp) + (gz + zup(gz)) + bottom)

    loop(0, BLOCK, finish, 2)


def shards(velocity, density, viscosity, grad_out, density_gradient):
    z = density.shape[2]
    size_x, size_y = lax.axis_size("gx"), lax.axis_size("gy")
    at_x = lax.axis_index("gx")
    odd = lax.rem(at_x, 2).astype(jnp.int32).reshape(1)
    even_pairs = [[i, i + 1] for i in range(0, size_x, 2)]
    odd_pairs = [[i, (i + 1) % size_x] for i in range(1, size_x, 2)]
    forward = [(i, (i + 1) % size_y) for i in range(size_y)]
    backward = [(j, i) for i, j in forward]

    def along_y(up, down):
        return lax.ppermute(up, "gy", forward), lax.ppermute(down, "gy", backward)

    fine = (40, 40, z)
    mid = (20, 24, z)
    low = (16, 16, z)
    rim = (2 * BLOCK + 1, BLOCK, z)
    own = (BLOCK, BLOCK, z)
    fields = (velocity, viscosity, grad_out, density_gradient)
    single = [v[None] for v in (density, viscosity, density_gradient)]
    joined = jnp.concatenate([velocity, grad_out, *single], 0)
    up, down, b, d, planes = call(
        own_body,
        [rim, rim, own, own, (2, 4, 2 * BLOCK, z)],
        (joined,),
    )
    before, after = along_y(up, down)
    send = (25, 40, z)
    bb, dd, g0, even_send, odd_send = call(
        rows_body,
        [(BLOCK, 40, z), (BLOCK, 40, z), (40, z), send, send],
        (odd, b, d, down, planes, before, after),
        scalars=1,
    )
    even_got = lax.all_gather(even_send, "gx", axis_index_groups=even_pairs)
    odd_got = lax.all_gather(odd_send, "gx", axis_index_groups=odd_pairs)
    f1, b1, f2, b2, up, down, slots, kept0 = call(
        fine_body,
        [mid, mid, low, low, (18, 16, z), (18, 16, z), (size_y, 24, z), (8, 24, 24, z)],
        (odd, bb, dd, g0, even_got, odd_got),
        [(8, *fine), fine, fine, fine, (20, 40, z)]
        + [mid] * 9
        + [(8, 24, z)]
        + [low] * 10
        + [(4, 16, z)]
        + [mid, mid, low, low, (18, 16, z), (18, 16, z), (size_y, 24, z)],
        scalars=1,
        kept=8,
        sems=9,
        megabytes=51,
    )
    got = lax.all_to_all(slots, "gy", 0, 0, tiled=True)
    before2, after2 = along_y(up, down)
    f1, b1, f2, b2, even_send, odd_strip = call(
        rows2_body,
        [mid, mid, low, low, (14, 32, z), (8, 32, z)],
        (odd, f1, b1, f2, b2, before2, after2, got),
        [low, low, (18, 16, z), (18, 16, z), (size_y, 24, z)],
        scalars=1,
        fetched=7,
        sems=7,
    )
    at_odd = lax.rem(at_x, 2)
    pair = lax.all_gather(even_send, "gx", axis_index_groups=even_pairs)
    side = lax.all_gather(pair[:, 0:6], "gx", axis_index_groups=odd_pairs)
    side = lax.dynamic_index_in_dim(side, at_odd, 0, keepdims=False)
    other = lax.all_gather(side, "gx", axis_index_groups=even_pairs)
    far = lax.dynamic_index_in_dim(other.reshape(4, 6, 32, z), 2 - at_odd, 0, keepdims=False)
    far = jnp.concatenate([far, odd_strip], 0)
    far = lax.all_gather(far, "gx", axis_index_groups=odd_pairs)
    level3 = (14, 32, z)
    slots, f1, b1, f2, b2, kept3 = call(
        level3_body,
        [(size_x, 2, 16, z), mid, mid, low, low, (8, *level3)],
        (odd, f1, b1, f2, b2, pair, other, far),
        [(8, *level3), level3, level3, level3, (1, 32, z), (2, 16, z)],
        scalars=1,
        kept=1,
        sems=1,
    )
    got = lax.all_to_all(slots, "gx", 0, 0, tiled=True)
    devices = 2 * WIN + 1
    return tuple(
        call(
            up_body,
            [(3, *own), own, own],
            (kept3, kept0, *fields, f1, b1, f2, b2, got, before, after, even_got, odd_got),
            [(8, *level3), (8, 24, 24, z), (3, *own), own, (3, *own), own, (8, *mid), (8, *low)]
            + [(devices, 16, z)] * 12
            + [(11, 32, z), level3, level3, level3]
            + [low, (10, 16, z), low, low]
            + [mid, (12, 24, z), mid, mid]
            + [(24, 24, z), (16, 24, z), (24, 24, z), (24, 24, z)]
            + [(3, 18, 24, z), (3, 18, 24, z), (18, 24, z), (18, 24, z)],
            megabytes=24,
            fetched=6,
            sems=6,
        )
    )


def solution(mesh):
    placed = (
        P(None, "gx", "gy", None),
        P("gx", "gy", None),
        P("gx", "gy", None),
        P(None, "gx", "gy", None),
        P("gx", "gy", None),
    )
    return jax.shard_map(
        shards,
        mesh=mesh,
        in_specs=placed,
        out_specs=(P(None, "gx", "gy", None), P("gx", "gy", None), P("gx", "gy", None)),
        check_vma=False,
    )
```

```python
import functools

import jax
import jax.numpy as jnp
from jax import lax
from jax.experimental import pallas as pl
from jax.experimental.pallas import tpu as pltpu
from jax.sharding import PartitionSpec as P

INTERPRET = False
DT = 0.2
MID = 1.2
HALF = 0.8
SIGMA = MID / HALF
RHO0 = 1.0 / SIGMA
RHO1 = 1.0 / (2.0 * SIGMA - RHO0)
A1 = RHO1 * RHO0
B1 = 2.0 * RHO1 / HALF
BLOCK = 16
PAD = 8
PAD1 = 6
U0, U1, U2 = 4, 4, 6
WIN = 8
F32 = jnp.float32


def call(body, out_shapes, args, scratch=(), scalars=0, megabytes=16, fetched=0, kept=0, sems=0):
    smem = [pl.BlockSpec(memory_space=pltpu.SMEM)] * scalars
    far = pl.BlockSpec(memory_space=pltpu.HBM)
    near = pl.BlockSpec(memory_space=pltpu.VMEM)
    scratch = [pltpu.VMEM(s, F32) for s in scratch]
    if sems:
        scratch.append(pltpu.SemaphoreType.DMA((sems,)))
    return pl.pallas_call(
        body,
        out_shape=[jax.ShapeDtypeStruct(s, F32) for s in out_shapes],
        in_specs=smem + [far] * fetched + [near] * (len(args) - scalars - fetched),
        out_specs=[near] * (len(out_shapes) - kept) + [far] * kept,
        scratch_shapes=scratch,
        compiler_params=pltpu.CompilerParams(vmem_limit_bytes=megabytes * 2**20),
        interpret=INTERPRET,
    )(*args)


def loop(low, high, step, unroll=1):
    def group(base, count):
        stores = []
        for u in range(count):
            stores.extend(step(base + u) or ())
        for ref, index, value in stores:
            ref[index] = value

    groups = (high - low) // unroll
    if groups == 1:
        group(low, unroll)
    elif groups > 1:
        lax.fori_loop(0, groups, lambda n, c: (group(low + n * unroll, unroll), c)[1], 0)
    rest = (high - low) - groups * unroll
    if rest:
        group(high - rest, rest)


def ydn(v):
    return pltpu.roll(v, 1, axis=0)


def yup(v):
    return pltpu.roll(v, v.shape[0] - 1, axis=0)


def layer(v):
    return lax.broadcasted_iota(jnp.int32, v.shape, 1)


def zroll_dn(v):
    return pltpu.roll(v, 1, axis=1)


def zroll_up(v):
    return pltpu.roll(v, v.shape[1] - 1, axis=1)


def zdn(v):
    return jnp.where(layer(v) == 0, 0.0, zroll_dn(v))


def zdn_copy(v):
    return jnp.where(layer(v) == 0, v, zroll_dn(v))


def zup(v):
    return jnp.where(layer(v) == v.shape[1] - 1, 0.0, zroll_up(v))


def setup(b, n, diag, low, high, scale, unroll, f=None, g=None, g_range=None):
    half = 0.5 * scale

    def step(i):
        b0 = b[i]
        fxm = half * (b0 + b[i - 1])
        fxp = half * (b[i + 1] + b0)
        fym = half * (b0 + ydn(b0))
        fyp = yup(fym)
        fz = 0.5 * (b0 + zdn_copy(b0))
        fzp = zup(fz)
        d = (fxm + fxp) + (fym + fyp) + (fz + fzp)
        inv = 1.0 / d
        fzm = jnp.where(layer(fz) == 0, 0.0, fz)
        out = [(ref, i, v * inv) for ref, v in zip(n, (fxm, fxp, fym, fyp, fzm, fzp), strict=True)]
        if diag is not None:
            out.append((diag, i, d))
        if f is not None:
            out.append((g, i, f[i] * inv))
        return out

    loop(low, high, step, unroll)


def around_sum(q, n, i, q0):
    total = (n[0][i] * q[i - 1] + n[1][i] * q[i + 1]) + (n[2][i] * ydn(q0) + n[3][i] * yup(q0))
    return total + (n[4][i] * zroll_dn(q0) + n[5][i] * zroll_up(q0))


def pre(g, x, n, low, high, unroll):
    first = (1.0 + A1) / MID + B1 * (1.0 - 1.0 / MID)

    def step(i):
        g0 = g[i]
        return [(x, i, first * g0 + (B1 / MID) * around_sum(g, n, i, g0))]

    loop(low, high, step, unroll)


def post(x, g, y, out, n, low, high, unroll):
    def first(i):
        x0 = x[i]
        return [(y, i, x0 + (1.0 / MID) * ((g[i] - x0) + around_sum(x, n, i, x0)))]

    loop(low - 1, high + 1, first, unroll)

    def second(i):
        y0 = y[i]
        z = (g[i] - y0) + around_sum(y, n, i, y0)
        return [(out, i, y0 + (A1 * (y0 - x[i]) + B1 * z))]

    loop(low, high, second, unroll)


def residual_pairs(g, x, diag, n, pairs, start, low, high, unroll):
    def one(i):
        x0 = x[i]
        return diag[i] * ((g[i] - x0) + around_sum(x, n, i, x0))

    def step(m):
        i = start + 2 * m
        return [(pairs, m, one(i) + one(i + 1))]

    loop(low, high, step, unroll)


def plane_pairs(b, pairs, start, low, high, unroll=4):
    def step(m):
        return [(pairs, m, b[start + 2 * m] + b[start + 2 * m + 1])]

    loop(low, high, step, unroll)


def row_pairs(pairs, coarse, low, high, row, count, target, shift=0, unroll=8):
    def step(m):
        even = pairs[m, pl.ds(row, count, 2), :]
        odd = pairs[m, pl.ds(row + 1, count, 2), :]
        return [(coarse, (m + shift, slice(target, target + count)), 0.25 * (even + odd))]

    loop(low, high, step, unroll)


def correct(x, coarse, wide, low, high, plane, row, count, target, unroll=4, out=None):
    def widen(m):
        v = coarse[m, row : row + count, :]
        return [
            (wide, (m, pl.ds(target, count, 2)), v),
            (wide, (m, pl.ds(target + 1, count, 2)), v),
        ]

    loop(low, high, widen, 2 * unroll)
    out = x if out is None else out

    def add(m):
        i = 2 * m + plane
        w = wide[m]
        return [(out, i, x[i] + w), (out, i + 1, x[i + 1] + w)]

    loop(low, high, add, unroll)


def own_body(joined, up, down, b, d, planes):
    vel, g = joined.at[0:3], joined.at[3:6]
    den, vis, ndg = joined.at[6], joined.at[7], joined.at[8]

    def invert(i):
        return [(b, i, 1.0 / den[i])]

    loop(0, BLOCK, invert, 8)
    edge = BLOCK - 1

    def step(i):
        b0 = b[i]
        fz = 0.5 * (b0 + zdn_copy(b0)) * g[2, i]
        fy = 0.5 * (b0 + ydn(b0)) * g[1, i]
        rows = lax.broadcasted_iota(jnp.int32, fy.shape, 0)
        fy = jnp.where(rows == 0, 0.0, fy)
        total = (zup(fz) - fz) + (yup(fy) - fy)
        left = jnp.maximum(i - 1, 0)
        right = jnp.minimum(i + 1, edge)
        inner = jnp.where(i > 0, 0.5, 0.0) * (b0 + b[left]) * g[0, i]
        outer = jnp.where(i < edge, 0.5, 0.0) * (b0 + b[right]) * g[0, right]
        total = total + (outer - inner)
        head, next_rows = slice(0, PAD), slice(PAD, 2 * PAD)
        out = [
            (d, i, total),
            (up, (i, head), b0[BLOCK - PAD :]),
            (up, (i, next_rows), total[BLOCK - PAD :]),
            (down, (i, head), b0[:PAD]),
            (down, (i, next_rows), total[:PAD]),
        ]
        for send, row in ((up, edge), (down, 0)):
            for c in range(3):
                out.append((send, (i, 16 + c), vel[c, i, row, :]))
                out.append((send, (i, 21 + c), g[c, i, row, :]))
            out.append((send, (i, 19), vis[i, row, :]))
            out.append((send, (i, 20), ndg[i, row, :]))
        return out

    loop(0, BLOCK, step, 4)
    z = b.shape[2]
    up[BLOCK] = jnp.zeros((24, z), F32)
    down[BLOCK] = jnp.zeros((24, z), F32)
    up[BLOCK, 0:PAD, :] = g[0, 0, BLOCK - PAD :, :]
    down[BLOCK, 0:PAD, :] = g[0, 0, :PAD, :]
    for n, plane in enumerate((0, edge)):
        for c in range(3):
            planes[n, c, 0:BLOCK, :] = vel[c, plane]
            planes[n, c, BLOCK : 2 * BLOCK, :] = g[c, plane]
        planes[n, 3, 0:BLOCK, :] = vis[plane]
        planes[n, 3, BLOCK : 2 * BLOCK, :] = ndg[plane]


def rows_body(odd, b, d, down, planes, before, after, bb, dd, g0, even_send, odd_send):
    top = PAD + BLOCK

    def step(i):
        own_flux = 0.5 * (b[i, 0:1, :] + before[i, PAD - 1 : PAD, :]) * down[i, 22:23, :]
        next_flux = 0.5 * (b[i, BLOCK - 1 : BLOCK, :] + after[i, 0:1, :]) * after[i, 22:23, :]
        out = []
        for ref, own, row in ((bb, b, 0), (dd, d, PAD)):
            out.append((ref, (i, slice(0, PAD)), before[i, row : row + PAD, :]))
            out.append((ref, (i, slice(PAD, top)), own[i]))
            out.append((ref, (i, slice(top, top + PAD)), after[i, row : row + PAD, :]))
        out.append((dd, (i, slice(PAD - 1, PAD)), before[i, 2 * PAD - 1 : 2 * PAD, :] + own_flux))
        out.append((dd, (i, slice(PAD, PAD + 1)), d[i, 0:1, :] - own_flux))
        out.append((dd, (i, slice(top - 1, top)), d[i, BLOCK - 1 : BLOCK, :] + next_flux))
        out.append((dd, (i, slice(top, top + 1)), after[i, PAD : PAD + 1, :] - next_flux))
        return out

    loop(0, BLOCK, step, 4)
    g0[0:PAD, :] = before[BLOCK, 0:PAD, :]
    g0[PAD:top, :] = planes[0, 0, BLOCK : 2 * BLOCK, :]
    g0[top : top + PAD, :] = after[BLOCK, 0:PAD, :]
    is_odd = odd[0]
    for send, last in ((even_send, 1 - is_odd), (odd_send, is_odd)):
        b_start = 8 * last
        d_start = 10 * last

        def b_step(m, send=send, b_start=b_start):
            return [(send, m, bb[b_start + m])]

        def d_step(m, send=send, d_start=d_start):
            return [(send, 8 + m, dd[d_start + m])]

        loop(0, 8, b_step, 8)
        loop(0, 6, d_step, 6)
        for c in range(4):
            send[14 + c] = planes[last, c]
        send[18] = g0[...]


def fine_body(
    odd, bb, dd, g0, even_got, odd_got,
    f1_out, b1_out, f2_out, b2_out, up_out, down_out, slots_out, kept,
    pack, b, f0, diag, pairs, g1, xb, *rest,
):
    n1, (diag1, pairs1) = rest[:6], rest[6:8]
    n2, (g2, x2, diag2, pairs2) = rest[8:14], rest[14:18]
    f1, b1, f2, b2, up, down, slots, sems = rest[18:]
    outs = ((f1, f1_out), (b1, b1_out), (up, up_out), (down, down_out))
    outs += ((f2, f2_out), (b2, b2_out), (slots, slots_out))
    moves = [pltpu.make_async_copy(a, b, sems.at[2 + n]) for n, (a, b) in enumerate(outs)]
    gf, x0 = pack.at[0], pack.at[7]
    n0 = tuple(pack.at[n] for n in range(1, 7))
    keep = slice(4, 28)
    saves = (
        pltpu.make_async_copy(pack.at[0:7, keep], kept.at[0:7], sems.at[0]),
        pltpu.make_async_copy(pack.at[7, keep], kept.at[7], sems.at[1]),
    )
    is_odd = odd[0] == 1
    top = PAD + BLOCK

    def left(m):
        return jnp.where(is_odd, even_got[0, m], odd_got[0, m])

    def right(m):
        return jnp.where(is_odd, odd_got[1, m], even_got[1, m])

    loop(0, BLOCK, lambda i: [(b, PAD + i, bb[i]), (f0, PAD + i, dd[i])], 4)
    loop(0, 8, lambda m: [(b, m, left(m)), (b, top + m, right(m))], 4)
    loop(0, 6, lambda m: [(f0, 2 + m, left(8 + m)), (f0, top + m, right(8 + m))], 6)
    flux = 0.5 * (b[PAD] + b[PAD - 1]) * g0[...]
    f0[PAD - 1] = f0[PAD - 1] + flux
    f0[PAD] = f0[PAD] - flux
    flux = 0.5 * (b[top] + b[top - 1]) * right(18)
    f0[top - 1] = f0[top - 1] + flux
    f0[top] = f0[top] - flux

    setup(b, n0, diag, 2, 30, 1.0, U0, f0, gf)
    saves[0].start()
    pre(gf, x0, n0, 3, 29, U0)
    saves[1].start()
    residual_pairs(gf, x0, diag, n0, pairs, 0, 2, 14, U0 // 2)
    row_pairs(pairs, f1, 2, 14, 0, 16, 0)
    plane_pairs(b, pairs, 0, 0, 16)
    row_pairs(pairs, b1, 0, 16, 0, 16, 0)

    z = b.shape[2]
    setup(b1, n1, diag1, 2, 14, 0.25, U2, f1, g1)
    pre(g1, xb, n1, 3, 13, U2)
    residual_pairs(g1, xb, diag1, n1, pairs1, 4, 0, 4, 4)
    f2[...] = jnp.zeros((16, 16, z), F32)
    b2[...] = jnp.ones((16, 16, z), F32)
    row_pairs(pairs1, f2, 0, 4, 4, 4, 6, shift=6)
    plane_pairs(b1, pairs1, 0, 0, 8)
    row_pairs(pairs1, b2, 0, 8, 0, 8, 4, shift=4)

    for send, brow, f1row, b1row in ((up, 4, 7, 6), (down, 6, 6, 8)):
        for m in range(4):
            send[m, 0:4, :] = f2[6 + m, 6:10, :]
        for m in range(8):
            send[m, 4:10, :] = b2[4 + m, brow : brow + 6, :]
        for m in range(2, 14):
            send[m, 10:13, :] = f1[m, f1row : f1row + 3, :]
        for m in range(16):
            send[m, 13:15, :] = b1[m, b1row : b1row + 2, :]
    for move in moves[:6]:
        move.start()
    x2[...] = jnp.zeros((16, 16, z), F32)
    setup(b2, n2, diag2, 4, 12, 0.25**2, 4, f2, g2)
    pre(g2, x2, n2, 5, 11, U2)
    residual_pairs(g2, x2, diag2, n2, pairs2, 4, 0, 4, 4)
    parts = []
    for m in range(4):
        even = pairs2[m, pl.ds(4, 4, 2), :]
        parts.append(0.25 * (even + pairs2[m, pl.ds(5, 4, 2), :]))
    plane_pairs(b2, pairs2, 6, 0, 2)
    for m in range(2):
        even = pairs2[m, pl.ds(6, 2, 2), :]
        parts.append(0.25 * (even + pairs2[m, pl.ds(7, 2, 2), :]))
    for n in range(4):
        slots[0, 4 * n : 4 * n + 4, :] = parts[n]
    slots[0, 16:18, :] = parts[4]
    slots[0, 18:20, :] = parts[5]
    for n in range(4):
        slots[0, 20 + n : 21 + n, :] = f2[6 + n, 6:7, :]
        slots[0, 24 + n : 25 + n, :] = f2[6 + n, 9:10, :]
    slots[0, 28:32, :] = jnp.zeros((4, z), F32)
    value = slots[0]
    for m in range(1, 16):
        slots[m] = value
    moves[6].start()
    for save in (*saves, *moves):
        save.wait()


def rows2_body(
    odd, f1_in, b1_in, f2_in, b2_in, before_in, after_in, got_in,
    g1, h1, g2, h2, even_send, odd_strip, f1, b1, f2, b2, before, after, got, sems,
):
    pairs = ((got_in, got), (f1_in, f1), (b1_in, b1), (f2_in, f2), (b2_in, b2))
    pairs += ((before_in, before), (after_in, after))
    moves = [pltpu.make_async_copy(a, b, sems.at[n]) for n, (a, b) in enumerate(pairs)]
    for move in moves:
        move.start()
    for move in moves:
        move.wait()
    z = g1.shape[2]
    g1[...] = jnp.zeros((20, 24, z), F32)
    h1[...] = jnp.ones((20, 24, z), F32)
    g2[...] = jnp.zeros((16, 16, z), F32)
    h2[...] = jnp.ones((16, 16, z), F32)
    at_y = lax.axis_index("gy")
    back, ahead = lax.rem(at_y + 14, 16), lax.rem(at_y + 2, 16)
    for m in range(4):
        g2[6 + m, 6:10, :] = f2[6 + m, 6:10, :]
        g2[6 + m, 2:6, :] = before[m, 0:4, :]
        g2[6 + m, 10:14, :] = after[m, 0:4, :]
        g2[6 + m, 1:2, :] = got[back, 24 + m : 25 + m, :]
        g2[6 + m, 14:15, :] = got[ahead, 20 + m : 21 + m, :]
    for m in range(8):
        h2[4 + m, 6:10, :] = b2[4 + m, 6:10, :]
        h2[4 + m, 0:6, :] = before[m, 4:10, :]
        h2[4 + m, 10:16, :] = after[m, 4:10, :]
    for m in range(2, 14):
        g1[2 + m, 4:16, :] = f1[m, 2:14, :]
        g1[2 + m, 1:4, :] = before[m, 10:13, :]
        g1[2 + m, 16:19, :] = after[m, 10:13, :]
    for m in range(16):
        h1[2 + m, 2:18, :] = b1[m]
        h1[2 + m, 0:2, :] = before[m, 13:15, :]
        h1[2 + m, 18:20, :] = after[m, 13:15, :]
    for p in range(16):
        here = lax.rem(at_y + (p + 8), 16)
        above = lax.rem(at_y + (p + 9), 16)
        below = lax.rem(at_y + (p + 7), 16)
        for n in range(4):
            k = 4 * n
            low = got[here, k + 1 : k + 2, :] + got[below, k + 3 : k + 4, :]
            high = got[here, k + 2 : k + 3, :] + got[above, k : k + 1, :]
            even_send[n, 2 * p : 2 * p + 1, :] = low
            even_send[n, 2 * p + 1 : 2 * p + 2, :] = high
        for n in range(2):
            even_send[4 + n, 2 * p : 2 * p + 2, :] = got[here, 16 + 2 * n : 18 + 2 * n, :]
    is_odd = odd[0]
    even_send[6, 0:16, :] = g2[6]
    even_send[6, 16:32, :] = g2[9]
    for send, first, last in ((even_send, 7, 1 - is_odd), (odd_strip, 0, is_odd)):
        for u in range(10):
            v = g2[6 + u] if u < 4 else h2[6 - 2 * last + (u - 4)]
            send[first + u // 2, (u % 2) * 16 : (u % 2) * 16 + 16, :] = v
        for n in range(5):
            v = g1[8 + last + n] if n < 3 else h1[10 - 2 * last + (n - 3)]
            send[first + 5 + n, 0:24, :] = v
            send[first + 5 + n, 24:32, :] = jnp.zeros((8, z), F32)


def level3_body(
    odd, f1i, b1i, f2i, b2i, pair, other, far, slots, f1, b1, f2, b2, kept,
    pack, f3, b3, diag, pairs, small, sems,
):
    g3, x3, n3 = pack.at[0], pack.at[7], tuple(pack.at[n] for n in range(1, 7))
    save = pltpu.make_async_copy(pack, kept, sems.at[0])
    is_odd = odd[0] == 1
    blocks = [(other, (0, 0)), (other, (0, 1)), (pair, (0,)), (pair, (1,))]
    blocks += [(other, (1, 0)), (other, (1, 1))]

    z = f3.shape[2]

    def distant(slot, k):
        rim = (jnp.zeros if k < 4 else jnp.ones)((8, z), F32)
        rows = slice((k % 2) * 16, (k % 2) * 16 + 16)
        return jnp.concatenate([rim, far[slot, k // 2, rows, :], rim], 0)

    def part(p, k):
        even = distant(0, k) if p == 0 else blocks[p - 1][0][(*blocks[p - 1][1], k)]
        odds = distant(1, k) if p == 6 else blocks[p][0][(*blocks[p][1], k)]
        return jnp.where(is_odd, odds, even)

    for p in range(7):
        low, high = part(p, 1), part(p, 2)
        f3[2 * p] = low + part(p - 1, 3) if p > 0 else low
        f3[2 * p + 1] = high + part(p + 1, 0) if p < 6 else high
        b3[2 * p] = part(p, 4)
        b3[2 * p + 1] = part(p, 5)
    setup(b3, n3, diag, 1, 13, 0.25**3, U0, f3, g3)
    pre(g3, x3, n3, 2, 12, 5)
    save.start()
    residual_pairs(g3, x3, diag, n3, pairs, 6, 0, 1, 1)
    row_pairs(pairs, small, 0, 1, 0, 16, 0)
    plane_pairs(b3, pairs, 6, 0, 1)
    row_pairs(pairs, small, 0, 1, 0, 16, 0, shift=1)

    def spread(m):
        return [(slots, (m, n), small[n]) for n in range(2)]

    loop(0, 32, spread, 4)

    def left(n, rows):
        return jnp.where(is_odd, pair[0, 7 + n, rows, :], far[0, 3 + n, rows, :])

    def right(n, rows):
        return jnp.where(is_odd, far[1, 3 + n, rows, :], pair[1, 7 + n, rows, :])

    f1[...] = f1i[...]
    b1[...] = b1i[...]
    f2[...] = f2i[...]
    b2[...] = b2i[...]
    for u in range(10):
        rows = slice((u % 2) * 16, (u % 2) * 16 + 16)
        if u < 4:
            f2[2 + u] = left(u // 2, rows)
            f2[10 + u] = right(u // 2, rows)
        else:
            b2[u - 4] = left(u // 2, rows)
            b2[u + 6] = right(u // 2, rows)
    f2[1] = part(1, 6)[16:32]
    f2[14] = part(5, 6)[0:16]
    rows = slice(0, 24)
    for n in range(3):
        f1[1 + n] = left(5 + n, rows)
        f1[16 + n] = right(5 + n, rows)
    for n in range(2):
        b1[n] = left(8 + n, rows)
        b1[18 + n] = right(8 + n, rows)
    save.wait()


def up_body(*refs):
    refs = list(refs)
    at_x = lax.axis_index("gx")

    def take(count):
        head = tuple(refs[:count])
        del refs[:count]
        return head

    kept = take(6)
    f1, b1, f2, b2, got, before, after, even_got, odd_got = take(9)
    out_vel, out_ndg, out_vis = take(3)
    held = take(6)
    pack3, pack0, vel, vis, g, ndg = held
    pack1, pack2 = take(2)
    f4, b4, g4, xa4, xb4, e4 = take(6)
    n4 = take(6)
    w3, v3, y3, t3, v2, w2, y2, t2, v1, w1, y1, t1, v0, w0, y0, t0 = take(16)
    vp, ap, visp, np_ = take(4)
    (sems,) = refs
    (g3, x3, n3), (g2, x2, n2), (g1, x1, n1), (g0, x0, n0) = (
        (pack.at[0], pack.at[7], tuple(pack.at[n] for n in range(1, 7)))
        for pack in (pack3, pack2, pack1, pack0)
    )
    loads = [
        pltpu.make_async_copy(source, target, sems.at[n])
        for n, (source, target) in enumerate(zip(kept, held, strict=True))
    ]
    for load in loads:
        load.start()
    devices = 2 * WIN + 1

    def gather(q):
        source = lax.rem(at_x + (q + 32 - WIN), 32)
        return [(f4, q, got[source, 0]), (b4, q, got[source, 1])]

    loop(0, devices, gather, devices)
    low, high = 1, devices - 1
    setup(b4, n4, None, low, high, 0.25**4, U2, f4, g4)

    def start(i):
        u = g4[i] * (1.0 / MID)
        return [(e4, i, u), (xa4, i, u)]

    loop(low, high, start, U2)
    ratio = RHO0
    x_now, x_next = xa4, xb4
    for _ in range(5):
        following = 1.0 / (2.0 * SIGMA - ratio)
        low, high = low + 1, high - 1

        def sweep(i, x_now=x_now, x_next=x_next, following=following, ratio=ratio):
            q0 = x_now[i]
            scaled = (g4[i] - q0) + around_sum(x_now, n4, i, q0)
            u = following * ratio * e4[i] + (2.0 * following / HALF) * scaled
            return [(e4, i, u), (x_next, i, q0 + u)]

        loop(low, high, sweep, U2)
        ratio = following
        x_now, x_next = x_next, x_now
    loads[0].wait()
    correct(x3, x_now, w3, 6, 11, -10, 0, 16, 0, out=v3)
    post(v3, g3, y3, t3, n3, 4, 10, U0)
    setup(b2, n2, None, 1, 15, 0.25**2, U2, f2, g2)
    pre(g2, x2, n2, 2, 14, U2)
    correct(x2, t3, w2, 4, 10, -6, 14, 6, 2, out=v2)
    post(v2, g2, y2, t2, n2, 4, 12, U2)
    setup(b1, n1, None, 1, 19, 0.25, U1, f1, g1)
    pre(g1, x1, n1, 2, 18, U1)
    correct(x1, t2, w1, 4, 12, -6, 4, 8, 2, out=v1)
    post(v1, g1, y1, t1, n1, 4, 16, U1)
    loads[1].wait()
    correct(x0, t1, w0, 4, 16, -8, 4, 12, 4, 2, out=v0)
    post(v0, g0, y0, t0, n0, 2, 21, U0)
    for load in loads[2:]:
        load.wait()

    def pad(i):
        def put(out, own, source, row):
            out[0:1, :] = before[source, row : row + 1, :]
            out[1:17, :] = own
            out[17:18, :] = after[source, row : row + 1, :]

        for c in range(3):
            put(vp.at[c, i + 1], vel[c, i], i, 16 + c)
            put(ap.at[c, i + 1], g[c, i], i, 21 + c)
        put(visp.at[i + 1], vis[i], i, 19)
        put(np_.at[i + 1], ndg[i], i, 20)

    loop(0, BLOCK, pad, 2)
    is_odd = lax.rem(at_x, 2) == 1

    def left(m):
        return jnp.where(is_odd, even_got[0, m], odd_got[0, m])

    def right(m):
        return jnp.where(is_odd, odd_got[1, m], even_got[1, m])

    for plane, side in ((0, left), (BLOCK + 1, right)):
        for c in range(3):
            both = side(14 + c)
            vp[c, plane, 1:17, :] = both[0:BLOCK]
            ap[c, plane, 1:17, :] = both[BLOCK : 2 * BLOCK]
        both = side(17)
        visp[plane, 1:17, :] = both[0:BLOCK]
        np_[plane, 1:17, :] = both[BLOCK : 2 * BLOCK]

    def lift(m):
        rows = slice(0, BLOCK + 2)
        centre = t0[m + 3, 7:25, :]
        return [
            (ap, (0, m, rows), ap[0, m, rows, :] + (centre - t0[m + 2, 7:25, :])),
            (ap, (1, m, rows), ap[1, m, rows, :] + (centre - t0[m + 3, 6:24, :])),
            (ap, (2, m, rows), ap[2, m, rows, :] + (centre - zdn(centre))),
        ]

    loop(0, BLOCK + 2, lift, 3)

    def finish(i):
        m = i + 1

        def around(ref):
            return (
                ref[m, 1:17, :],
                ref[m - 1, 1:17, :],
                ref[m + 1, 1:17, :],
                ref[m, 0:16, :],
                ref[m, 2:18, :],
            )

        speeds = [around(vp.at[c]) for c in range(3)]
        n0, nxm, nxp, nym, nyp = around(visp)
        fxm, fxp = 0.5 * (n0 + nxm), 0.5 * (nxp + n0)
        fym, fyp = 0.5 * (n0 + nym), 0.5 * (nyp + n0)
        fz = 0.5 * (n0 + zdn_copy(n0))
        u0m, u0p = speeds[0][1], speeds[0][2]
        u1m, u1p = speeds[1][3], speeds[1][4]
        u2 = speeds[2][0]

        def transport(q0, qxm, qxp, qym, qyp):
            up = u2 * q0
            return 0.5 * ((u0p * qxp - u0m * qxm) + (u1p * qyp - u1m * qym) + (zup(up) - zdn(up)))

        fields = around(np_)
        out_ndg[i] = fields[0] + DT * transport(*fields)
        gxm = gxp = gym = gyp = gz = 0.0
        for c in range(3):
            fields = around(ap.at[c])
            q0, qxm, qxp, qym, qyp = fields
            s0, sxm, sxp, sym, syp = speeds[c]
            dxm, dxp, dym, dyp = q0 - qxm, qxp - q0, q0 - qym, qyp - q0
            dz = q0 - zdn(q0)
            flux = fz * dz
            spread = (fxp * dxp - fxm * dxm) + (fyp * dyp - fym * dym) + (zup(flux) - flux)
            out_vel[c, i] = q0 + DT * (transport(*fields) + spread)
            gxm = gxm + dxm * (s0 - sxm)
            gxp = gxp + dxp * (sxp - s0)
            gym = gym + dym * (s0 - sym)
            gyp = gyp + dyp * (syp - s0)
            gz = gz + dz * (s0 - zdn(s0))
        bottom = jnp.where(layer(gz) == 0, gz, 0.0)
        out_vis[i] = (-0.5 * DT) * ((gxm + gxp) + (gym + gyp) + (gz + zup(gz)) + bottom)

    loop(0, BLOCK, finish, 2)


def shards(velocity, density, viscosity, grad_out, density_gradient):
    z = density.shape[2]
    size_x, size_y = lax.axis_size("gx"), lax.axis_size("gy")
    at_x = lax.axis_index("gx")
    odd = lax.rem(at_x, 2).astype(jnp.int32).reshape(1)
    even_pairs = [[i, i + 1] for i in range(0, size_x, 2)]
    odd_pairs = [[i, (i + 1) % size_x] for i in range(1, size_x, 2)]
    forward = [(i, (i + 1) % size_y) for i in range(size_y)]
    backward = [(j, i) for i, j in forward]

    def along_y(up, down):
        return lax.ppermute(up, "gy", forward), lax.ppermute(down, "gy", backward)

    fine = (32, 32, z)
    mid = (20, 24, z)
    low = (16, 16, z)
    rim = (BLOCK + 1, 24, z)
    rim2 = (16, 16, z)
    own = (BLOCK, BLOCK, z)
    fields = (velocity, viscosity, grad_out, density_gradient)
    single = [v[None] for v in (density, viscosity, density_gradient)]
    joined = jnp.concatenate([velocity, grad_out, *single], 0)
    up, down, b, d, planes = call(
        own_body,
        [rim, rim, own, own, (2, 4, 2 * BLOCK, z)],
        (joined,),
    )
    before, after = along_y(up, down)
    send = (19, 32, z)
    bb, dd, g0, even_send, odd_send = call(
        rows_body,
        [(BLOCK, 32, z), (BLOCK, 32, z), (32, z), send, send],
        (odd, b, d, down, planes, before, after),
        scalars=1,
    )
    even_got = lax.all_gather(even_send, "gx", axis_index_groups=even_pairs)
    odd_got = lax.all_gather(odd_send, "gx", axis_index_groups=odd_pairs)
    f1, b1, f2, b2, up, down, slots, kept0 = call(
        fine_body,
        [low, low, low, low, rim2, rim2, (size_y, 32, z), (8, 24, 32, z)],
        (odd, bb, dd, g0, even_got, odd_got),
        [(8, *fine), fine, fine, fine, (16, 32, z)]
        + [low] * 9
        + [(8, 16, z)]
        + [low] * 9
        + [(4, 16, z)]
        + [low, low, low, low, rim2, rim2, (size_y, 32, z)],
        scalars=1,
        kept=8,
        sems=9,
        megabytes=50,
    )
    got = lax.all_to_all(slots, "gy", 0, 0, tiled=True)
    before2, after2 = along_y(up, down)
    f1, b1, f2, b2, even_send, odd_strip = call(
        rows2_body,
        [mid, mid, low, low, (17, 32, z), (10, 32, z)],
        (odd, f1, b1, f2, b2, before2, after2, got),
        [low, low, low, low, rim2, rim2, (size_y, 32, z)],
        scalars=1,
        fetched=7,
        sems=7,
    )
    at_odd = lax.rem(at_x, 2)
    pair = lax.all_gather(even_send, "gx", axis_index_groups=even_pairs)
    side = lax.all_gather(pair[:, 0:7], "gx", axis_index_groups=odd_pairs)
    side = lax.dynamic_index_in_dim(side, at_odd, 0, keepdims=False)
    other = lax.all_gather(side, "gx", axis_index_groups=even_pairs)
    far = lax.dynamic_index_in_dim(other.reshape(4, 7, 32, z), 2 - at_odd, 0, keepdims=False)
    far = jnp.concatenate([far[0:6, 8:24].reshape(3, 32, z), odd_strip], 0)
    far = lax.all_gather(far, "gx", axis_index_groups=odd_pairs)
    level3 = (14, 32, z)
    slots, f1, b1, f2, b2, kept3 = call(
        level3_body,
        [(size_x, 2, 16, z), mid, mid, low, low, (8, *level3)],
        (odd, f1, b1, f2, b2, pair, other, far),
        [(8, *level3), level3, level3, level3, (1, 32, z), (2, 16, z)],
        scalars=1,
        kept=1,
        sems=1,
    )
    got = lax.all_to_all(slots, "gx", 0, 0, tiled=True)
    devices = 2 * WIN + 1
    return tuple(
        call(
            up_body,
            [(3, *own), own, own],
            (kept3, kept0, *fields, f1, b1, f2, b2, got, before, after, even_got, odd_got),
            [(8, *level3), (8, 24, 32, z), (3, *own), own, (3, *own), own, (8, *mid), (8, *low)]
            + [(devices, 16, z)] * 12
            + [(11, 32, z), level3, level3, level3]
            + [low, (10, 16, z), low, low]
            + [mid, (12, 24, z), mid, mid]
            + [(24, 32, z), (16, 32, z), (24, 32, z), (24, 32, z)]
            + [(3, 18, 24, z), (3, 18, 24, z), (18, 24, z), (18, 24, z)],
            megabytes=24,
            fetched=6,
            sems=6,
        )
    )


def solution(mesh):
    placed = (
        P(None, "gx", "gy", None),
        P("gx", "gy", None),
        P("gx", "gy", None),
        P(None, "gx", "gy", None),
        P("gx", "gy", None),
    )
    return jax.shard_map(
        shards,
        mesh=mesh,
        in_specs=placed,
        out_specs=(P(None, "gx", "gy", None), P("gx", "gy", None), P("gx", "gy", None)),
        check_vma=False,
    )
```

```python
import functools

import jax
import jax.numpy as jnp
from jax import lax
from jax.experimental import pallas as pl
from jax.experimental.pallas import tpu as pltpu
from jax.sharding import PartitionSpec as P

INTERPRET = False
DT = 0.2
MID = 1.2
HALF = 0.8
SIGMA = MID / HALF
RHO0 = 1.0 / SIGMA
RHO1 = 1.0 / (2.0 * SIGMA - RHO0)
A1 = RHO1 * RHO0
B1 = 2.0 * RHO1 / HALF
BLOCK = 16
PAD = 8
PAD1 = 6
U0, U1, U2 = 4, 4, 6
WIN = 8
F32 = jnp.float32


def call(body, out_shapes, args, scratch=(), scalars=0, megabytes=16, fetched=0, kept=0, sems=0):
    smem = [pl.BlockSpec(memory_space=pltpu.SMEM)] * scalars
    far = pl.BlockSpec(memory_space=pltpu.HBM)
    near = pl.BlockSpec(memory_space=pltpu.VMEM)
    scratch = [pltpu.VMEM(s, F32) for s in scratch]
    if sems:
        scratch.append(pltpu.SemaphoreType.DMA((sems,)))
    return pl.pallas_call(
        body,
        out_shape=[jax.ShapeDtypeStruct(s, F32) for s in out_shapes],
        in_specs=smem + [far] * fetched + [near] * (len(args) - scalars - fetched),
        out_specs=[near] * (len(out_shapes) - kept) + [far] * kept,
        scratch_shapes=scratch,
        compiler_params=pltpu.CompilerParams(vmem_limit_bytes=megabytes * 2**20),
        interpret=INTERPRET,
    )(*args)


def loop(low, high, step, unroll=1):
    def group(base, count):
        stores = []
        for u in range(count):
            stores.extend(step(base + u) or ())
        for ref, index, value in stores:
            ref[index] = value

    groups = (high - low) // unroll
    if groups == 1:
        group(low, unroll)
    elif groups > 1:
        lax.fori_loop(0, groups, lambda n, c: (group(low + n * unroll, unroll), c)[1], 0)
    rest = (high - low) - groups * unroll
    if rest:
        group(high - rest, rest)


def ydn(v):
    return pltpu.roll(v, 1, axis=0)


def yup(v):
    return pltpu.roll(v, v.shape[0] - 1, axis=0)


def layer(v):
    return lax.broadcasted_iota(jnp.int32, v.shape, 1)


def zroll_dn(v):
    return pltpu.roll(v, 1, axis=1)


def zroll_up(v):
    return pltpu.roll(v, v.shape[1] - 1, axis=1)


def zdn(v):
    return jnp.where(layer(v) == 0, 0.0, zroll_dn(v))


def zdn_copy(v):
    return jnp.where(layer(v) == 0, v, zroll_dn(v))


def zup(v):
    return jnp.where(layer(v) == v.shape[1] - 1, 0.0, zroll_up(v))


def setup(b, n, diag, low, high, scale, unroll, f=None, g=None, g_range=None):
    half = 0.5 * scale

    def step(i):
        b0 = b[i]
        fxm = half * (b0 + b[i - 1])
        fxp = half * (b[i + 1] + b0)
        fym = half * (b0 + ydn(b0))
        fyp = yup(fym)
        fz = 0.5 * (b0 + zdn_copy(b0))
        fzp = zup(fz)
        d = (fxm + fxp) + (fym + fyp) + (fz + fzp)
        inv = 1.0 / d
        fzm = jnp.where(layer(fz) == 0, 0.0, fz)
        out = [(ref, i, v * inv) for ref, v in zip(n, (fxm, fxp, fym, fyp, fzm, fzp), strict=True)]
        if diag is not None:
            out.append((diag, i, d))
        if f is not None:
            out.append((g, i, f[i] * inv))
        return out

    loop(low, high, step, unroll)


def around_sum(q, n, i, q0):
    total = (n[0][i] * q[i - 1] + n[1][i] * q[i + 1]) + (n[2][i] * ydn(q0) + n[3][i] * yup(q0))
    return total + (n[4][i] * zroll_dn(q0) + n[5][i] * zroll_up(q0))


def pre(g, x, n, low, high, unroll):
    first = (1.0 + A1) / MID + B1 * (1.0 - 1.0 / MID)

    def step(i):
        g0 = g[i]
        return [(x, i, first * g0 + (B1 / MID) * around_sum(g, n, i, g0))]

    loop(low, high, step, unroll)


def post(x, g, y, out, n, low, high, unroll):
    def first(i):
        x0 = x[i]
        return [(y, i, x0 + (1.0 / MID) * ((g[i] - x0) + around_sum(x, n, i, x0)))]

    loop(low - 1, high + 1, first, unroll)

    def second(i):
        y0 = y[i]
        z = (g[i] - y0) + around_sum(y, n, i, y0)
        return [(out, i, y0 + (A1 * (y0 - x[i]) + B1 * z))]

    loop(low, high, second, unroll)


def residual_pairs(g, x, diag, n, pairs, start, low, high, unroll):
    def one(i):
        x0 = x[i]
        return diag[i] * ((g[i] - x0) + around_sum(x, n, i, x0))

    def step(m):
        i = start + 2 * m
        return [(pairs, m, one(i) + one(i + 1))]

    loop(low, high, step, unroll)


def plane_pairs(b, pairs, start, low, high, unroll=4):
    def step(m):
        return [(pairs, m, b[start + 2 * m] + b[start + 2 * m + 1])]

    loop(low, high, step, unroll)


def row_pairs(pairs, coarse, low, high, row, count, target, shift=0, unroll=8):
    def step(m):
        even = pairs[m, pl.ds(row, count, 2), :]
        odd = pairs[m, pl.ds(row + 1, count, 2), :]
        return [(coarse, (m + shift, slice(target, target + count)), 0.25 * (even + odd))]

    loop(low, high, step, unroll)


def correct(x, coarse, wide, low, high, plane, row, count, target, unroll=4, out=None):
    def widen(m):
        v = coarse[m, row : row + count, :]
        return [
            (wide, (m, pl.ds(target, count, 2)), v),
            (wide, (m, pl.ds(target + 1, count, 2)), v),
        ]

    loop(low, high, widen, 2 * unroll)
    out = x if out is None else out

    def add(m):
        i = 2 * m + plane
        w = wide[m]
        return [(out, i, x[i] + w), (out, i + 1, x[i + 1] + w)]

    loop(low, high, add, unroll)


def own_body(joined, up, down, b, d, planes):
    vel, g = joined.at[0:3], joined.at[3:6]
    den, vis, ndg = joined.at[6], joined.at[7], joined.at[8]

    def invert(i):
        return [(b, i, 1.0 / den[i])]

    loop(0, BLOCK, invert, 8)
    edge = BLOCK - 1

    def step(i):
        b0 = b[i]
        fz = 0.5 * (b0 + zdn_copy(b0)) * g[2, i]
        fy = 0.5 * (b0 + ydn(b0)) * g[1, i]
        rows = lax.broadcasted_iota(jnp.int32, fy.shape, 0)
        fy = jnp.where(rows == 0, 0.0, fy)
        total = (zup(fz) - fz) + (yup(fy) - fy)
        left = jnp.maximum(i - 1, 0)
        right = jnp.minimum(i + 1, edge)
        inner = jnp.where(i > 0, 0.5, 0.0) * (b0 + b[left]) * g[0, i]
        outer = jnp.where(i < edge, 0.5, 0.0) * (b0 + b[right]) * g[0, right]
        total = total + (outer - inner)
        head, next_rows = slice(0, PAD), slice(PAD, 2 * PAD)
        out = [
            (d, i, total),
            (up, (i, head), b0[BLOCK - PAD :]),
            (up, (i, next_rows), total[BLOCK - PAD :]),
            (down, (i, head), b0[:PAD]),
            (down, (i, next_rows), total[:PAD]),
        ]
        for send, row in ((up, edge), (down, 0)):
            for c in range(3):
                out.append((send, (i, 16 + c), vel[c, i, row, :]))
                out.append((send, (i, 21 + c), g[c, i, row, :]))
            out.append((send, (i, 19), vis[i, row, :]))
            out.append((send, (i, 20), ndg[i, row, :]))
        return out

    loop(0, BLOCK, step, 4)
    z = b.shape[2]
    up[BLOCK] = jnp.zeros((24, z), F32)
    down[BLOCK] = jnp.zeros((24, z), F32)
    up[BLOCK, 0:PAD, :] = g[0, 0, BLOCK - PAD :, :]
    down[BLOCK, 0:PAD, :] = g[0, 0, :PAD, :]
    for n, plane in enumerate((0, edge)):
        for c in range(3):
            planes[n, c, 0:BLOCK, :] = vel[c, plane]
            planes[n, c, BLOCK : 2 * BLOCK, :] = g[c, plane]
        planes[n, 3, 0:BLOCK, :] = vis[plane]
        planes[n, 3, BLOCK : 2 * BLOCK, :] = ndg[plane]


def rows_body(odd, b, d, down, planes, before, after, bb, dd, g0, even_send, odd_send):
    top = PAD + BLOCK

    def step(i):
        own_flux = 0.5 * (b[i, 0:1, :] + before[i, PAD - 1 : PAD, :]) * down[i, 22:23, :]
        next_flux = 0.5 * (b[i, BLOCK - 1 : BLOCK, :] + after[i, 0:1, :]) * after[i, 22:23, :]
        out = []
        for ref, own, row in ((bb, b, 0), (dd, d, PAD)):
            out.append((ref, (i, slice(0, PAD)), before[i, row : row + PAD, :]))
            out.append((ref, (i, slice(PAD, top)), own[i]))
            out.append((ref, (i, slice(top, top + PAD)), after[i, row : row + PAD, :]))
        out.append((dd, (i, slice(PAD - 1, PAD)), before[i, 2 * PAD - 1 : 2 * PAD, :] + own_flux))
        out.append((dd, (i, slice(PAD, PAD + 1)), d[i, 0:1, :] - own_flux))
        out.append((dd, (i, slice(top - 1, top)), d[i, BLOCK - 1 : BLOCK, :] + next_flux))
        out.append((dd, (i, slice(top, top + 1)), after[i, PAD : PAD + 1, :] - next_flux))
        return out

    loop(0, BLOCK, step, 4)
    g0[0:PAD, :] = before[BLOCK, 0:PAD, :]
    g0[PAD:top, :] = planes[0, 0, BLOCK : 2 * BLOCK, :]
    g0[top : top + PAD, :] = after[BLOCK, 0:PAD, :]
    is_odd = odd[0]
    for send, last in ((even_send, 1 - is_odd), (odd_send, is_odd)):
        b_start = 8 * last
        d_start = 10 * last

        def b_step(m, send=send, b_start=b_start):
            return [(send, m, bb[b_start + m])]

        def d_step(m, send=send, d_start=d_start):
            return [(send, 8 + m, dd[d_start + m])]

        loop(0, 8, b_step, 8)
        loop(0, 6, d_step, 6)
        for c in range(4):
            send[14 + c] = planes[last, c]
        send[18] = g0[...]


def fine_body(
    odd, bb, dd, g0, even_got, odd_got,
    f1_out, b1_out, f2_out, b2_out, up_out, down_out, slots_out, kept,
    pack, b, f0, diag, pairs, g1, xb, *rest,
):
    n1, (diag1, pairs1) = rest[:6], rest[6:8]
    n2, (g2, x2, diag2, pairs2) = rest[8:14], rest[14:18]
    f1, b1, f2, b2, up, down, slots, sems = rest[18:]
    outs = ((f1, f1_out), (b1, b1_out), (up, up_out), (down, down_out))
    outs += ((f2, f2_out), (b2, b2_out), (slots, slots_out))
    moves = [pltpu.make_async_copy(a, b, sems.at[2 + n]) for n, (a, b) in enumerate(outs)]
    gf, x0 = pack.at[0], pack.at[7]
    n0 = tuple(pack.at[n] for n in range(1, 7))
    keep = slice(4, 28)
    saves = (
        pltpu.make_async_copy(pack.at[0:7, keep], kept.at[0:7], sems.at[0]),
        pltpu.make_async_copy(pack.at[7, keep], kept.at[7], sems.at[1]),
    )
    is_odd = odd[0] == 1
    top = PAD + BLOCK

    def left(m):
        return jnp.where(is_odd, even_got[0, m], odd_got[0, m])

    def right(m):
        return jnp.where(is_odd, odd_got[1, m], even_got[1, m])

    loop(0, BLOCK, lambda i: [(b, PAD + i, bb[i]), (f0, PAD + i, dd[i])], 4)
    loop(0, 8, lambda m: [(b, m, left(m)), (b, top + m, right(m))], 4)
    loop(0, 6, lambda m: [(f0, 2 + m, left(8 + m)), (f0, top + m, right(8 + m))], 6)
    flux = 0.5 * (b[PAD] + b[PAD - 1]) * g0[...]
    f0[PAD - 1] = f0[PAD - 1] + flux
    f0[PAD] = f0[PAD] - flux
    flux = 0.5 * (b[top] + b[top - 1]) * right(18)
    f0[top - 1] = f0[top - 1] + flux
    f0[top] = f0[top] - flux

    setup(b, n0, diag, 2, 30, 1.0, U0, f0, gf)
    saves[0].start()
    pre(gf, x0, n0, 3, 29, U0)
    saves[1].start()
    residual_pairs(gf, x0, diag, n0, pairs, 0, 2, 14, U0 // 2)
    row_pairs(pairs, f1, 2, 14, 0, 16, 0)
    plane_pairs(b, pairs, 0, 0, 16)
    row_pairs(pairs, b1, 0, 16, 0, 16, 0)

    z = b.shape[2]
    setup(b1, n1, diag1, 2, 14, 0.25, U2, f1, g1)
    pre(g1, xb, n1, 3, 13, U2)
    residual_pairs(g1, xb, diag1, n1, pairs1, 4, 0, 4, 4)
    f2[...] = jnp.zeros((16, 16, z), F32)
    b2[...] = jnp.ones((16, 16, z), F32)
    row_pairs(pairs1, f2, 0, 4, 4, 4, 6, shift=6)
    plane_pairs(b1, pairs1, 0, 0, 8)
    row_pairs(pairs1, b2, 0, 8, 0, 8, 4, shift=4)

    for send, brow, f1row, b1row in ((up, 4, 7, 6), (down, 6, 6, 8)):
        for m in range(4):
            send[m, 0:4, :] = f2[6 + m, 6:10, :]
        for m in range(8):
            send[m, 4:10, :] = b2[4 + m, brow : brow + 6, :]
        for m in range(2, 14):
            send[m, 10:13, :] = f1[m, f1row : f1row + 3, :]
        for m in range(16):
            send[m, 13:15, :] = b1[m, b1row : b1row + 2, :]
    for move in moves[:6]:
        move.start()
    x2[...] = jnp.zeros((16, 16, z), F32)
    setup(b2, n2, diag2, 4, 12, 0.25**2, 4, f2, g2)
    pre(g2, x2, n2, 5, 11, U2)
    residual_pairs(g2, x2, diag2, n2, pairs2, 4, 0, 4, 4)
    parts = []
    for m in range(4):
        even = pairs2[m, pl.ds(4, 4, 2), :]
        parts.append(0.25 * (even + pairs2[m, pl.ds(5, 4, 2), :]))
    plane_pairs(b2, pairs2, 6, 0, 2)
    for m in range(2):
        even = pairs2[m, pl.ds(6, 2, 2), :]
        parts.append(0.25 * (even + pairs2[m, pl.ds(7, 2, 2), :]))
    for n in range(4):
        slots[0, 4 * n : 4 * n + 4, :] = parts[n]
    slots[0, 16:18, :] = parts[4]
    slots[0, 18:20, :] = parts[5]
    for n in range(4):
        slots[0, 20 + n : 21 + n, :] = f2[6 + n, 6:7, :]
        slots[0, 24 + n : 25 + n, :] = f2[6 + n, 9:10, :]
    slots[0, 28:32, :] = jnp.zeros((4, z), F32)
    value = slots[0]
    for m in range(1, 16):
        slots[m] = value
    moves[6].start()
    for save in (*saves, *moves):
        save.wait()


def rows2_body(
    odd, f1_in, b1_in, f2_in, b2_in, before_in, after_in, got_in,
    g1, h1, g2, h2, even_send, odd_strip, f1, b1, f2, b2, before, after, got, sems,
):
    pairs = ((got_in, got), (f1_in, f1), (b1_in, b1), (f2_in, f2), (b2_in, b2))
    pairs += ((before_in, before), (after_in, after))
    moves = [pltpu.make_async_copy(a, b, sems.at[n]) for n, (a, b) in enumerate(pairs)]
    for move in moves:
        move.start()
    for move in moves:
        move.wait()
    z = g1.shape[2]
    g1[...] = jnp.zeros((20, 24, z), F32)
    h1[...] = jnp.ones((20, 24, z), F32)
    g2[...] = jnp.zeros((16, 16, z), F32)
    h2[...] = jnp.ones((16, 16, z), F32)
    at_y = lax.axis_index("gy")
    back, ahead = lax.rem(at_y + 14, 16), lax.rem(at_y + 2, 16)
    for m in range(4):
        g2[6 + m, 6:10, :] = f2[6 + m, 6:10, :]
        g2[6 + m, 2:6, :] = before[m, 0:4, :]
        g2[6 + m, 10:14, :] = after[m, 0:4, :]
        g2[6 + m, 1:2, :] = got[back, 24 + m : 25 + m, :]
        g2[6 + m, 14:15, :] = got[ahead, 20 + m : 21 + m, :]
    for m in range(8):
        h2[4 + m, 6:10, :] = b2[4 + m, 6:10, :]
        h2[4 + m, 0:6, :] = before[m, 4:10, :]
        h2[4 + m, 10:16, :] = after[m, 4:10, :]
    for m in range(2, 14):
        g1[2 + m, 4:16, :] = f1[m, 2:14, :]
        g1[2 + m, 1:4, :] = before[m, 10:13, :]
        g1[2 + m, 16:19, :] = after[m, 10:13, :]
    for m in range(16):
        h1[2 + m, 2:18, :] = b1[m]
        h1[2 + m, 0:2, :] = before[m, 13:15, :]
        h1[2 + m, 18:20, :] = after[m, 13:15, :]
    for p in range(16):
        here = lax.rem(at_y + (p + 8), 16)
        above = lax.rem(at_y + (p + 9), 16)
        below = lax.rem(at_y + (p + 7), 16)
        for n in range(4):
            k = 4 * n
            low = got[here, k + 1 : k + 2, :] + got[below, k + 3 : k + 4, :]
            high = got[here, k + 2 : k + 3, :] + got[above, k : k + 1, :]
            even_send[n, 2 * p : 2 * p + 1, :] = low
            even_send[n, 2 * p + 1 : 2 * p + 2, :] = high
        for n in range(2):
            even_send[4 + n, 2 * p : 2 * p + 2, :] = got[here, 16 + 2 * n : 18 + 2 * n, :]
    is_odd = odd[0]
    even_send[6, 0:16, :] = g2[6]
    even_send[6, 16:32, :] = g2[9]
    for send, first, last in ((even_send, 7, 1 - is_odd), (odd_strip, 0, is_odd)):
        for u in range(10):
            v = g2[6 + u] if u < 4 else h2[6 - 2 * last + (u - 4)]
            send[first + u // 2, (u % 2) * 16 : (u % 2) * 16 + 16, :] = v
        for n in range(5):
            v = g1[8 + last + n] if n < 3 else h1[10 - 2 * last + (n - 3)]
            send[first + 5 + n, 0:24, :] = v
            send[first + 5 + n, 24:32, :] = jnp.zeros((8, z), F32)


def level3_body(
    odd, f1i, b1i, f2i, b2i, pair, other, far, slots, f1, b1, f2, b2, kept,
    pack, f3, b3, diag, pairs, small, sems,
):
    g3, x3, n3 = pack.at[0], pack.at[7], tuple(pack.at[n] for n in range(1, 7))
    save = pltpu.make_async_copy(pack, kept, sems.at[0])
    is_odd = odd[0] == 1
    blocks = [(other, (0, 0)), (other, (0, 1)), (pair, (0,)), (pair, (1,))]
    blocks += [(other, (1, 0)), (other, (1, 1))]

    z = f3.shape[2]

    def distant(slot, k):
        rim = (jnp.zeros if k < 4 else jnp.ones)((8, z), F32)
        rows = slice((k % 2) * 16, (k % 2) * 16 + 16)
        return jnp.concatenate([rim, far[slot, k // 2, rows, :], rim], 0)

    def part(p, k):
        even = distant(0, k) if p == 0 else blocks[p - 1][0][(*blocks[p - 1][1], k)]
        odds = distant(1, k) if p == 6 else blocks[p][0][(*blocks[p][1], k)]
        return jnp.where(is_odd, odds, even)

    for p in range(7):
        low, high = part(p, 1), part(p, 2)
        f3[2 * p] = low + part(p - 1, 3) if p > 0 else low
        f3[2 * p + 1] = high + part(p + 1, 0) if p < 6 else high
        b3[2 * p] = part(p, 4)
        b3[2 * p + 1] = part(p, 5)
    setup(b3, n3, diag, 1, 13, 0.25**3, U0, f3, g3)
    pre(g3, x3, n3, 2, 12, 5)
    save.start()
    residual_pairs(g3, x3, diag, n3, pairs, 6, 0, 1, 1)
    row_pairs(pairs, small, 0, 1, 0, 16, 0)
    plane_pairs(b3, pairs, 6, 0, 1)
    row_pairs(pairs, small, 0, 1, 0, 16, 0, shift=1)

    def spread(m):
        return [(slots, (m, n), small[n]) for n in range(2)]

    loop(0, 32, spread, 4)

    def left(n, rows):
        return jnp.where(is_odd, pair[0, 7 + n, rows, :], far[0, 3 + n, rows, :])

    def right(n, rows):
        return jnp.where(is_odd, far[1, 3 + n, rows, :], pair[1, 7 + n, rows, :])

    f1[...] = f1i[...]
    b1[...] = b1i[...]
    f2[...] = f2i[...]
    b2[...] = b2i[...]
    for u in range(10):
        rows = slice((u % 2) * 16, (u % 2) * 16 + 16)
        if u < 4:
            f2[2 + u] = left(u // 2, rows)
            f2[10 + u] = right(u // 2, rows)
        else:
            b2[u - 4] = left(u // 2, rows)
            b2[u + 6] = right(u // 2, rows)
    f2[1] = part(1, 6)[16:32]
    f2[14] = part(5, 6)[0:16]
    rows = slice(0, 24)
    for n in range(3):
        f1[1 + n] = left(5 + n, rows)
        f1[16 + n] = right(5 + n, rows)
    for n in range(2):
        b1[n] = left(8 + n, rows)
        b1[18 + n] = right(8 + n, rows)
    save.wait()


def up_body(*refs):
    refs = list(refs)
    at_x = lax.axis_index("gx")

    def take(count):
        head = tuple(refs[:count])
        del refs[:count]
        return head

    kept = take(6)
    f1, b1, f2, b2, got, before, after, even_got, odd_got = take(9)
    out_vel, out_ndg, out_vis = take(3)
    held = take(6)
    pack3, pack0, vel, vis, g, ndg = held
    pack1, pack2 = take(2)
    f4, b4, g4, xa4, xb4, e4 = take(6)
    n4 = take(6)
    w3, v3, y3, t3, v2, w2, y2, t2, v1, w1, y1, t1, v0, w0, y0, t0 = take(16)
    vp, ap, visp, np_ = take(4)
    (sems,) = refs
    (g3, x3, n3), (g2, x2, n2), (g1, x1, n1), (g0, x0, n0) = (
        (pack.at[0], pack.at[7], tuple(pack.at[n] for n in range(1, 7)))
        for pack in (pack3, pack2, pack1, pack0)
    )
    loads = [
        pltpu.make_async_copy(source, target, sems.at[n])
        for n, (source, target) in enumerate(zip(kept, held, strict=True))
    ]
    for load in loads:
        load.start()
    devices = 2 * WIN + 1

    def gather(q):
        source = lax.rem(at_x + (q + 32 - WIN), 32)
        return [(f4, q, got[source, 0]), (b4, q, got[source, 1])]

    loop(0, devices, gather, devices)
    low, high = 1, devices - 1
    setup(b4, n4, None, low, high, 0.25**4, U2, f4, g4)

    def start(i):
        u = g4[i] * (1.0 / MID)
        return [(e4, i, u), (xa4, i, u)]

    loop(low, high, start, U2)
    ratio = RHO0
    x_now, x_next = xa4, xb4
    for _ in range(5):
        following = 1.0 / (2.0 * SIGMA - ratio)
        low, high = low + 1, high - 1

        def sweep(i, x_now=x_now, x_next=x_next, following=following, ratio=ratio):
            q0 = x_now[i]
            scaled = (g4[i] - q0) + around_sum(x_now, n4, i, q0)
            u = following * ratio * e4[i] + (2.0 * following / HALF) * scaled
            return [(e4, i, u), (x_next, i, q0 + u)]

        loop(low, high, sweep, U2)
        ratio = following
        x_now, x_next = x_next, x_now
    loads[0].wait()
    correct(x3, x_now, w3, 6, 11, -10, 0, 16, 0, out=v3)
    post(v3, g3, y3, t3, n3, 4, 10, U0)
    setup(b2, n2, None, 1, 15, 0.25**2, U2, f2, g2)
    pre(g2, x2, n2, 2, 14, U2)
    correct(x2, t3, w2, 4, 10, -6, 14, 6, 2, out=v2)
    post(v2, g2, y2, t2, n2, 4, 12, U2)
    setup(b1, n1, None, 1, 19, 0.25, U1, f1, g1)
    pre(g1, x1, n1, 2, 18, U1)
    correct(x1, t2, w1, 4, 12, -6, 4, 8, 2, out=v1)
    post(v1, g1, y1, t1, n1, 4, 16, U1)
    loads[1].wait()
    correct(x0, t1, w0, 4, 16, -8, 4, 12, 4, 2, out=v0)
    post(v0, g0, y0, t0, n0, 2, 21, U0)
    for load in loads[2:]:
        load.wait()

    def pad(i):
        def put(out, own, source, row):
            out[7:8, :] = before[source, row : row + 1, :]
            out[8:24, :] = own
            out[24:25, :] = after[source, row : row + 1, :]

        for c in range(3):
            put(vp.at[c, i + 1], vel[c, i], i, 16 + c)
            put(ap.at[c, i + 1], g[c, i], i, 21 + c)
        put(visp.at[i + 1], vis[i], i, 19)
        put(np_.at[i + 1], ndg[i], i, 20)

    loop(0, BLOCK, pad, 2)
    is_odd = lax.rem(at_x, 2) == 1

    def left(m):
        return jnp.where(is_odd, even_got[0, m], odd_got[0, m])

    def right(m):
        return jnp.where(is_odd, odd_got[1, m], even_got[1, m])

    for plane, side in ((0, left), (BLOCK + 1, right)):
        for c in range(3):
            both = side(14 + c)
            vp[c, plane, 8:24, :] = both[0:BLOCK]
            ap[c, plane, 8:24, :] = both[BLOCK : 2 * BLOCK]
        both = side(17)
        visp[plane, 8:24, :] = both[0:BLOCK]
        np_[plane, 8:24, :] = both[BLOCK : 2 * BLOCK]

    def lift(m):
        centre = t0[m + 3]
        return [
            (ap, (0, m), ap[0, m] + (centre - t0[m + 2])),
            (ap, (1, m), ap[1, m] + (centre - ydn(centre))),
            (ap, (2, m), ap[2, m] + (centre - zdn(centre))),
        ]

    loop(0, BLOCK + 2, lift, 3)

    def finish(i):
        m = i + 1

        def around(ref):
            return (
                ref[m, 8:24, :],
                ref[m - 1, 8:24, :],
                ref[m + 1, 8:24, :],
                ref[m, 7:23, :],
                ref[m, 9:25, :],
            )

        speeds = [around(vp.at[c]) for c in range(3)]
        n0, nxm, nxp, nym, nyp = around(visp)
        fxm, fxp = 0.5 * (n0 + nxm), 0.5 * (nxp + n0)
        fym, fyp = 0.5 * (n0 + nym), 0.5 * (nyp + n0)
        fz = 0.5 * (n0 + zdn_copy(n0))
        u0m, u0p = speeds[0][1], speeds[0][2]
        u1m, u1p = speeds[1][3], speeds[1][4]
        u2 = speeds[2][0]

        def transport(q0, qxm, qxp, qym, qyp):
            up = u2 * q0
            return 0.5 * ((u0p * qxp - u0m * qxm) + (u1p * qyp - u1m * qym) + (zup(up) - zdn(up)))

        fields = around(np_)
        out_ndg[i] = fields[0] + DT * transport(*fields)
        gxm = gxp = gym = gyp = gz = 0.0
        for c in range(3):
            fields = around(ap.at[c])
            q0, qxm, qxp, qym, qyp = fields
            s0, sxm, sxp, sym, syp = speeds[c]
            dxm, dxp, dym, dyp = q0 - qxm, qxp - q0, q0 - qym, qyp - q0
            dz = q0 - zdn(q0)
            flux = fz * dz
            spread = (fxp * dxp - fxm * dxm) + (fyp * dyp - fym * dym) + (zup(flux) - flux)
            out_vel[c, i] = q0 + DT * (transport(*fields) + spread)
            gxm = gxm + dxm * (s0 - sxm)
            gxp = gxp + dxp * (sxp - s0)
            gym = gym + dym * (s0 - sym)
            gyp = gyp + dyp * (syp - s0)
            gz = gz + dz * (s0 - zdn(s0))
        bottom = jnp.where(layer(gz) == 0, gz, 0.0)
        out_vis[i] = (-0.5 * DT) * ((gxm + gxp) + (gym + gyp) + (gz + zup(gz)) + bottom)

    loop(0, BLOCK, finish, 2)


def shards(velocity, density, viscosity, grad_out, density_gradient):
    z = density.shape[2]
    size_x, size_y = lax.axis_size("gx"), lax.axis_size("gy")
    at_x = lax.axis_index("gx")
    odd = lax.rem(at_x, 2).astype(jnp.int32).reshape(1)
    even_pairs = [[i, i + 1] for i in range(0, size_x, 2)]
    odd_pairs = [[i, (i + 1) % size_x] for i in range(1, size_x, 2)]
    forward = [(i, (i + 1) % size_y) for i in range(size_y)]
    backward = [(j, i) for i, j in forward]

    def along_y(up, down):
        return lax.ppermute(up, "gy", forward), lax.ppermute(down, "gy", backward)

    fine = (32, 32, z)
    mid = (20, 24, z)
    low = (16, 16, z)
    rim = (BLOCK + 1, 24, z)
    rim2 = (16, 16, z)
    own = (BLOCK, BLOCK, z)
    fields = (velocity, viscosity, grad_out, density_gradient)
    single = [v[None] for v in (density, viscosity, density_gradient)]
    joined = jnp.concatenate([velocity, grad_out, *single], 0)
    up, down, b, d, planes = call(
        own_body,
        [rim, rim, own, own, (2, 4, 2 * BLOCK, z)],
        (joined,),
    )
    before, after = along_y(up, down)
    send = (19, 32, z)
    bb, dd, g0, even_send, odd_send = call(
        rows_body,
        [(BLOCK, 32, z), (BLOCK, 32, z), (32, z), send, send],
        (odd, b, d, down, planes, before, after),
        scalars=1,
    )
    even_got = lax.all_gather(even_send, "gx", axis_index_groups=even_pairs)
    odd_got = lax.all_gather(odd_send, "gx", axis_index_groups=odd_pairs)
    f1, b1, f2, b2, up, down, slots, kept0 = call(
        fine_body,
        [low, low, low, low, rim2, rim2, (size_y, 32, z), (8, 24, 32, z)],
        (odd, bb, dd, g0, even_got, odd_got),
        [(8, *fine), fine, fine, fine, (16, 32, z)]
        + [low] * 9
        + [(8, 16, z)]
        + [low] * 9
        + [(4, 16, z)]
        + [low, low, low, low, rim2, rim2, (size_y, 32, z)],
        scalars=1,
        kept=8,
        sems=9,
        megabytes=50,
    )
    got = lax.all_to_all(slots, "gy", 0, 0, tiled=True)
    before2, after2 = along_y(up, down)
    f1, b1, f2, b2, even_send, odd_strip = call(
        rows2_body,
        [mid, mid, low, low, (17, 32, z), (10, 32, z)],
        (odd, f1, b1, f2, b2, before2, after2, got),
        [low, low, low, low, rim2, rim2, (size_y, 32, z)],
        scalars=1,
        fetched=7,
        sems=7,
    )
    at_odd = lax.rem(at_x, 2)
    pair = lax.all_gather(even_send, "gx", axis_index_groups=even_pairs)
    side = lax.all_gather(pair[:, 0:7], "gx", axis_index_groups=odd_pairs)
    side = lax.dynamic_index_in_dim(side, at_odd, 0, keepdims=False)
    other = lax.all_gather(side, "gx", axis_index_groups=even_pairs)
    far = lax.dynamic_index_in_dim(other.reshape(4, 7, 32, z), 2 - at_odd, 0, keepdims=False)
    far = jnp.concatenate([far[0:6, 8:24].reshape(3, 32, z), odd_strip], 0)
    far = lax.all_gather(far, "gx", axis_index_groups=odd_pairs)
    level3 = (14, 32, z)
    slots, f1, b1, f2, b2, kept3 = call(
        level3_body,
        [(size_x, 2, 16, z), mid, mid, low, low, (8, *level3)],
        (odd, f1, b1, f2, b2, pair, other, far),
        [(8, *level3), level3, level3, level3, (1, 32, z), (2, 16, z)],
        scalars=1,
        kept=1,
        sems=1,
    )
    got = lax.all_to_all(slots, "gx", 0, 0, tiled=True)
    devices = 2 * WIN + 1
    return tuple(
        call(
            up_body,
            [(3, *own), own, own],
            (kept3, kept0, *fields, f1, b1, f2, b2, got, before, after, even_got, odd_got),
            [(8, *level3), (8, 24, 32, z), (3, *own), own, (3, *own), own, (8, *mid), (8, *low)]
            + [(devices, 16, z)] * 12
            + [(11, 32, z), level3, level3, level3]
            + [low, (10, 16, z), low, low]
            + [mid, (12, 24, z), mid, mid]
            + [(24, 32, z), (16, 32, z), (24, 32, z), (24, 32, z)]
            + [(3, 18, 32, z), (3, 18, 32, z), (18, 32, z), (18, 32, z)],
            megabytes=24,
            fetched=6,
            sems=6,
        )
    )


def solution(mesh):
    placed = (
        P(None, "gx", "gy", None),
        P("gx", "gy", None),
        P("gx", "gy", None),
        P(None, "gx", "gy", None),
        P("gx", "gy", None),
    )
    return jax.shard_map(
        shards,
        mesh=mesh,
        in_specs=placed,
        out_specs=(P(None, "gx", "gy", None), P("gx", "gy", None), P("gx", "gy", None)),
        check_vma=False,
    )
```

```python
import functools

import jax
import jax.numpy as jnp
from jax import lax
from jax.experimental import pallas as pl
from jax.experimental.pallas import tpu as pltpu
from jax.sharding import PartitionSpec as P

INTERPRET = False
DT = 0.2
MID = 1.2
HALF = 0.8
SIGMA = MID / HALF
RHO0 = 1.0 / SIGMA
RHO1 = 1.0 / (2.0 * SIGMA - RHO0)
A1 = RHO1 * RHO0
B1 = 2.0 * RHO1 / HALF
BLOCK = 16
PAD = 8
PAD1 = 6
U0, U1, U2 = 4, 4, 6
WIN = 8
F32 = jnp.float32


def call(body, out_shapes, args, scratch=(), scalars=0, megabytes=16, fetched=0, kept=0, sems=0):
    smem = [pl.BlockSpec(memory_space=pltpu.SMEM)] * scalars
    far = pl.BlockSpec(memory_space=pltpu.HBM)
    near = pl.BlockSpec(memory_space=pltpu.VMEM)
    scratch = [pltpu.VMEM(s, F32) for s in scratch]
    if sems:
        scratch.append(pltpu.SemaphoreType.DMA((sems,)))
    return pl.pallas_call(
        body,
        out_shape=[jax.ShapeDtypeStruct(s, F32) for s in out_shapes],
        in_specs=smem + [far] * fetched + [near] * (len(args) - scalars - fetched),
        out_specs=[near] * (len(out_shapes) - kept) + [far] * kept,
        scratch_shapes=scratch,
        compiler_params=pltpu.CompilerParams(vmem_limit_bytes=megabytes * 2**20),
        interpret=INTERPRET,
    )(*args)


def loop(low, high, step, unroll=1):
    def group(base, count):
        stores = []
        for u in range(count):
            stores.extend(step(base + u) or ())
        for ref, index, value in stores:
            ref[index] = value

    groups = (high - low) // unroll
    if groups == 1:
        group(low, unroll)
    elif groups > 1:
        lax.fori_loop(0, groups, lambda n, c: (group(low + n * unroll, unroll), c)[1], 0)
    rest = (high - low) - groups * unroll
    if rest:
        group(high - rest, rest)


def ydn(v):
    return pltpu.roll(v, 1, axis=0)


def yup(v):
    return pltpu.roll(v, v.shape[0] - 1, axis=0)


def layer(v):
    return lax.broadcasted_iota(jnp.int32, v.shape, 1)


def zroll_dn(v):
    return pltpu.roll(v, 1, axis=1)


def zroll_up(v):
    return pltpu.roll(v, v.shape[1] - 1, axis=1)


def zdn(v):
    return jnp.where(layer(v) == 0, 0.0, zroll_dn(v))


def zdn_copy(v):
    return jnp.where(layer(v) == 0, v, zroll_dn(v))


def zup(v):
    return jnp.where(layer(v) == v.shape[1] - 1, 0.0, zroll_up(v))


def setup(b, n, diag, low, high, scale, unroll, f=None, g=None, g_range=None):
    half = 0.5 * scale

    def step(i):
        b0 = b[i]
        fxm = half * (b0 + b[i - 1])
        fxp = half * (b[i + 1] + b0)
        fym = half * (b0 + ydn(b0))
        fyp = yup(fym)
        fz = 0.5 * (b0 + zdn_copy(b0))
        fzp = zup(fz)
        d = (fxm + fxp) + (fym + fyp) + (fz + fzp)
        inv = 1.0 / d
        fzm = jnp.where(layer(fz) == 0, 0.0, fz)
        out = [(ref, i, v * inv) for ref, v in zip(n, (fxm, fxp, fym, fyp, fzm, fzp), strict=True)]
        if diag is not None:
            out.append((diag, i, d))
        if f is not None:
            out.append((g, i, f[i] * inv))
        return out

    loop(low, high, step, unroll)


def around_sum(q, n, i, q0):
    total = (n[0][i] * q[i - 1] + n[1][i] * q[i + 1]) + (n[2][i] * ydn(q0) + n[3][i] * yup(q0))
    return total + (n[4][i] * zroll_dn(q0) + n[5][i] * zroll_up(q0))


def pre(g, x, n, low, high, unroll):
    first = (1.0 + A1) / MID + B1 * (1.0 - 1.0 / MID)

    def step(i):
        g0 = g[i]
        return [(x, i, first * g0 + (B1 / MID) * around_sum(g, n, i, g0))]

    loop(low, high, step, unroll)


def post(x, g, y, out, n, low, high, unroll):
    def first(i):
        x0 = x[i]
        return [(y, i, x0 + (1.0 / MID) * ((g[i] - x0) + around_sum(x, n, i, x0)))]

    loop(low - 1, high + 1, first, unroll)

    def second(i):
        y0 = y[i]
        z = (g[i] - y0) + around_sum(y, n, i, y0)
        return [(out, i, y0 + (A1 * (y0 - x[i]) + B1 * z))]

    loop(low, high, second, unroll)


def residual_pairs(g, x, diag, n, pairs, start, low, high, unroll):
    def one(i):
        x0 = x[i]
        return diag[i] * ((g[i] - x0) + around_sum(x, n, i, x0))

    def step(m):
        i = start + 2 * m
        return [(pairs, m, one(i) + one(i + 1))]

    loop(low, high, step, unroll)


def plane_pairs(b, pairs, start, low, high, unroll=4):
    def step(m):
        return [(pairs, m, b[start + 2 * m] + b[start + 2 * m + 1])]

    loop(low, high, step, unroll)


def row_pairs(pairs, coarse, low, high, row, count, target, shift=0, unroll=8):
    def step(m):
        even = pairs[m, pl.ds(row, count, 2), :]
        odd = pairs[m, pl.ds(row + 1, count, 2), :]
        return [(coarse, (m + shift, slice(target, target + count)), 0.25 * (even + odd))]

    loop(low, high, step, unroll)


def correct(x, coarse, wide, low, high, plane, row, count, target, unroll=4, out=None):
    def widen(m):
        v = coarse[m, row : row + count, :]
        return [
            (wide, (m, pl.ds(target, count, 2)), v),
            (wide, (m, pl.ds(target + 1, count, 2)), v),
        ]

    loop(low, high, widen, 2 * unroll)
    out = x if out is None else out

    def add(m):
        i = 2 * m + plane
        w = wide[m]
        return [(out, i, x[i] + w), (out, i + 1, x[i + 1] + w)]

    loop(low, high, add, unroll)


def own_body(joined, up, down, b, d, planes):
    vel, g = joined.at[0:3], joined.at[3:6]
    den, vis, ndg = joined.at[6], joined.at[7], joined.at[8]

    def invert(i):
        return [(b, i, 1.0 / den[i])]

    loop(0, BLOCK, invert, 8)
    edge = BLOCK - 1

    def step(i):
        b0 = b[i]
        fz = 0.5 * (b0 + zdn_copy(b0)) * g[2, i]
        fy = 0.5 * (b0 + ydn(b0)) * g[1, i]
        rows = lax.broadcasted_iota(jnp.int32, fy.shape, 0)
        fy = jnp.where(rows == 0, 0.0, fy)
        total = (zup(fz) - fz) + (yup(fy) - fy)
        left = jnp.maximum(i - 1, 0)
        right = jnp.minimum(i + 1, edge)
        inner = jnp.where(i > 0, 0.5, 0.0) * (b0 + b[left]) * g[0, i]
        outer = jnp.where(i < edge, 0.5, 0.0) * (b0 + b[right]) * g[0, right]
        total = total + (outer - inner)
        head, next_rows = slice(0, PAD), slice(PAD, 2 * PAD)
        out = [
            (d, i, total),
            (up, (i, head), b0[BLOCK - PAD :]),
            (up, (i, next_rows), total[BLOCK - PAD :]),
            (down, (i, head), b0[:PAD]),
            (down, (i, next_rows), total[:PAD]),
        ]
        for send, row in ((up, edge), (down, 0)):
            for c in range(3):
                out.append((send, (i, 16 + c), vel[c, i, row, :]))
                out.append((send, (i, 21 + c), g[c, i, row, :]))
            out.append((send, (i, 19), vis[i, row, :]))
            out.append((send, (i, 20), ndg[i, row, :]))
        return out

    loop(0, BLOCK, step, 4)
    z = b.shape[2]
    up[BLOCK] = jnp.zeros((24, z), F32)
    down[BLOCK] = jnp.zeros((24, z), F32)
    up[BLOCK, 0:PAD, :] = g[0, 0, BLOCK - PAD :, :]
    down[BLOCK, 0:PAD, :] = g[0, 0, :PAD, :]
    for n, plane in enumerate((0, edge)):
        for c in range(3):
            planes[n, c, 0:BLOCK, :] = vel[c, plane]
            planes[n, c, BLOCK : 2 * BLOCK, :] = g[c, plane]
        planes[n, 3, 0:BLOCK, :] = vis[plane]
        planes[n, 3, BLOCK : 2 * BLOCK, :] = ndg[plane]


def rows_body(odd, b, d, down, planes, before, after, bb, dd, g0, even_send, odd_send):
    top = PAD + BLOCK

    def step(i):
        own_flux = 0.5 * (b[i, 0:1, :] + before[i, PAD - 1 : PAD, :]) * down[i, 22:23, :]
        next_flux = 0.5 * (b[i, BLOCK - 1 : BLOCK, :] + after[i, 0:1, :]) * after[i, 22:23, :]
        out = []
        for ref, own, row in ((bb, b, 0), (dd, d, PAD)):
            out.append((ref, (i, slice(0, PAD)), before[i, row : row + PAD, :]))
            out.append((ref, (i, slice(PAD, top)), own[i]))
            out.append((ref, (i, slice(top, top + PAD)), after[i, row : row + PAD, :]))
        out.append((dd, (i, slice(PAD - 1, PAD)), before[i, 2 * PAD - 1 : 2 * PAD, :] + own_flux))
        out.append((dd, (i, slice(PAD, PAD + 1)), d[i, 0:1, :] - own_flux))
        out.append((dd, (i, slice(top - 1, top)), d[i, BLOCK - 1 : BLOCK, :] + next_flux))
        out.append((dd, (i, slice(top, top + 1)), after[i, PAD : PAD + 1, :] - next_flux))
        return out

    loop(0, BLOCK, step, 4)
    g0[0:PAD, :] = before[BLOCK, 0:PAD, :]
    g0[PAD:top, :] = planes[0, 0, BLOCK : 2 * BLOCK, :]
    g0[top : top + PAD, :] = after[BLOCK, 0:PAD, :]
    is_odd = odd[0]
    for send, last in ((even_send, 1 - is_odd), (odd_send, is_odd)):
        b_start = 8 * last
        d_start = 10 * last

        def b_step(m, send=send, b_start=b_start):
            return [(send, m, bb[b_start + m])]

        def d_step(m, send=send, d_start=d_start):
            return [(send, 8 + m, dd[d_start + m])]

        loop(0, 8, b_step, 8)
        loop(0, 6, d_step, 6)
        for c in range(4):
            send[14 + c] = planes[last, c]
        send[18] = g0[...]


def fine_body(
    odd, bb, dd, g0, even_got, odd_got,
    f1_out, b1_out, f2_out, b2_out, up_out, down_out, slots_out, kept,
    pack, b, f0, diag, pairs, g1, xb, *rest,
):
    n1, (diag1, pairs1) = rest[:6], rest[6:8]
    n2, (g2, x2, diag2, pairs2) = rest[8:14], rest[14:18]
    f1, b1, f2, b2, up, down, slots, sems = rest[18:]
    outs = ((f1, f1_out), (b1, b1_out), (up, up_out), (down, down_out))
    outs += ((f2, f2_out), (b2, b2_out), (slots, slots_out))
    moves = [pltpu.make_async_copy(a, b, sems.at[2 + n]) for n, (a, b) in enumerate(outs)]
    gf, x0 = pack.at[0], pack.at[7]
    n0 = tuple(pack.at[n] for n in range(1, 7))
    keep = slice(4, 28)
    saves = (
        pltpu.make_async_copy(pack.at[0:7, keep], kept.at[0:7], sems.at[0]),
        pltpu.make_async_copy(pack.at[7, keep], kept.at[7], sems.at[1]),
    )
    is_odd = odd[0] == 1
    top = PAD + BLOCK

    def left(m):
        return jnp.where(is_odd, even_got[0, m], odd_got[0, m])

    def right(m):
        return jnp.where(is_odd, odd_got[1, m], even_got[1, m])

    loop(0, BLOCK, lambda i: [(b, PAD + i, bb[i]), (f0, PAD + i, dd[i])], 4)
    loop(0, 8, lambda m: [(b, m, left(m)), (b, top + m, right(m))], 4)
    loop(0, 6, lambda m: [(f0, 2 + m, left(8 + m)), (f0, top + m, right(8 + m))], 6)
    flux = 0.5 * (b[PAD] + b[PAD - 1]) * g0[...]
    f0[PAD - 1] = f0[PAD - 1] + flux
    f0[PAD] = f0[PAD] - flux
    flux = 0.5 * (b[top] + b[top - 1]) * right(18)
    f0[top - 1] = f0[top - 1] + flux
    f0[top] = f0[top] - flux

    setup(b, n0, diag, 2, 30, 1.0, U0, f0, gf)
    saves[0].start()
    pre(gf, x0, n0, 3, 29, U0)
    saves[1].start()
    residual_pairs(gf, x0, diag, n0, pairs, 0, 2, 14, U0 // 2)
    row_pairs(pairs, f1, 2, 14, 0, 16, 0)
    plane_pairs(b, pairs, 0, 0, 16)
    row_pairs(pairs, b1, 0, 16, 0, 16, 0)

    z = b.shape[2]
    setup(b1, n1, diag1, 2, 14, 0.25, U2, f1, g1)
    pre(g1, xb, n1, 3, 13, U2)
    residual_pairs(g1, xb, diag1, n1, pairs1, 4, 0, 4, 4)
    f2[...] = jnp.zeros((16, 16, z), F32)
    b2[...] = jnp.ones((16, 16, z), F32)
    row_pairs(pairs1, f2, 0, 4, 4, 4, 6, shift=6)
    plane_pairs(b1, pairs1, 0, 0, 8)
    row_pairs(pairs1, b2, 0, 8, 0, 8, 4, shift=4)

    for send, brow, f1row, b1row in ((up, 4, 7, 6), (down, 6, 6, 8)):
        for m in range(4):
            send[m, 0:4, :] = f2[6 + m, 6:10, :]
        for m in range(8):
            send[m, 4:10, :] = b2[4 + m, brow : brow + 6, :]
        for m in range(2, 14):
            send[m, 10:13, :] = f1[m, f1row : f1row + 3, :]
        for m in range(16):
            send[m, 13:15, :] = b1[m, b1row : b1row + 2, :]
    for move in moves[:6]:
        move.start()
    x2[...] = jnp.zeros((16, 16, z), F32)
    setup(b2, n2, diag2, 4, 12, 0.25**2, 4, f2, g2)
    pre(g2, x2, n2, 5, 11, U2)
    residual_pairs(g2, x2, diag2, n2, pairs2, 4, 0, 4, 4)
    parts = []
    for m in range(4):
        even = pairs2[m, pl.ds(4, 4, 2), :]
        parts.append(0.25 * (even + pairs2[m, pl.ds(5, 4, 2), :]))
    plane_pairs(b2, pairs2, 6, 0, 2)
    for m in range(2):
        even = pairs2[m, pl.ds(6, 2, 2), :]
        parts.append(0.25 * (even + pairs2[m, pl.ds(7, 2, 2), :]))
    for n in range(4):
        slots[0, 4 * n : 4 * n + 4, :] = parts[n]
    slots[0, 16:18, :] = parts[4]
    slots[0, 18:20, :] = parts[5]
    for n in range(4):
        slots[0, 20 + n : 21 + n, :] = f2[6 + n, 6:7, :]
    value = slots[0]
    for m in range(1, 16):
        slots[m] = value
    ahead = lax.rem(lax.axis_index("gy") + 2, 16)
    for n in range(4):
        slots[ahead, 20 + n : 21 + n, :] = f2[6 + n, 9:10, :]
    moves[6].start()
    for save in (*saves, *moves):
        save.wait()


def rows2_body(
    odd, f1_in, b1_in, f2_in, b2_in, before_in, after_in, got_in,
    g1, h1, g2, h2, even_send, odd_strip, f1, b1, f2, b2, before, after, got, sems,
):
    pairs = ((got_in, got), (f1_in, f1), (b1_in, b1), (f2_in, f2), (b2_in, b2))
    pairs += ((before_in, before), (after_in, after))
    moves = [pltpu.make_async_copy(a, b, sems.at[n]) for n, (a, b) in enumerate(pairs)]
    for move in moves:
        move.start()
    for move in moves:
        move.wait()
    z = g1.shape[2]
    g1[...] = jnp.zeros((20, 24, z), F32)
    h1[...] = jnp.ones((20, 24, z), F32)
    g2[...] = jnp.zeros((16, 16, z), F32)
    h2[...] = jnp.ones((16, 16, z), F32)
    at_y = lax.axis_index("gy")
    back, ahead = lax.rem(at_y + 14, 16), lax.rem(at_y + 2, 16)
    for m in range(4):
        g2[6 + m, 6:10, :] = f2[6 + m, 6:10, :]
        g2[6 + m, 2:6, :] = before[m, 0:4, :]
        g2[6 + m, 10:14, :] = after[m, 0:4, :]
        g2[6 + m, 1:2, :] = got[back, 20 + m : 21 + m, :]
        g2[6 + m, 14:15, :] = got[ahead, 20 + m : 21 + m, :]
    for m in range(8):
        h2[4 + m, 6:10, :] = b2[4 + m, 6:10, :]
        h2[4 + m, 0:6, :] = before[m, 4:10, :]
        h2[4 + m, 10:16, :] = after[m, 4:10, :]
    for m in range(2, 14):
        g1[2 + m, 4:16, :] = f1[m, 2:14, :]
        g1[2 + m, 1:4, :] = before[m, 10:13, :]
        g1[2 + m, 16:19, :] = after[m, 10:13, :]
    for m in range(16):
        h1[2 + m, 2:18, :] = b1[m]
        h1[2 + m, 0:2, :] = before[m, 13:15, :]
        h1[2 + m, 18:20, :] = after[m, 13:15, :]
    for p in range(16):
        here = lax.rem(at_y + (p + 8), 16)
        above = lax.rem(at_y + (p + 9), 16)
        below = lax.rem(at_y + (p + 7), 16)
        for n in range(4):
            k = 4 * n
            low = got[here, k + 1 : k + 2, :] + got[below, k + 3 : k + 4, :]
            high = got[here, k + 2 : k + 3, :] + got[above, k : k + 1, :]
            even_send[n, 2 * p : 2 * p + 1, :] = low
            even_send[n, 2 * p + 1 : 2 * p + 2, :] = high
        for n in range(2):
            even_send[4 + n, 2 * p : 2 * p + 2, :] = got[here, 16 + 2 * n : 18 + 2 * n, :]
    is_odd = odd[0]
    even_send[6, 0:16, :] = g2[6]
    even_send[6, 16:32, :] = g2[9]
    for send, first, last in ((even_send, 7, 1 - is_odd), (odd_strip, 0, is_odd)):
        for u in range(10):
            v = g2[6 + u] if u < 4 else h2[6 - 2 * last + (u - 4)]
            send[first + u // 2, (u % 2) * 16 : (u % 2) * 16 + 16, :] = v
        for n in range(5):
            v = g1[8 + last + n] if n < 3 else h1[10 - 2 * last + (n - 3)]
            send[first + 5 + n, 0:24, :] = v
            send[first + 5 + n, 24:32, :] = jnp.zeros((8, z), F32)


def level3_body(
    odd, f1i, b1i, f2i, b2i, pair, other, far, slots, f1, b1, f2, b2, kept,
    pack, f3, b3, diag, pairs, small, sems,
):
    g3, x3, n3 = pack.at[0], pack.at[7], tuple(pack.at[n] for n in range(1, 7))
    save = pltpu.make_async_copy(pack, kept, sems.at[0])
    is_odd = odd[0] == 1
    blocks = [(other, (0, 0)), (other, (0, 1)), (pair, (0,)), (pair, (1,))]
    blocks += [(other, (1, 0)), (other, (1, 1))]

    z = f3.shape[2]

    def distant(slot, k):
        rim = (jnp.zeros if k < 4 else jnp.ones)((8, z), F32)
        rows = slice((k % 2) * 16, (k % 2) * 16 + 16)
        return jnp.concatenate([rim, far[slot, k // 2, rows, :], rim], 0)

    def part(p, k):
        even = distant(0, k) if p == 0 else blocks[p - 1][0][(*blocks[p - 1][1], k)]
        odds = distant(1, k) if p == 6 else blocks[p][0][(*blocks[p][1], k)]
        return jnp.where(is_odd, odds, even)

    for p in range(7):
        low, high = part(p, 1), part(p, 2)
        f3[2 * p] = low + part(p - 1, 3) if p > 0 else low
        f3[2 * p + 1] = high + part(p + 1, 0) if p < 6 else high
        b3[2 * p] = part(p, 4)
        b3[2 * p + 1] = part(p, 5)
    setup(b3, n3, diag, 1, 13, 0.25**3, U0, f3, g3)
    pre(g3, x3, n3, 2, 12, 5)
    save.start()
    residual_pairs(g3, x3, diag, n3, pairs, 6, 0, 1, 1)
    row_pairs(pairs, small, 0, 1, 0, 16, 0)
    plane_pairs(b3, pairs, 6, 0, 1)
    row_pairs(pairs, small, 0, 1, 0, 16, 0, shift=1)

    def spread(m):
        return [(slots, (m, n), small[n]) for n in range(2)]

    loop(0, 32, spread, 4)

    def left(n, rows):
        return jnp.where(is_odd, pair[0, 7 + n, rows, :], far[0, 3 + n, rows, :])

    def right(n, rows):
        return jnp.where(is_odd, far[1, 3 + n, rows, :], pair[1, 7 + n, rows, :])

    f1[...] = f1i[...]
    b1[...] = b1i[...]
    f2[...] = f2i[...]
    b2[...] = b2i[...]
    for u in range(10):
        rows = slice((u % 2) * 16, (u % 2) * 16 + 16)
        if u < 4:
            f2[2 + u] = left(u // 2, rows)
            f2[10 + u] = right(u // 2, rows)
        else:
            b2[u - 4] = left(u // 2, rows)
            b2[u + 6] = right(u // 2, rows)
    f2[1] = part(1, 6)[16:32]
    f2[14] = part(5, 6)[0:16]
    rows = slice(0, 24)
    for n in range(3):
        f1[1 + n] = left(5 + n, rows)
        f1[16 + n] = right(5 + n, rows)
    for n in range(2):
        b1[n] = left(8 + n, rows)
        b1[18 + n] = right(8 + n, rows)
    save.wait()


def up_body(*refs):
    refs = list(refs)
    at_x = lax.axis_index("gx")

    def take(count):
        head = tuple(refs[:count])
        del refs[:count]
        return head

    kept = take(6)
    f1, b1, f2, b2, got, before, after, even_got, odd_got = take(9)
    out_vel, out_ndg, out_vis = take(3)
    held = take(6)
    pack3, pack0, vel, vis, g, ndg = held
    pack1, pack2 = take(2)
    f4, b4, g4, xa4, xb4, e4 = take(6)
    n4 = take(6)
    w3, v3, y3, t3, v2, w2, y2, t2, v1, w1, y1, t1, v0, w0, y0, t0 = take(16)
    vp, ap, visp, np_ = take(4)
    (sems,) = refs
    (g3, x3, n3), (g2, x2, n2), (g1, x1, n1), (g0, x0, n0) = (
        (pack.at[0], pack.at[7], tuple(pack.at[n] for n in range(1, 7)))
        for pack in (pack3, pack2, pack1, pack0)
    )
    loads = [
        pltpu.make_async_copy(source, target, sems.at[n])
        for n, (source, target) in enumerate(zip(kept, held, strict=True))
    ]
    for load in loads:
        load.start()
    devices = 2 * WIN + 1

    def gather(q):
        source = lax.rem(at_x + (q + 32 - WIN), 32)
        return [(f4, q, got[source, 0]), (b4, q, got[source, 1])]

    loop(0, devices, gather, devices)
    low, high = 1, devices - 1
    setup(b4, n4, None, low, high, 0.25**4, U2, f4, g4)

    def start(i):
        u = g4[i] * (1.0 / MID)
        return [(e4, i, u), (xa4, i, u)]

    loop(low, high, start, U2)
    ratio = RHO0
    x_now, x_next = xa4, xb4
    for _ in range(5):
        following = 1.0 / (2.0 * SIGMA - ratio)
        low, high = low + 1, high - 1

        def sweep(i, x_now=x_now, x_next=x_next, following=following, ratio=ratio):
            q0 = x_now[i]
            scaled = (g4[i] - q0) + around_sum(x_now, n4, i, q0)
            u = following * ratio * e4[i] + (2.0 * following / HALF) * scaled
            return [(e4, i, u), (x_next, i, q0 + u)]

        loop(low, high, sweep, U2)
        ratio = following
        x_now, x_next = x_next, x_now
    loads[0].wait()
    correct(x3, x_now, w3, 6, 11, -10, 0, 16, 0, out=v3)
    post(v3, g3, y3, t3, n3, 4, 10, U0)
    setup(b2, n2, None, 1, 15, 0.25**2, U2, f2, g2)
    pre(g2, x2, n2, 2, 14, U2)
    correct(x2, t3, w2, 4, 10, -6, 14, 6, 2, out=v2)
    post(v2, g2, y2, t2, n2, 4, 12, U2)
    setup(b1, n1, None, 1, 19, 0.25, U1, f1, g1)
    pre(g1, x1, n1, 2, 18, U1)
    correct(x1, t2, w1, 4, 12, -6, 4, 8, 2, out=v1)
    post(v1, g1, y1, t1, n1, 4, 16, U1)
    loads[1].wait()
    correct(x0, t1, w0, 4, 16, -8, 4, 12, 4, 2, out=v0)
    post(v0, g0, y0, t0, n0, 2, 21, U0)
    for load in loads[2:]:
        load.wait()

    def pad(i):
        def put(out, own, source, row):
            out[7:8, :] = before[source, row : row + 1, :]
            out[8:24, :] = own
            out[24:25, :] = after[source, row : row + 1, :]

        for c in range(3):
            put(vp.at[c, i + 1], vel[c, i], i, 16 + c)
            put(ap.at[c, i + 1], g[c, i], i, 21 + c)
        put(visp.at[i + 1], vis[i], i, 19)
        put(np_.at[i + 1], ndg[i], i, 20)

    loop(0, BLOCK, pad, 2)
    is_odd = lax.rem(at_x, 2) == 1

    def left(m):
        return jnp.where(is_odd, even_got[0, m], odd_got[0, m])

    def right(m):
        return jnp.where(is_odd, odd_got[1, m], even_got[1, m])

    for plane, side in ((0, left), (BLOCK + 1, right)):
        for c in range(3):
            both = side(14 + c)
            vp[c, plane, 8:24, :] = both[0:BLOCK]
            ap[c, plane, 8:24, :] = both[BLOCK : 2 * BLOCK]
        both = side(17)
        visp[plane, 8:24, :] = both[0:BLOCK]
        np_[plane, 8:24, :] = both[BLOCK : 2 * BLOCK]

    def lift(m):
        centre = t0[m + 3]
        return [
            (ap, (0, m), ap[0, m] + (centre - t0[m + 2])),
            (ap, (1, m), ap[1, m] + (centre - ydn(centre))),
            (ap, (2, m), ap[2, m] + (centre - zdn(centre))),
        ]

    loop(0, BLOCK + 2, lift, 3)

    def finish(i):
        m = i + 1

        def around(ref):
            return (
                ref[m, 8:24, :],
                ref[m - 1, 8:24, :],
                ref[m + 1, 8:24, :],
                ref[m, 7:23, :],
                ref[m, 9:25, :],
            )

        speeds = [around(vp.at[c]) for c in range(3)]
        n0, nxm, nxp, nym, nyp = around(visp)
        fxm, fxp = 0.5 * (n0 + nxm), 0.5 * (nxp + n0)
        fym, fyp = 0.5 * (n0 + nym), 0.5 * (nyp + n0)
        fz = 0.5 * (n0 + zdn_copy(n0))
        u0m, u0p = speeds[0][1], speeds[0][2]
        u1m, u1p = speeds[1][3], speeds[1][4]
        u2 = speeds[2][0]

        def transport(q0, qxm, qxp, qym, qyp):
            up = u2 * q0
            return 0.5 * ((u0p * qxp - u0m * qxm) + (u1p * qyp - u1m * qym) + (zup(up) - zdn(up)))

        fields = around(np_)
        out_ndg[i] = fields[0] + DT * transport(*fields)
        gxm = gxp = gym = gyp = gz = 0.0
        for c in range(3):
            fields = around(ap.at[c])
            q0, qxm, qxp, qym, qyp = fields
            s0, sxm, sxp, sym, syp = speeds[c]
            dxm, dxp, dym, dyp = q0 - qxm, qxp - q0, q0 - qym, qyp - q0
            dz = q0 - zdn(q0)
            flux = fz * dz
            spread = (fxp * dxp - fxm * dxm) + (fyp * dyp - fym * dym) + (zup(flux) - flux)
            out_vel[c, i] = q0 + DT * (transport(*fields) + spread)
            gxm = gxm + dxm * (s0 - sxm)
            gxp = gxp + dxp * (sxp - s0)
            gym = gym + dym * (s0 - sym)
            gyp = gyp + dyp * (syp - s0)
            gz = gz + dz * (s0 - zdn(s0))
        bottom = jnp.where(layer(gz) == 0, gz, 0.0)
        out_vis[i] = (-0.5 * DT) * ((gxm + gxp) + (gym + gyp) + (gz + zup(gz)) + bottom)

    loop(0, BLOCK, finish, 2)


def shards(velocity, density, viscosity, grad_out, density_gradient):
    z = density.shape[2]
    size_x, size_y = lax.axis_size("gx"), lax.axis_size("gy")
    at_x = lax.axis_index("gx")
    odd = lax.rem(at_x, 2).astype(jnp.int32).reshape(1)
    even_pairs = [[i, i + 1] for i in range(0, size_x, 2)]
    odd_pairs = [[i, (i + 1) % size_x] for i in range(1, size_x, 2)]
    forward = [(i, (i + 1) % size_y) for i in range(size_y)]
    backward = [(j, i) for i, j in forward]

    def along_y(up, down):
        return lax.ppermute(up, "gy", forward), lax.ppermute(down, "gy", backward)

    fine = (32, 32, z)
    mid = (20, 24, z)
    low = (16, 16, z)
    rim = (BLOCK + 1, 24, z)
    rim2 = (16, 16, z)
    own = (BLOCK, BLOCK, z)
    fields = (velocity, viscosity, grad_out, density_gradient)
    single = [v[None] for v in (density, viscosity, density_gradient)]
    joined = jnp.concatenate([velocity, grad_out, *single], 0)
    up, down, b, d, planes = call(
        own_body,
        [rim, rim, own, own, (2, 4, 2 * BLOCK, z)],
        (joined,),
    )
    before, after = along_y(up, down)
    send = (19, 32, z)
    bb, dd, g0, even_send, odd_send = call(
        rows_body,
        [(BLOCK, 32, z), (BLOCK, 32, z), (32, z), send, send],
        (odd, b, d, down, planes, before, after),
        scalars=1,
    )
    even_got = lax.all_gather(even_send, "gx", axis_index_groups=even_pairs)
    odd_got = lax.all_gather(odd_send, "gx", axis_index_groups=odd_pairs)
    f1, b1, f2, b2, up, down, slots, kept0 = call(
        fine_body,
        [low, low, low, low, rim2, rim2, (size_y, 24, z), (8, 24, 32, z)],
        (odd, bb, dd, g0, even_got, odd_got),
        [(8, *fine), fine, fine, fine, (16, 32, z)]
        + [low] * 9
        + [(8, 16, z)]
        + [low] * 9
        + [(4, 16, z)]
        + [low, low, low, low, rim2, rim2, (size_y, 24, z)],
        scalars=1,
        kept=8,
        sems=9,
        megabytes=50,
    )
    got = lax.all_to_all(slots, "gy", 0, 0, tiled=True)
    before2, after2 = along_y(up, down)
    f1, b1, f2, b2, even_send, odd_strip = call(
        rows2_body,
        [mid, mid, low, low, (17, 32, z), (10, 32, z)],
        (odd, f1, b1, f2, b2, before2, after2, got),
        [low, low, low, low, rim2, rim2, (size_y, 24, z)],
        scalars=1,
        fetched=7,
        sems=7,
    )
    at_odd = lax.rem(at_x, 2)
    pair = lax.all_gather(even_send, "gx", axis_index_groups=even_pairs)
    side = lax.all_gather(pair[:, 0:7], "gx", axis_index_groups=odd_pairs)
    side = lax.dynamic_index_in_dim(side, at_odd, 0, keepdims=False)
    other = lax.all_gather(side, "gx", axis_index_groups=even_pairs)
    far = lax.dynamic_index_in_dim(other.reshape(4, 7, 32, z), 2 - at_odd, 0, keepdims=False)
    far = jnp.concatenate([far[0:6, 8:24].reshape(3, 32, z), odd_strip], 0)
    far = lax.all_gather(far, "gx", axis_index_groups=odd_pairs)
    level3 = (14, 32, z)
    slots, f1, b1, f2, b2, kept3 = call(
        level3_body,
        [(size_x, 2, 16, z), mid, mid, low, low, (8, *level3)],
        (odd, f1, b1, f2, b2, pair, other, far),
        [(8, *level3), level3, level3, level3, (1, 32, z), (2, 16, z)],
        scalars=1,
        kept=1,
        sems=1,
    )
    got = lax.all_to_all(slots, "gx", 0, 0, tiled=True)
    devices = 2 * WIN + 1
    return tuple(
        call(
            up_body,
            [(3, *own), own, own],
            (kept3, kept0, *fields, f1, b1, f2, b2, got, before, after, even_got, odd_got),
            [(8, *level3), (8, 24, 32, z), (3, *own), own, (3, *own), own, (8, *mid), (8, *low)]
            + [(devices, 16, z)] * 12
            + [(11, 32, z), level3, level3, level3]
            + [low, (10, 16, z), low, low]
            + [mid, (12, 24, z), mid, mid]
            + [(24, 32, z), (16, 32, z), (24, 32, z), (24, 32, z)]
            + [(3, 18, 32, z), (3, 18, 32, z), (18, 32, z), (18, 32, z)],
            megabytes=24,
            fetched=6,
            sems=6,
        )
    )


def solution(mesh):
    placed = (
        P(None, "gx", "gy", None),
        P("gx", "gy", None),
        P("gx", "gy", None),
        P(None, "gx", "gy", None),
        P("gx", "gy", None),
    )
    return jax.shard_map(
        shards,
        mesh=mesh,
        in_specs=placed,
        out_specs=(P(None, "gx", "gy", None), P("gx", "gy", None), P("gx", "gy", None)),
        check_vma=False,
    )
```

```python
import functools

import jax
import jax.numpy as jnp
from jax import lax
from jax.experimental import pallas as pl
from jax.experimental.pallas import tpu as pltpu
from jax.sharding import PartitionSpec as P

INTERPRET = False
DT = 0.2
MID = 1.2
HALF = 0.8
SIGMA = MID / HALF
RHO0 = 1.0 / SIGMA
RHO1 = 1.0 / (2.0 * SIGMA - RHO0)
A1 = RHO1 * RHO0
B1 = 2.0 * RHO1 / HALF
BLOCK = 16
PAD = 8
PAD1 = 6
U0, U1, U2 = 2, 4, 6
WIN = 8
F32 = jnp.float32


def call(body, out_shapes, args, scratch=(), scalars=0, megabytes=16, fetched=0, kept=0, sems=0):
    smem = [pl.BlockSpec(memory_space=pltpu.SMEM)] * scalars
    far = pl.BlockSpec(memory_space=pltpu.HBM)
    near = pl.BlockSpec(memory_space=pltpu.VMEM)
    scratch = [pltpu.VMEM(s, F32) for s in scratch]
    if sems:
        scratch.append(pltpu.SemaphoreType.DMA((sems,)))
    return pl.pallas_call(
        body,
        out_shape=[jax.ShapeDtypeStruct(s, F32) for s in out_shapes],
        in_specs=smem + [far] * fetched + [near] * (len(args) - scalars - fetched),
        out_specs=[near] * (len(out_shapes) - kept) + [far] * kept,
        scratch_shapes=scratch,
        compiler_params=pltpu.CompilerParams(vmem_limit_bytes=megabytes * 2**20),
        interpret=INTERPRET,
    )(*args)


def loop(low, high, step, unroll=1):
    def group(base, count):
        stores = []
        for u in range(count):
            stores.extend(step(base + u) or ())
        for ref, index, value in stores:
            ref[index] = value

    groups = (high - low) // unroll
    if groups == 1:
        group(low, unroll)
    elif groups > 1:
        lax.fori_loop(0, groups, lambda n, c: (group(low + n * unroll, unroll), c)[1], 0)
    rest = (high - low) - groups * unroll
    if rest:
        group(high - rest, rest)


def ydn(v):
    return pltpu.roll(v, 1, axis=0)


def yup(v):
    return pltpu.roll(v, v.shape[0] - 1, axis=0)


def layer(v):
    return lax.broadcasted_iota(jnp.int32, v.shape, 1)


def zroll_dn(v):
    return pltpu.roll(v, 1, axis=1)


def zroll_up(v):
    return pltpu.roll(v, v.shape[1] - 1, axis=1)


def zdn(v):
    return jnp.where(layer(v) == 0, 0.0, zroll_dn(v))


def zdn_copy(v):
    return jnp.where(layer(v) == 0, v, zroll_dn(v))


def zup(v):
    return jnp.where(layer(v) == v.shape[1] - 1, 0.0, zroll_up(v))


def setup(b, n, diag, low, high, scale, unroll, f=None, g=None, g_range=None):
    half = 0.5 * scale

    def step(i):
        b0 = b[i]
        fxm = half * (b0 + b[i - 1])
        fxp = half * (b[i + 1] + b0)
        fym = half * (b0 + ydn(b0))
        fyp = yup(fym)
        fz = 0.5 * (b0 + zdn_copy(b0))
        fzp = zup(fz)
        d = (fxm + fxp) + (fym + fyp) + (fz + fzp)
        inv = 1.0 / d
        fzm = jnp.where(layer(fz) == 0, 0.0, fz)
        out = [(ref, i, v * inv) for ref, v in zip(n, (fxm, fxp, fym, fyp, fzm, fzp), strict=True)]
        if diag is not None:
            out.append((diag, i, d))
        if f is not None:
            out.append((g, i, f[i] * inv))
        return out

    loop(low, high, step, unroll)


def around_sum(q, n, i, q0):
    total = (n[0][i] * q[i - 1] + n[1][i] * q[i + 1]) + (n[2][i] * ydn(q0) + n[3][i] * yup(q0))
    return total + (n[4][i] * zroll_dn(q0) + n[5][i] * zroll_up(q0))


def pre(g, x, n, low, high, unroll):
    first = (1.0 + A1) / MID + B1 * (1.0 - 1.0 / MID)

    def step(i):
        g0 = g[i]
        return [(x, i, first * g0 + (B1 / MID) * around_sum(g, n, i, g0))]

    loop(low, high, step, unroll)


def post(x, g, y, out, n, low, high, unroll):
    def first(i):
        x0 = x[i]
        return [(y, i, x0 + (1.0 / MID) * ((g[i] - x0) + around_sum(x, n, i, x0)))]

    loop(low - 1, high + 1, first, unroll)

    def second(i):
        y0 = y[i]
        z = (g[i] - y0) + around_sum(y, n, i, y0)
        return [(out, i, y0 + (A1 * (y0 - x[i]) + B1 * z))]

    loop(low, high, second, unroll)


def residual_pairs(g, x, diag, n, pairs, start, low, high, unroll):
    def one(i):
        x0 = x[i]
        return diag[i] * ((g[i] - x0) + around_sum(x, n, i, x0))

    def step(m):
        i = start + 2 * m
        return [(pairs, m, one(i) + one(i + 1))]

    loop(low, high, step, unroll)


def plane_pairs(b, pairs, start, low, high, unroll=4):
    def step(m):
        return [(pairs, m, b[start + 2 * m] + b[start + 2 * m + 1])]

    loop(low, high, step, unroll)


def row_pairs(pairs, coarse, low, high, row, count, target, shift=0, unroll=8):
    def step(m):
        even = pairs[m, pl.ds(row, count, 2), :]
        odd = pairs[m, pl.ds(row + 1, count, 2), :]
        return [(coarse, (m + shift, slice(target, target + count)), 0.25 * (even + odd))]

    loop(low, high, step, unroll)


def correct(x, coarse, wide, low, high, plane, row, count, target, unroll=4, out=None):
    def widen(m):
        v = coarse[m, row : row + count, :]
        return [
            (wide, (m, pl.ds(target, count, 2)), v),
            (wide, (m, pl.ds(target + 1, count, 2)), v),
        ]

    loop(low, high, widen, 2 * unroll)
    out = x if out is None else out

    def add(m):
        i = 2 * m + plane
        w = wide[m]
        return [(out, i, x[i] + w), (out, i + 1, x[i + 1] + w)]

    loop(low, high, add, unroll)


def own_body(joined, up, down, b, d, planes):
    vel, g = joined.at[0:3], joined.at[3:6]
    den, vis, ndg = joined.at[6], joined.at[7], joined.at[8]

    def invert(i):
        return [(b, i, 1.0 / den[i])]

    loop(0, BLOCK, invert, 8)
    edge = BLOCK - 1

    def step(i):
        b0 = b[i]
        fz = 0.5 * (b0 + zdn_copy(b0)) * g[2, i]
        fy = 0.5 * (b0 + ydn(b0)) * g[1, i]
        rows = lax.broadcasted_iota(jnp.int32, fy.shape, 0)
        fy = jnp.where(rows == 0, 0.0, fy)
        total = (zup(fz) - fz) + (yup(fy) - fy)
        left = jnp.maximum(i - 1, 0)
        right = jnp.minimum(i + 1, edge)
        inner = jnp.where(i > 0, 0.5, 0.0) * (b0 + b[left]) * g[0, i]
        outer = jnp.where(i < edge, 0.5, 0.0) * (b0 + b[right]) * g[0, right]
        total = total + (outer - inner)
        head, next_rows = slice(0, PAD), slice(PAD, 2 * PAD)
        out = [
            (d, i, total),
            (up, (i, head), b0[BLOCK - PAD :]),
            (up, (i, next_rows), total[BLOCK - PAD :]),
            (down, (i, head), b0[:PAD]),
            (down, (i, next_rows), total[:PAD]),
        ]
        for send, row in ((up, edge), (down, 0)):
            for c in range(3):
                out.append((send, (i, 16 + c), vel[c, i, row, :]))
                out.append((send, (i, 21 + c), g[c, i, row, :]))
            out.append((send, (i, 19), vis[i, row, :]))
            out.append((send, (i, 20), ndg[i, row, :]))
        return out

    loop(0, BLOCK, step, 4)
    z = b.shape[2]
    up[BLOCK] = jnp.zeros((24, z), F32)
    down[BLOCK] = jnp.zeros((24, z), F32)
    up[BLOCK, 0:PAD, :] = g[0, 0, BLOCK - PAD :, :]
    down[BLOCK, 0:PAD, :] = g[0, 0, :PAD, :]
    for n, plane in enumerate((0, edge)):
        for c in range(3):
            planes[n, c, 0:BLOCK, :] = vel[c, plane]
            planes[n, c, BLOCK : 2 * BLOCK, :] = g[c, plane]
        planes[n, 3, 0:BLOCK, :] = vis[plane]
        planes[n, 3, BLOCK : 2 * BLOCK, :] = ndg[plane]


def rows_body(odd, b, d, down, planes, before, after, bb, dd, g0, even_send, odd_send):
    top = PAD + BLOCK

    def step(i):
        own_flux = 0.5 * (b[i, 0:1, :] + before[i, PAD - 1 : PAD, :]) * down[i, 22:23, :]
        next_flux = 0.5 * (b[i, BLOCK - 1 : BLOCK, :] + after[i, 0:1, :]) * after[i, 22:23, :]
        out = []
        for ref, own, row in ((bb, b, 0), (dd, d, PAD)):
            out.append((ref, (i, slice(0, PAD)), before[i, row : row + PAD, :]))
            out.append((ref, (i, slice(PAD, top)), own[i]))
            out.append((ref, (i, slice(top, top + PAD)), after[i, row : row + PAD, :]))
        out.append((dd, (i, slice(PAD - 1, PAD)), before[i, 2 * PAD - 1 : 2 * PAD, :] + own_flux))
        out.append((dd, (i, slice(PAD, PAD + 1)), d[i, 0:1, :] - own_flux))
        out.append((dd, (i, slice(top - 1, top)), d[i, BLOCK - 1 : BLOCK, :] + next_flux))
        out.append((dd, (i, slice(top, top + 1)), after[i, PAD : PAD + 1, :] - next_flux))
        return out

    loop(0, BLOCK, step, 4)
    g0[0:PAD, :] = before[BLOCK, 0:PAD, :]
    g0[PAD:top, :] = planes[0, 0, BLOCK : 2 * BLOCK, :]
    g0[top : top + PAD, :] = after[BLOCK, 0:PAD, :]
    is_odd = odd[0]
    for send, last in ((even_send, 1 - is_odd), (odd_send, is_odd)):
        b_start = 8 * last
        d_start = 10 * last

        def b_step(m, send=send, b_start=b_start):
            return [(send, m, bb[b_start + m])]

        def d_step(m, send=send, d_start=d_start):
            return [(send, 8 + m, dd[d_start + m])]

        loop(0, 8, b_step, 8)
        loop(0, 6, d_step, 6)
        for c in range(4):
            send[14 + c] = planes[last, c]
        send[18] = g0[...]


def fine_body(
    odd, bb, dd, g0, even_got, odd_got,
    f1_out, b1_out, f2_out, b2_out, up_out, down_out, slots_out, kept,
    pack, b, f0, diag, pairs, g1, xb, *rest,
):
    n1, (diag1, pairs1) = rest[:6], rest[6:8]
    n2, (g2, x2, diag2, pairs2) = rest[8:14], rest[14:18]
    f1, b1, f2, b2, up, down, slots, sems = rest[18:]
    outs = ((f1, f1_out), (b1, b1_out), (up, up_out), (down, down_out))
    outs += ((f2, f2_out), (b2, b2_out), (slots, slots_out))
    moves = [pltpu.make_async_copy(a, b, sems.at[2 + n]) for n, (a, b) in enumerate(outs)]
    gf, x0 = pack.at[0], pack.at[7]
    n0 = tuple(pack.at[n] for n in range(1, 7))
    keep = slice(4, 28)
    saves = (
        pltpu.make_async_copy(pack.at[0:7, keep], kept.at[0:7], sems.at[0]),
        pltpu.make_async_copy(pack.at[7, keep], kept.at[7], sems.at[1]),
    )
    is_odd = odd[0] == 1
    top = PAD + BLOCK

    def left(m):
        return jnp.where(is_odd, even_got[0, m], odd_got[0, m])

    def right(m):
        return jnp.where(is_odd, odd_got[1, m], even_got[1, m])

    loop(0, BLOCK, lambda i: [(b, PAD + i, bb[i]), (f0, PAD + i, dd[i])], 4)
    loop(0, 8, lambda m: [(b, m, left(m)), (b, top + m, right(m))], 4)
    loop(0, 6, lambda m: [(f0, 2 + m, left(8 + m)), (f0, top + m, right(8 + m))], 6)
    flux = 0.5 * (b[PAD] + b[PAD - 1]) * g0[...]
    f0[PAD - 1] = f0[PAD - 1] + flux
    f0[PAD] = f0[PAD] - flux
    flux = 0.5 * (b[top] + b[top - 1]) * right(18)
    f0[top - 1] = f0[top - 1] + flux
    f0[top] = f0[top] - flux

    setup(b, n0, diag, 2, 30, 1.0, U0, f0, gf)
    saves[0].start()
    pre(gf, x0, n0, 3, 29, U0)
    saves[1].start()
    residual_pairs(gf, x0, diag, n0, pairs, 0, 2, 14, U0 // 2)
    row_pairs(pairs, f1, 2, 14, 0, 16, 0)
    plane_pairs(b, pairs, 0, 0, 16)
    row_pairs(pairs, b1, 0, 16, 0, 16, 0)

    z = b.shape[2]
    setup(b1, n1, diag1, 2, 14, 0.25, U2, f1, g1)
    pre(g1, xb, n1, 3, 13, U2)
    residual_pairs(g1, xb, diag1, n1, pairs1, 4, 0, 4, 4)
    f2[...] = jnp.zeros((16, 16, z), F32)
    b2[...] = jnp.ones((16, 16, z), F32)
    row_pairs(pairs1, f2, 0, 4, 4, 4, 6, shift=6)
    plane_pairs(b1, pairs1, 0, 0, 8)
    row_pairs(pairs1, b2, 0, 8, 0, 8, 4, shift=4)

    for send, brow, f1row, b1row in ((up, 4, 7, 6), (down, 6, 6, 8)):
        for m in range(4):
            send[m, 0:4, :] = f2[6 + m, 6:10, :]
        for m in range(8):
            send[m, 4:10, :] = b2[4 + m, brow : brow + 6, :]
        for m in range(2, 14):
            send[m, 10:13, :] = f1[m, f1row : f1row + 3, :]
        for m in range(16):
            send[m, 13:15, :] = b1[m, b1row : b1row + 2, :]
    for move in moves[:6]:
        move.start()
    x2[...] = jnp.zeros((16, 16, z), F32)
    setup(b2, n2, diag2, 4, 12, 0.25**2, 4, f2, g2)
    pre(g2, x2, n2, 5, 11, U2)
    residual_pairs(g2, x2, diag2, n2, pairs2, 4, 0, 4, 4)
    parts = []
    for m in range(4):
        even = pairs2[m, pl.ds(4, 4, 2), :]
        parts.append(0.25 * (even + pairs2[m, pl.ds(5, 4, 2), :]))
    plane_pairs(b2, pairs2, 6, 0, 2)
    for m in range(2):
        even = pairs2[m, pl.ds(6, 2, 2), :]
        parts.append(0.25 * (even + pairs2[m, pl.ds(7, 2, 2), :]))
    for n in range(4):
        slots[0, 4 * n : 4 * n + 4, :] = parts[n]
    slots[0, 16:18, :] = parts[4]
    slots[0, 18:20, :] = parts[5]
    for n in range(4):
        slots[0, 20 + n : 21 + n, :] = f2[6 + n, 6:7, :]
    value = slots[0]
    for m in range(1, 16):
        slots[m] = value
    ahead = lax.rem(lax.axis_index("gy") + 2, 16)
    for n in range(4):
        slots[ahead, 20 + n : 21 + n, :] = f2[6 + n, 9:10, :]
    moves[6].start()
    for save in (*saves, *moves):
        save.wait()


def rows2_body(
    odd, f1_in, b1_in, f2_in, b2_in, before_in, after_in, got_in,
    g1, h1, g2, h2, even_send, odd_strip, f1, b1, f2, b2, before, after, got, sems,
):
    pairs = ((got_in, got), (f1_in, f1), (b1_in, b1), (f2_in, f2), (b2_in, b2))
    pairs += ((before_in, before), (after_in, after))
    moves = [pltpu.make_async_copy(a, b, sems.at[n]) for n, (a, b) in enumerate(pairs)]
    for move in moves:
        move.start()
    for move in moves:
        move.wait()
    z = g1.shape[2]
    g1[...] = jnp.zeros((20, 24, z), F32)
    h1[...] = jnp.ones((20, 24, z), F32)
    g2[...] = jnp.zeros((16, 16, z), F32)
    h2[...] = jnp.ones((16, 16, z), F32)
    at_y = lax.axis_index("gy")
    back, ahead = lax.rem(at_y + 14, 16), lax.rem(at_y + 2, 16)
    for m in range(4):
        g2[6 + m, 6:10, :] = f2[6 + m, 6:10, :]
        g2[6 + m, 2:6, :] = before[m, 0:4, :]
        g2[6 + m, 10:14, :] = after[m, 0:4, :]
        g2[6 + m, 1:2, :] = got[back, 20 + m : 21 + m, :]
        g2[6 + m, 14:15, :] = got[ahead, 20 + m : 21 + m, :]
    for m in range(8):
        h2[4 + m, 6:10, :] = b2[4 + m, 6:10, :]
        h2[4 + m, 0:6, :] = before[m, 4:10, :]
        h2[4 + m, 10:16, :] = after[m, 4:10, :]
    for m in range(2, 14):
        g1[2 + m, 4:16, :] = f1[m, 2:14, :]
        g1[2 + m, 1:4, :] = before[m, 10:13, :]
        g1[2 + m, 16:19, :] = after[m, 10:13, :]
    for m in range(16):
        h1[2 + m, 2:18, :] = b1[m]
        h1[2 + m, 0:2, :] = before[m, 13:15, :]
        h1[2 + m, 18:20, :] = after[m, 13:15, :]
    for p in range(16):
        here = lax.rem(at_y + (p + 8), 16)
        above = lax.rem(at_y + (p + 9), 16)
        below = lax.rem(at_y + (p + 7), 16)
        for n in range(4):
            k = 4 * n
            low = got[here, k + 1 : k + 2, :] + got[below, k + 3 : k + 4, :]
            high = got[here, k + 2 : k + 3, :] + got[above, k : k + 1, :]
            even_send[n, 2 * p : 2 * p + 1, :] = low
            even_send[n, 2 * p + 1 : 2 * p + 2, :] = high
        for n in range(2):
            even_send[4 + n, 2 * p : 2 * p + 2, :] = got[here, 16 + 2 * n : 18 + 2 * n, :]
    is_odd = odd[0]
    even_send[6, 0:16, :] = g2[6]
    even_send[6, 16:32, :] = g2[9]
    for send, first, last in ((even_send, 7, 1 - is_odd), (odd_strip, 0, is_odd)):
        for u in range(10):
            v = g2[6 + u] if u < 4 else h2[6 - 2 * last + (u - 4)]
            send[first + u // 2, (u % 2) * 16 : (u % 2) * 16 + 16, :] = v
        for n in range(5):
            v = g1[8 + last + n] if n < 3 else h1[10 - 2 * last + (n - 3)]
            send[first + 5 + n, 0:24, :] = v
            send[first + 5 + n, 24:32, :] = jnp.zeros((8, z), F32)


def level3_body(
    odd, f1i, b1i, f2i, b2i, pair, other, far, slots, f1, b1, f2, b2, kept,
    pack, f3, b3, diag, pairs, small, sems,
):
    g3, x3, n3 = pack.at[0], pack.at[7], tuple(pack.at[n] for n in range(1, 7))
    save = pltpu.make_async_copy(pack, kept, sems.at[0])
    is_odd = odd[0] == 1
    blocks = [(other, (0, 0)), (other, (0, 1)), (pair, (0,)), (pair, (1,))]
    blocks += [(other, (1, 0)), (other, (1, 1))]

    z = f3.shape[2]

    def distant(slot, k):
        rim = (jnp.zeros if k < 4 else jnp.ones)((8, z), F32)
        rows = slice((k % 2) * 16, (k % 2) * 16 + 16)
        return jnp.concatenate([rim, far[slot, k // 2, rows, :], rim], 0)

    def part(p, k):
        even = distant(0, k) if p == 0 else blocks[p - 1][0][(*blocks[p - 1][1], k)]
        odds = distant(1, k) if p == 6 else blocks[p][0][(*blocks[p][1], k)]
        return jnp.where(is_odd, odds, even)

    for p in range(7):
        low, high = part(p, 1), part(p, 2)
        f3[2 * p] = low + part(p - 1, 3) if p > 0 else low
        f3[2 * p + 1] = high + part(p + 1, 0) if p < 6 else high
        b3[2 * p] = part(p, 4)
        b3[2 * p + 1] = part(p, 5)
    setup(b3, n3, diag, 1, 13, 0.25**3, U0, f3, g3)
    pre(g3, x3, n3, 2, 12, 5)
    save.start()
    residual_pairs(g3, x3, diag, n3, pairs, 6, 0, 1, 1)
    row_pairs(pairs, small, 0, 1, 0, 16, 0)
    plane_pairs(b3, pairs, 6, 0, 1)
    row_pairs(pairs, small, 0, 1, 0, 16, 0, shift=1)

    def spread(m):
        return [(slots, (m, n), small[n]) for n in range(2)]

    loop(0, 32, spread, 4)

    def left(n, rows):
        return jnp.where(is_odd, pair[0, 7 + n, rows, :], far[0, 3 + n, rows, :])

    def right(n, rows):
        return jnp.where(is_odd, far[1, 3 + n, rows, :], pair[1, 7 + n, rows, :])

    f1[...] = f1i[...]
    b1[...] = b1i[...]
    f2[...] = f2i[...]
    b2[...] = b2i[...]
    for u in range(10):
        rows = slice((u % 2) * 16, (u % 2) * 16 + 16)
        if u < 4:
            f2[2 + u] = left(u // 2, rows)
            f2[10 + u] = right(u // 2, rows)
        else:
            b2[u - 4] = left(u // 2, rows)
            b2[u + 6] = right(u // 2, rows)
    f2[1] = part(1, 6)[16:32]
    f2[14] = part(5, 6)[0:16]
    rows = slice(0, 24)
    for n in range(3):
        f1[1 + n] = left(5 + n, rows)
        f1[16 + n] = right(5 + n, rows)
    for n in range(2):
        b1[n] = left(8 + n, rows)
        b1[18 + n] = right(8 + n, rows)
    save.wait()


def up_body(*refs):
    refs = list(refs)
    at_x = lax.axis_index("gx")

    def take(count):
        head = tuple(refs[:count])
        del refs[:count]
        return head

    kept = take(6)
    f1, b1, f2, b2, got, before, after, even_got, odd_got = take(9)
    out_vel, out_ndg, out_vis = take(3)
    held = take(6)
    pack3, pack0, vel, vis, g, ndg = held
    pack1, pack2 = take(2)
    f4, b4, g4, xa4, xb4, e4 = take(6)
    n4 = take(6)
    w3, v3, y3, t3, v2, w2, y2, t2, v1, w1, y1, t1, v0, w0, y0, t0 = take(16)
    vp, ap, visp, np_ = take(4)
    (sems,) = refs
    (g3, x3, n3), (g2, x2, n2), (g1, x1, n1), (g0, x0, n0) = (
        (pack.at[0], pack.at[7], tuple(pack.at[n] for n in range(1, 7)))
        for pack in (pack3, pack2, pack1, pack0)
    )
    loads = [
        pltpu.make_async_copy(source, target, sems.at[n])
        for n, (source, target) in enumerate(zip(kept, held, strict=True))
    ]
    for load in loads:
        load.start()
    devices = 2 * WIN + 1

    def gather(q):
        source = lax.rem(at_x + (q + 32 - WIN), 32)
        return [(f4, q, got[source, 0]), (b4, q, got[source, 1])]

    loop(0, devices, gather, devices)
    low, high = 1, devices - 1
    setup(b4, n4, None, low, high, 0.25**4, U2, f4, g4)

    def start(i):
        u = g4[i] * (1.0 / MID)
        return [(e4, i, u), (xa4, i, u)]

    loop(low, high, start, U2)
    ratio = RHO0
    x_now, x_next = xa4, xb4
    for _ in range(5):
        following = 1.0 / (2.0 * SIGMA - ratio)
        low, high = low + 1, high - 1

        def sweep(i, x_now=x_now, x_next=x_next, following=following, ratio=ratio):
            q0 = x_now[i]
            scaled = (g4[i] - q0) + around_sum(x_now, n4, i, q0)
            u = following * ratio * e4[i] + (2.0 * following / HALF) * scaled
            return [(e4, i, u), (x_next, i, q0 + u)]

        loop(low, high, sweep, U2)
        ratio = following
        x_now, x_next = x_next, x_now
    loads[0].wait()
    correct(x3, x_now, w3, 6, 11, -10, 0, 16, 0, out=v3)
    post(v3, g3, y3, t3, n3, 4, 10, U0)
    setup(b2, n2, None, 1, 15, 0.25**2, U2, f2, g2)
    pre(g2, x2, n2, 2, 14, U2)
    correct(x2, t3, w2, 4, 10, -6, 14, 6, 2, out=v2)
    post(v2, g2, y2, t2, n2, 4, 12, U2)
    setup(b1, n1, None, 1, 19, 0.25, U1, f1, g1)
    pre(g1, x1, n1, 2, 18, U1)
    correct(x1, t2, w1, 4, 12, -6, 4, 8, 2, out=v1)
    post(v1, g1, y1, t1, n1, 4, 16, U1)
    loads[1].wait()
    correct(x0, t1, w0, 4, 16, -8, 4, 12, 4, 2, out=v0)
    post(v0, g0, y0, t0, n0, 2, 21, U0)
    for load in loads[2:]:
        load.wait()

    def pad(i):
        def put(out, own, source, row):
            out[7:8, :] = before[source, row : row + 1, :]
            out[8:24, :] = own
            out[24:25, :] = after[source, row : row + 1, :]

        for c in range(3):
            put(vp.at[c, i + 1], vel[c, i], i, 16 + c)
            put(ap.at[c, i + 1], g[c, i], i, 21 + c)
        put(visp.at[i + 1], vis[i], i, 19)
        put(np_.at[i + 1], ndg[i], i, 20)

    loop(0, BLOCK, pad, 2)
    is_odd = lax.rem(at_x, 2) == 1

    def left(m):
        return jnp.where(is_odd, even_got[0, m], odd_got[0, m])

    def right(m):
        return jnp.where(is_odd, odd_got[1, m], even_got[1, m])

    for plane, side in ((0, left), (BLOCK + 1, right)):
        for c in range(3):
            both = side(14 + c)
            vp[c, plane, 8:24, :] = both[0:BLOCK]
            ap[c, plane, 8:24, :] = both[BLOCK : 2 * BLOCK]
        both = side(17)
        visp[plane, 8:24, :] = both[0:BLOCK]
        np_[plane, 8:24, :] = both[BLOCK : 2 * BLOCK]

    def lift(m):
        centre = t0[m + 3]
        return [
            (ap, (0, m), ap[0, m] + (centre - t0[m + 2])),
            (ap, (1, m), ap[1, m] + (centre - ydn(centre))),
            (ap, (2, m), ap[2, m] + (centre - zdn(centre))),
        ]

    loop(0, BLOCK + 2, lift, 3)

    def finish(i):
        m = i + 1

        def around(ref):
            return (
                ref[m, 8:24, :],
                ref[m - 1, 8:24, :],
                ref[m + 1, 8:24, :],
                ref[m, 7:23, :],
                ref[m, 9:25, :],
            )

        speeds = [around(vp.at[c]) for c in range(3)]
        n0, nxm, nxp, nym, nyp = around(visp)
        fxm, fxp = 0.5 * (n0 + nxm), 0.5 * (nxp + n0)
        fym, fyp = 0.5 * (n0 + nym), 0.5 * (nyp + n0)
        fz = 0.5 * (n0 + zdn_copy(n0))
        u0m, u0p = speeds[0][1], speeds[0][2]
        u1m, u1p = speeds[1][3], speeds[1][4]
        u2 = speeds[2][0]

        def transport(q0, qxm, qxp, qym, qyp):
            up = u2 * q0
            return 0.5 * ((u0p * qxp - u0m * qxm) + (u1p * qyp - u1m * qym) + (zup(up) - zdn(up)))

        fields = around(np_)
        out_ndg[i] = fields[0] + DT * transport(*fields)
        gxm = gxp = gym = gyp = gz = 0.0
        for c in range(3):
            fields = around(ap.at[c])
            q0, qxm, qxp, qym, qyp = fields
            s0, sxm, sxp, sym, syp = speeds[c]
            dxm, dxp, dym, dyp = q0 - qxm, qxp - q0, q0 - qym, qyp - q0
            dz = q0 - zdn(q0)
            flux = fz * dz
            spread = (fxp * dxp - fxm * dxm) + (fyp * dyp - fym * dym) + (zup(flux) - flux)
            out_vel[c, i] = q0 + DT * (transport(*fields) + spread)
            gxm = gxm + dxm * (s0 - sxm)
            gxp = gxp + dxp * (sxp - s0)
            gym = gym + dym * (s0 - sym)
            gyp = gyp + dyp * (syp - s0)
            gz = gz + dz * (s0 - zdn(s0))
        bottom = jnp.where(layer(gz) == 0, gz, 0.0)
        out_vis[i] = (-0.5 * DT) * ((gxm + gxp) + (gym + gyp) + (gz + zup(gz)) + bottom)

    loop(0, BLOCK, finish, 2)


def shards(velocity, density, viscosity, grad_out, density_gradient):
    z = density.shape[2]
    size_x, size_y = lax.axis_size("gx"), lax.axis_size("gy")
    at_x = lax.axis_index("gx")
    odd = lax.rem(at_x, 2).astype(jnp.int32).reshape(1)
    even_pairs = [[i, i + 1] for i in range(0, size_x, 2)]
    odd_pairs = [[i, (i + 1) % size_x] for i in range(1, size_x, 2)]
    forward = [(i, (i + 1) % size_y) for i in range(size_y)]
    backward = [(j, i) for i, j in forward]

    def along_y(up, down):
        return lax.ppermute(up, "gy", forward), lax.ppermute(down, "gy", backward)

    fine = (32, 32, z)
    mid = (20, 24, z)
    low = (16, 16, z)
    rim = (BLOCK + 1, 24, z)
    rim2 = (16, 16, z)
    own = (BLOCK, BLOCK, z)
    fields = (velocity, viscosity, grad_out, density_gradient)
    single = [v[None] for v in (density, viscosity, density_gradient)]
    joined = jnp.concatenate([velocity, grad_out, *single], 0)
    up, down, b, d, planes = call(
        own_body,
        [rim, rim, own, own, (2, 4, 2 * BLOCK, z)],
        (joined,),
    )
    before, after = along_y(up, down)
    send = (19, 32, z)
    bb, dd, g0, even_send, odd_send = call(
        rows_body,
        [(BLOCK, 32, z), (BLOCK, 32, z), (32, z), send, send],
        (odd, b, d, down, planes, before, after),
        scalars=1,
    )
    even_got = lax.all_gather(even_send, "gx", axis_index_groups=even_pairs)
    odd_got = lax.all_gather(odd_send, "gx", axis_index_groups=odd_pairs)
    f1, b1, f2, b2, up, down, slots, kept0 = call(
        fine_body,
        [low, low, low, low, rim2, rim2, (size_y, 24, z), (8, 24, 32, z)],
        (odd, bb, dd, g0, even_got, odd_got),
        [(8, *fine), fine, fine, fine, (16, 32, z)]
        + [low] * 9
        + [(8, 16, z)]
        + [low] * 9
        + [(4, 16, z)]
        + [low, low, low, low, rim2, rim2, (size_y, 24, z)],
        scalars=1,
        kept=8,
        sems=9,
        megabytes=50,
    )
    got = lax.all_to_all(slots, "gy", 0, 0, tiled=True)
    before2, after2 = along_y(up, down)
    f1, b1, f2, b2, even_send, odd_strip = call(
        rows2_body,
        [mid, mid, low, low, (17, 32, z), (10, 32, z)],
        (odd, f1, b1, f2, b2, before2, after2, got),
        [low, low, low, low, rim2, rim2, (size_y, 24, z)],
        scalars=1,
        fetched=7,
        sems=7,
    )
    at_odd = lax.rem(at_x, 2)
    pair = lax.all_gather(even_send, "gx", axis_index_groups=even_pairs)
    side = lax.all_gather(pair[:, 0:7], "gx", axis_index_groups=odd_pairs)
    side = lax.dynamic_index_in_dim(side, at_odd, 0, keepdims=False)
    other = lax.all_gather(side, "gx", axis_index_groups=even_pairs)
    far = lax.dynamic_index_in_dim(other.reshape(4, 7, 32, z), 2 - at_odd, 0, keepdims=False)
    far = jnp.concatenate([far[0:6, 8:24].reshape(3, 32, z), odd_strip], 0)
    far = lax.all_gather(far, "gx", axis_index_groups=odd_pairs)
    level3 = (14, 32, z)
    slots, f1, b1, f2, b2, kept3 = call(
        level3_body,
        [(size_x, 2, 16, z), mid, mid, low, low, (8, *level3)],
        (odd, f1, b1, f2, b2, pair, other, far),
        [(8, *level3), level3, level3, level3, (1, 32, z), (2, 16, z)],
        scalars=1,
        kept=1,
        sems=1,
    )
    got = lax.all_to_all(slots, "gx", 0, 0, tiled=True)
    devices = 2 * WIN + 1
    return tuple(
        call(
            up_body,
            [(3, *own), own, own],
            (kept3, kept0, *fields, f1, b1, f2, b2, got, before, after, even_got, odd_got),
            [(8, *level3), (8, 24, 32, z), (3, *own), own, (3, *own), own, (8, *mid), (8, *low)]
            + [(devices, 16, z)] * 12
            + [(11, 32, z), level3, level3, level3]
            + [low, (10, 16, z), low, low]
            + [mid, (12, 24, z), mid, mid]
            + [(24, 32, z), (16, 32, z), (24, 32, z), (24, 32, z)]
            + [(3, 18, 32, z), (3, 18, 32, z), (18, 32, z), (18, 32, z)],
            megabytes=24,
            fetched=6,
            sems=6,
        )
    )


def solution(mesh):
    placed = (
        P(None, "gx", "gy", None),
        P("gx", "gy", None),
        P("gx", "gy", None),
        P(None, "gx", "gy", None),
        P("gx", "gy", None),
    )
    return jax.shard_map(
        shards,
        mesh=mesh,
        in_specs=placed,
        out_specs=(P(None, "gx", "gy", None), P("gx", "gy", None), P("gx", "gy", None)),
        check_vma=False,
    )
```
